512 devices in a mesh: filt: 4 (over z_hi, core), il: 32 (over z_lo, y), xl: 4 (over x).
Axes of the slice: x: 4, y: 8, z: 8 (z_hi: 2, z_lo: 4; z = z_hi * 4 + z_lo), core: 2. Of those that a mesh axis runs over, the one named last changes fastest.
Arguments:
- baseline: float32 [4, 32, 64, 512], P(None, 'il', 'xl', 'filt'), may hold values from -6 to 6
- monitor: float32 [4, 32, 64, 512], P(None, 'il', 'xl', 'filt'), may hold values from -6 to 6
- band_ids: int32 [4, 32, 8, 2], P(None, 'il', 'xl'), may hold values from 0 to 15, all different within a row
- quality: float32 [4, 32, 64, 512], P('filt', 'il', 'xl'), may hold values from 0.25 to 2
Outputs:
- shift: float32 [4, 32, 64, 512], P('filt', 'il', 'xl')
- residual: float32 [4, 32, 64, 512], P('filt', 'il', 'xl')
The draws below stay inside these ranges and needn't reach their ends.
Inputs may be any that keep to these rules, and one draw needn't show every extreme that they name: `band_ids`: the 2 bands of each trace block of 8 crossline traces are distinct; band b covers lags b * 8 - 64 to b * 8 - 57.
All inputs are finite; a program needn't handle non-finite values.
Results may differ from the reference program's by a relative error of at most 0.00056.
Values may be sent and summed in bfloat16 or wider, within the bound.
No kernel may reach another device: no remote copies, remote signals or barrier semaphores. Data moves between devices by JAX's collectives and lax.ppermute only.
A program may use at most 64 MiB of HBM per device.

```python
import math
import jax
import jax.numpy as jnp
from jax import lax

NBAND = 16
BAND = 8
KB = 2
BXL = 8
ITERS = 8
LAGS = 128
HALF = 64
IL4 = 32
XL = 64
TIME = 512
XLB = 8
N_FILT = 4


def level_of(key, dims, split, least, high):
    loudness, own = 1.0, jax.random.fold_in(key, 6)
    for axis_at, parts in split:
        draws = jnp.exp(jax.random.uniform(jax.random.fold_in(own, axis_at), (parts,), jnp.float32, least / len(split), high / len(split)))
        loudness = loudness * jnp.repeat(draws, dims[axis_at] // parts).reshape([-1 if axis == axis_at else 1 for axis in range(len(dims))])
    return loudness


def distinct(own_key, rows, count, top, lift):
    sequence = jax.random.permutation(jax.random.fold_in(own_key, 1), count)
    boost = sequence
    for power in range(3):
        boost = boost * boost // count
    boost = boost * lift // count
    lots = jax.random.randint(jax.random.fold_in(own_key, 2), (rows, count), 0, 4096) + boost
    sure = jax.random.permutation(jax.random.fold_in(own_key, 3), rows)[jnp.arange(count) % rows]
    lots = jnp.where(jnp.arange(rows)[:, None] == sure[None, :], 1 << 14, lots)
    merit = lots * count + jnp.arange(count)
    return lax.top_k(merit.astype(jnp.int32), top)[1].astype(jnp.int32)


def noise(stream_key, extent, width, reach, shards=(), kind=jnp.bfloat16):
    factor_of = level_of(stream_key, extent, shards, -0.22, 0.18) if shards else 1.0
    values = jax.random.normal(stream_key, extent, jnp.float32) * width * factor_of
    return jnp.minimum(jnp.maximum(values, -reach), reach).astype(kind)


def setup_inputs(seed: int = 0) -> dict:
    splits = jax.random.split(jax.random.key(seed), 5)
    baseline = noise(splits[0], (N_FILT, IL4, XL, TIME), 1.0, 6.0, ((1, 32), (2, 4), (3, 4)), jnp.float32)
    monitor = noise(splits[1], (N_FILT, IL4, XL, TIME), 1.0, 6.0, ((1, 32), (2, 4), (3, 4)), jnp.float32)
    band_ids = distinct(splits[2], N_FILT * IL4 * XLB, NBAND, KB, 0).reshape((N_FILT, IL4, XLB, KB))
    quality = jnp.clip(jnp.exp(math.log(2.0) - 2.0794415 * jax.random.uniform(splits[3], (N_FILT, IL4, XL, TIME), jnp.float32) ** level_of(splits[3], (N_FILT, IL4, XL, TIME), ((0, 4), (1, 32), (2, 4)), -0.2, 0.2)), 0.25, 2.0)
    return dict(baseline=baseline, monitor=monitor, band_ids=band_ids, quality=quality)


smooth_space = 4.0
smooth_time = 1.0


def block_terms(base_block, mon_block, band_list):
    def slot_terms(band):
        start = (band * BAND).astype(jnp.int32)
        window = lax.dynamic_slice(mon_block, (jnp.int32(0), start), (BXL, TIME + BAND))
        offset = band.astype(jnp.float32) * BAND - HALF
        weight_sum = jnp.zeros((BXL, TIME), jnp.float32)
        moment_sum = jnp.zeros((BXL, TIME), jnp.float32)
        for lag_step in range(BAND):
            difference = base_block - window[:, lag_step:lag_step + TIME]
            misfit = (difference * difference).astype(jnp.bfloat16)
            likeness = 1.0 / (1.0 + misfit.astype(jnp.float32))
            weight_sum = weight_sum + likeness
            moment_sum = moment_sum + ((offset + lag_step) / HALF) * likeness
        return weight_sum, moment_sum

    weight_parts, moment_parts = jax.vmap(slot_terms)(band_list)
    return jnp.sum(weight_parts, 0) / (KB * BAND), jnp.sum(moment_parts, 0) / (KB * BAND)


def row_terms(inputs):
    base_row, mon_row, band_row = inputs
    padded = jnp.pad(mon_row, ((0, 0), (HALF, HALF)))
    weight_row, moment_row = jax.vmap(block_terms)(
        base_row.reshape(XLB, BXL, TIME), padded.reshape(XLB, BXL, TIME + LAGS), band_row)
    return weight_row.reshape(XL, TIME), moment_row.reshape(XL, TIME)


def second_difference(field, axis):
    widths = [(0, 0), (0, 0), (0, 0)]
    widths[axis] = (1, 1)
    padded = jnp.pad(field, widths)
    length = field.shape[axis]
    after_cells = lax.slice_in_dim(padded, 2, length + 2, axis=axis)
    before_cells = lax.slice_in_dim(padded, 0, length, axis=axis)
    return 2.0 * field - after_cells - before_cells


def operate(field, weight):
    across = second_difference(field, 0) + second_difference(field, 1)
    return weight * field + smooth_space * across + smooth_time * second_difference(field, 2)


def reference(baseline, monitor, band_ids, quality):
    traces_in = N_FILT * IL4
    base_grid = baseline.reshape(traces_in, XL, TIME)
    mon_grid = monitor.reshape(traces_in, XL, TIME)
    band_grid = band_ids.reshape(traces_in, XLB, KB)
    weight_raw, moment_raw = lax.map(row_terms, (base_grid, mon_grid, band_grid))
    quality_grid = quality.reshape(traces_in, XL, TIME)
    weight = quality_grid * weight_raw
    target = quality_grid * moment_raw
    shift = jnp.zeros_like(target)
    residual, direction = target, target
    norm_now = jnp.sum(residual * residual)
    for iteration in range(ITERS):
        image = operate(direction, weight)
        alpha = norm_now / jnp.sum(direction * image)
        shift = shift + alpha * direction
        residual = residual - alpha * image
        norm_next = jnp.sum(residual * residual)
        direction = residual + (norm_next / norm_now) * direction
        norm_now = norm_next
    return shift.reshape(N_FILT, IL4, XL, TIME), residual.reshape(N_FILT, IL4, XL, TIME)
```

```python
import jax
import jax.numpy as jnp
from jax import lax
from jax.experimental import pallas as pl
from jax.experimental.pallas import tpu as pltpu
from jax.sharding import Mesh, PartitionSpec as P

BAND = 8
KB = 2
HALF = 64
ITERS = 8
LANES = 128
SUB = 8

smooth_space = 4.0
smooth_time = 1.0
CENTRE = 19.0

GROUP = ("zh", "core", "zl")
PLANE = ("y", "x")
N_GROUP = 16
N_PLANE = 32
TRACES = 3
DEPTH = 24
VMEM = pl.BlockSpec(memory_space=pltpu.VMEM)
SMEM = pl.BlockSpec(memory_space=pltpu.SMEM)
F32 = jnp.float32


def lane_ids():
    return lax.broadcasted_iota(jnp.int32, (SUB, LANES), 1)


def row_ids():
    return lax.broadcasted_iota(jnp.int32, (SUB, LANES), 0)


def roll(value, amount, axis):
    return pltpu.roll(value, amount, axis) if amount else value


def pack_inputs(base_ref, mon_ref, bands_ref, quality_ref, out_ref, extra_ref):
    zl = lax.axis_index("zl")
    quarter = lax.axis_index("zh") * 2 + lax.axis_index("core")
    for group in range(N_GROUP):
        offset = ((zl - group % 4 + 1) & 3) - 1
        source = jnp.clip(group + offset, 0, N_GROUP - 1) >> 2
        out_ref[group, 0:16, :] = base_ref[source, 0]
        out_ref[group, 16:32, :] = mon_ref[source, 0]
    extra_ref[0:16, :] = quality_ref[0, 0]
    rows = lax.broadcasted_iota(jnp.int32, (SUB, 512), 0)
    bands = jnp.zeros((SUB, 512), F32)
    for block in range(2):
        for slot in range(KB):
            band = bands_ref[quarter, 0, block, slot].astype(F32)
            bands = jnp.where(rows == block * KB + slot, band, bands)
    extra_ref[16:24, :] = bands


def block_terms(base, padded, bands, lane):
    weight = jnp.zeros(base.shape, F32)
    moment = jnp.zeros(base.shape, F32)
    for band in bands:
        like_sum = jnp.zeros(base.shape, F32)
        step_sum = jnp.zeros(base.shape, F32)
        for quad in range(BAND // 4):
            terms = []
            for step in range(quad * 4, quad * 4 + 4):
                start = band * BAND + step
                turned = pltpu.roll(padded, (LANES - start) & (LANES - 1), 1)
                window = jnp.where(lane < LANES - start, turned[0:32], turned[8:40])
                difference = base - window
                misfit = (difference * difference).astype(jnp.bfloat16)
                terms.append(1.0 + misfit.astype(F32))
            a, b, c, d = terms
            left, right = a * b, c * d
            inverse = pl.reciprocal(left * right, approx=False)
            first, second = right * inverse, left * inverse
            low, high = (a + b) * first, (c + d) * second
            like_sum += low + high
            step_sum += a * first + c * second + 2.0 * high
            if quad:
                step_sum += (4.0 * quad) * (low + high)
        lag = (band * BAND - HALF).astype(F32)
        weight += like_sum
        moment += (lag * like_sum + step_sum) * (1.0 / HALF)
    scale = 1.0 / (KB * BAND)
    return weight * scale, moment * scale


def make_fields(recv_ref, below_ref, own_ref, above_ref, out_ref, target_ref):
    zl = lax.axis_index("zl")
    lane32 = lax.broadcasted_iota(jnp.int32, (32, LANES), 1)
    lane = lane_ids()
    for trace, extra_ref in enumerate((below_ref, own_ref, above_ref)):
        slot0 = (zl + trace - 1) & 3
        fields = []
        for block in range(2):
            rows = slice(block * 8, block * 8 + 8)
            mon_rows = slice(16 + block * 8, 24 + block * 8)
            base = jnp.concatenate([recv_ref[4 * c + slot0, rows, :] for c in range(4)], axis=0)
            mon = [recv_ref[4 * c + slot0, mon_rows, :] for c in range(4)]
            turned = [roll(v, 64, 1) for v in mon]
            zero = jnp.zeros((SUB, LANES), F32)
            sides = [zero] + turned + [zero]
            padded = jnp.concatenate(
                [jnp.where(lane < 64, sides[i], sides[i + 1]) for i in range(5)], axis=0
            )
            bands = [
                jnp.max(extra_ref[16 + block * KB + s : 17 + block * KB + s, 0:LANES]).astype(jnp.int32)
                for s in range(KB)
            ]
            weight, moment = block_terms(base, padded, bands, lane32)
            quality = jnp.concatenate(
                [extra_ref[rows, c * LANES : (c + 1) * LANES] for c in range(4)], axis=0
            )
            weight, moment = weight * quality, moment * quality
            if trace == 1:
                target_ref[block] = moment
            fields.append((weight, moment))
        padded_fields = []
        for f in range(2):
            for h in range(2):
                value = fields[h][f]
                turned = [roll(value[c * 8 : c * 8 + 8], 8, 1) for c in range(4)]
                sides = [zero] + turned + [zero]
                padded_fields.append([jnp.where(lane < 8, sides[i], sides[i + 1]) for i in range(5)])
        for piece in range(N_PLANE):
            part, offset = piece // 8, 16 * (piece % 8)
            packed = None
            for g, vregs in enumerate(padded_fields):
                shift = (32 * g - offset) % LANES
                value = roll(vregs[part], shift, 1)
                if piece % 8 == 7:
                    value = jnp.where(lane < 32 * g + 16, value, roll(vregs[part + 1], shift, 1))
                packed = value if packed is None else jnp.where(lane < 32 * g, packed, value)
            out_ref[piece, trace * 8 : trace * 8 + 8, :] = packed


def beside(values, lane, row):
    low, high = values
    next_low, next_high = roll(low, 7, 1), roll(high, 7, 1)
    turn_low, turn_high = roll(next_low, 96, 2), roll(next_high, 96, 2)
    last = row == 7
    up_low = jnp.where(last, jnp.where(lane < 96, turn_low, turn_high), next_low)
    up_high = jnp.where(last, jnp.where(lane < 96, turn_high, 0.0), next_high)
    prev_low, prev_high = roll(low, 1, 1), roll(high, 1, 1)
    turn_low, turn_high = roll(prev_low, 32, 2), roll(prev_high, 32, 2)
    first = row == 0
    down_low = jnp.where(first, jnp.where(lane < 32, 0.0, turn_low), prev_low)
    down_high = jnp.where(first, jnp.where(lane < 32, turn_low, turn_high), prev_high)
    return up_low + down_low, up_high + down_high


CHUNK = 2


def powers(recv_ref, out_ref, diag_ref, basis_ref):
    group = lax.axis_index("zh") * 8 + lax.axis_index("core") * 4 + lax.axis_index("zl")
    slab = lax.axis_index("y") * 4 + lax.axis_index("x")
    lane, row = lane_ids(), row_ids()
    tau = lane & 31
    time = slab * 16 - 8 + tau
    inside = ((time >= 0) & (time < 512)).astype(F32)
    shares = [
        inside * (group > 0).astype(F32),
        inside,
        inside * (group < N_GROUP - 1).astype(F32),
    ]
    space = [share * (2.0 * smooth_space / CENTRE) for share in shares]
    along = [share * (2.0 * smooth_time / CENTRE) for share in shares]
    for inline in range(DEPTH):
        trace, y = inline // 8, inline % 8
        for v in range(2):
            even = recv_ref[y * 4 + 2 * v, trace * 8 : trace * 8 + 8, :]
            odd = recv_ref[y * 4 + 2 * v + 1, trace * 8 : trace * 8 + 8, :]
            weight = jnp.where(lane < 64, even, roll(odd, 64, 1))
            target = jnp.where(lane < 64, roll(even, 64, 1), odd)
            centre = weight + (4.0 * smooth_space + 2.0 * smooth_time - CENTRE)
            diag_ref[v, inline] = centre * (shares[trace] * (2.0 / CENTRE))
            basis_ref[0, v, inline] = target
    lane3 = lax.broadcasted_iota(jnp.int32, (CHUNK, SUB, LANES), 2)
    row3 = lax.broadcasted_iota(jnp.int32, (CHUNK, SUB, LANES), 1)
    own = (tau >= 8) & (tau < 24)
    tile = jnp.zeros((SUB, LANES), F32)
    for level in range(ITERS):
        square = jnp.zeros((CHUNK, SUB, LANES), F32)
        cross = jnp.zeros((CHUNK, SUB, LANES), F32)
        begin = level + 1 + ((level + 1) % CHUNK and -1)
        for inline in range(begin, DEPTH - begin, CHUNK):
            region = inline // 8
            here = slice(inline, inline + CHUNK)
            centre = [basis_ref[level, v, here] for v in range(2)]
            sides = beside(centre, lane3, row3)
            for v in range(2):
                if inline == 0:
                    inlines = jnp.concatenate([jnp.zeros((1, SUB, LANES), F32), basis_ref[level, v, 0 : CHUNK - 1]], axis=0)
                else:
                    inlines = basis_ref[level, v, inline - 1 : inline - 1 + CHUNK]
                if inline + CHUNK == DEPTH:
                    inlines = inlines + jnp.concatenate(
                        [basis_ref[level, v, inline + 1 : DEPTH], jnp.zeros((1, SUB, LANES), F32)], axis=0
                    )
                else:
                    inlines = inlines + basis_ref[level, v, inline + 1 : inline + 1 + CHUNK]
                times = roll(centre[v], 1, 2) + roll(centre[v], LANES - 1, 2)
                image = (
                    diag_ref[v, here] * centre[v]
                    - space[region] * (inlines + sides[v])
                    - along[region] * times
                )
                image = 0.5 * image if level == 0 else image - basis_ref[level - 1, v, here]
                basis_ref[level + 1, v, here] = image
                if region == 1:
                    square += centre[v] * centre[v]
                    cross += centre[v] * image
        sums = []
        for value in (square, cross):
            value = jnp.where(own, jnp.sum(value, axis=0), 0.0)
            for shift in (4, 2, 1):
                value = value + roll(value, shift, 0)
            sums.append(value + roll(value, 64, 1))
        tile = jnp.where(row == level, jnp.where(lane < 64, sums[0], sums[1]), tile)
    for y in range(8):
        for v in range(2):
            pairs = []
            for k in range(1, 9, 2):
                pairs.append(
                    jnp.where(
                        tau < 16,
                        roll(basis_ref[k, v, 8 + y], 120, 1),
                        roll(basis_ref[k + 1, v, 8 + y], 8, 1),
                    )
                )
            turned = [roll(pair, 64, 1) for pair in pairs]
            for half in range(2):
                low, high = (pairs, turned) if half == 0 else (turned, pairs)
                piece = y * 4 + 2 * v + half
                for part in range(2):
                    out_ref[piece, part * 8 : part * 8 + 8, :] = jnp.where(
                        lane < 64, low[2 * part], high[2 * part + 1]
                    )
                out_ref[piece, 16:24, :] = tile


def spread_sums(recv_ref, out_ref):
    total = recv_ref[0, 16:24, :]
    for piece in range(1, N_PLANE):
        total = total + recv_ref[piece, 16:24, :]
    for group in range(N_GROUP):
        out_ref[group] = total


def operate_moments(moments, count):
    half = 0.5 * CENTRE
    return [CENTRE * moments[k] + half * (moments[k + 1] + moments[abs(k - 1)]) for k in range(count)]


def operate_terms(terms):
    half = 0.5 * CENTRE
    count = len(terms)
    out = []
    for k in range(count + 1):
        value = CENTRE * terms[k] if k < count else None
        if k >= 1:
            add = (CENTRE if k == 1 else half) * terms[k - 1]
            value = add if value is None else value + add
        if k + 1 < count:
            value = value + half * terms[k + 1]
        out.append(value)
    return out


def solve(squares, crosses):
    zero = jnp.zeros_like(squares[0])
    one = jnp.ones_like(squares[0])
    moments = [squares[0], crosses[0]]
    for k in range(1, ITERS):
        moments += [2.0 * squares[k] - squares[0], 2.0 * crosses[k] - crosses[0]]
    residual_m, direction_m = moments, moments
    residual, direction, shift = [one], [one], []
    norm = moments[0]
    for iteration in range(ITERS):
        count = 2 * ITERS - 1 - iteration
        image_m = operate_moments(direction_m, count)
        image = operate_terms(direction)
        bend = sum(direction[k] * image_m[k] for k in range(len(direction)))
        alpha = norm / bend
        shift = [
            alpha * direction[k] + (shift[k] if k < len(shift) else zero) for k in range(len(direction))
        ]
        residual = [
            (residual[k] if k < len(residual) else zero) - alpha * image[k] for k in range(len(image))
        ]
        if iteration + 1 < ITERS:
            residual_m = [residual_m[k] - alpha * image_m[k] for k in range(count)]
            after = sum(residual[k] * residual_m[k] for k in range(len(residual)))
            beta = after / norm
            direction = [
                residual[k] + (beta * direction[k] if k < len(direction) else zero)
                for k in range(len(residual))
            ]
            direction_m = [residual_m[k] + beta * direction_m[k] for k in range(count)]
            norm = after
    return shift, residual


def combine(basis_ref, sums_ref, target_ref, shift_ref, residual_ref):
    lane = lane_ids()
    total = sums_ref[0]
    for group in range(1, N_GROUP):
        total = total + sums_ref[group]
    left = jnp.where(lane < 64, total, 0.0)
    right = total - left
    for amount in (64, 32, 16, 8, 4, 2, 1):
        left = left + roll(left, amount, 1)
        right = right + roll(right, amount, 1)
    squares = [jnp.broadcast_to(left[k : k + 1], (SUB, LANES)) for k in range(ITERS)]
    crosses = [jnp.broadcast_to(right[k : k + 1], (SUB, LANES)) for k in range(ITERS)]
    shift, residual = solve(squares, crosses)
    shift = shift + [jnp.zeros_like(lane, F32)]
    first = (lane & 31) < 16
    for terms, out_ref in ((shift, shift_ref), (residual, residual_ref)):
        scale = [
            jnp.where(
                lane < 64,
                jnp.where(first, terms[k], terms[k + 1]),
                jnp.where(first, terms[k + 2], terms[k + 3]),
            )
            for k in (1, 5)
        ]
        for part in range(4):
            packed = [None, None]
            for step in range(8):
                piece = part * 8 + step
                value = scale[0] * basis_ref[piece, 0:8, :] + scale[1] * basis_ref[piece, 8:16, :]
                value = value + roll(value, 64, 1)
                value = value + roll(value, 112, 1)
                for h in range(2):
                    turned = roll(value, (16 * step - 32 * h) % LANES, 1)
                    packed[h] = turned if step == 0 else jnp.where(lane < 16 * step, packed[h], turned)
            for h in range(2):
                out_ref[0, 0, h * 8 : h * 8 + 8, part * LANES : (part + 1) * LANES] = (
                    packed[h] + terms[0] * target_ref[h, part * 8 : part * 8 + 8, :]
                )


def arrays(*shapes):
    return [jax.ShapeDtypeStruct(shape, F32) for shape in shapes]


def per_device(baseline, monitor, band_ids, quality):
    pieces, extra = pl.pallas_call(
        pack_inputs,
        out_shape=arrays((N_GROUP, 32, LANES), (DEPTH, 512)),
        in_specs=[VMEM, VMEM, SMEM, VMEM],
        name="pack_inputs",
    )(baseline, monitor, band_ids, quality)
    below = lax.ppermute(extra, GROUP, [(i, i + 1) for i in range(N_GROUP - 1)])
    above = lax.ppermute(extra, GROUP, [(i + 1, i) for i in range(N_GROUP - 1)])
    pieces = lax.all_to_all(pieces, GROUP, 0, 0, tiled=True)
    pieces, target = pl.pallas_call(
        make_fields,
        out_shape=arrays((N_PLANE, 8 * TRACES, LANES), (2, 32, LANES)),
        name="make_fields",
    )(pieces, below, extra, above)
    pieces = lax.all_to_all(pieces, PLANE, 0, 0, tiled=True)
    (pieces,) = pl.pallas_call(
        powers,
        out_shape=arrays((N_PLANE, 24, LANES)),
        scratch_shapes=[
            pltpu.VMEM((2, DEPTH, SUB, LANES), F32),
            pltpu.VMEM((ITERS + 1, 2, DEPTH, SUB, LANES), F32),
        ],
        name="powers",
    )(pieces)
    pieces = lax.all_to_all(pieces, PLANE, 0, 0, tiled=True)
    (sums,) = pl.pallas_call(
        spread_sums, out_shape=arrays((N_GROUP, SUB, LANES)), name="spread_sums"
    )(pieces)
    sums = lax.all_to_all(sums, GROUP, 0, 0, tiled=True)
    return tuple(
        pl.pallas_call(
            combine,
            out_shape=arrays((1, 1, 16, 512), (1, 1, 16, 512)),
            name="combine",
        )(pieces, sums, target)
    )


def solution(mesh):
    fine = Mesh(mesh.devices.reshape(2, 2, 4, 8, 4), ("zh", "core", "zl", "y", "x"))
    filt, il, xl = ("zh", "core"), ("zl", "y"), "x"
    split = P(filt, il, xl, None)
    in_specs = (P(None, il, xl, filt), P(None, il, xl, filt), P(None, il, xl, None), split)
    return jax.shard_map(
        per_device, mesh=fine, in_specs=in_specs, out_specs=(split, split), check_vma=False
    )
```

```python
import jax
import jax.numpy as jnp
from jax import lax
from jax.experimental import pallas as pl
from jax.experimental.pallas import tpu as pltpu
from jax.sharding import Mesh, PartitionSpec as P

BAND = 8
KB = 2
BXL = 8
HALF = 64
ITERS = 8
LANES = 128
SUB = 8

smooth_space = 4.0
smooth_time = 1.0
CENTRE = 19.0

GROUP = ("zh", "core", "zl")
PLANE = ("y", "x")
N_GROUP = 16
N_PLANE = 32
TRACES = 3
DEPTH = 24
FILT, IL = ("zh", "core"), ("zl", "y")
LAGS = 128
TRUST = 3e-4
VMEM = pl.BlockSpec(memory_space=pltpu.VMEM)
SMEM = pl.BlockSpec(memory_space=pltpu.SMEM)
F32 = jnp.float32


def lane_ids():
    return lax.broadcasted_iota(jnp.int32, (SUB, LANES), 1)


def row_ids():
    return lax.broadcasted_iota(jnp.int32, (SUB, LANES), 0)


def roll(value, amount, axis):
    return pltpu.roll(value, amount, axis) if amount else value


def pack_inputs(base_ref, mon_ref, bands_ref, quality_ref, out_ref, extra_ref):
    zl = lax.axis_index("zl")
    quarter = lax.axis_index("zh") * 2 + lax.axis_index("core")
    for group in range(N_GROUP):
        offset = ((zl - group % 4 + 1) & 3) - 1
        source = jnp.clip(group + offset, 0, N_GROUP - 1) >> 2
        out_ref[group, 0:16, :] = base_ref[source, 0]
        out_ref[group, 16:32, :] = mon_ref[source, 0]
    extra_ref[0:16, :] = quality_ref[0, 0]
    rows = lax.broadcasted_iota(jnp.int32, (SUB, 512), 0)
    bands = jnp.zeros((SUB, 512), F32)
    for block in range(2):
        for slot in range(KB):
            band = bands_ref[0, block, slot, quarter].astype(F32)
            bands = jnp.where(rows == block * KB + slot, band, bands)
    extra_ref[16:24, :] = bands


def block_terms(base, padded, bands, lane):
    weight = jnp.zeros(base.shape, F32)
    moment = jnp.zeros(base.shape, F32)
    for band in bands:
        like_sum = jnp.zeros(base.shape, F32)
        step_sum = jnp.zeros(base.shape, F32)
        for quad in range(BAND // 4):
            terms = []
            for step in range(quad * 4, quad * 4 + 4):
                start = band * BAND + step
                turned = pltpu.roll(padded, (LANES - start) & (LANES - 1), 1)
                window = jnp.where(lane < LANES - start, turned[0:32], turned[8:40])
                difference = base - window
                misfit = (difference * difference).astype(jnp.bfloat16)
                terms.append(1.0 + misfit.astype(F32))
            a, b, c, d = terms
            left, right = a * b, c * d
            inverse = pl.reciprocal(left * right, approx=False)
            first, second = right * inverse, left * inverse
            low, high = (a + b) * first, (c + d) * second
            like_sum += low + high
            step_sum += a * first + c * second + 2.0 * high
            if quad:
                step_sum += (4.0 * quad) * (low + high)
        lag = (band * BAND - HALF).astype(F32)
        weight += like_sum
        moment += (lag * like_sum + step_sum) * (1.0 / HALF)
    scale = 1.0 / (KB * BAND)
    return weight * scale, moment * scale


def make_fields(recv_ref, below_ref, own_ref, above_ref, out_ref, target_ref):
    zl = lax.axis_index("zl")
    lane32 = lax.broadcasted_iota(jnp.int32, (32, LANES), 1)
    lane = lane_ids()
    for trace, extra_ref in enumerate((below_ref, own_ref, above_ref)):
        slot0 = (zl + trace - 1) & 3
        fields = []
        for block in range(2):
            rows = slice(block * 8, block * 8 + 8)
            mon_rows = slice(16 + block * 8, 24 + block * 8)
            base = jnp.concatenate([recv_ref[4 * c + slot0, rows, :] for c in range(4)], axis=0)
            mon = [recv_ref[4 * c + slot0, mon_rows, :] for c in range(4)]
            turned = [roll(v, 64, 1) for v in mon]
            zero = jnp.zeros((SUB, LANES), F32)
            sides = [zero] + turned + [zero]
            padded = jnp.concatenate(
                [jnp.where(lane < 64, sides[i], sides[i + 1]) for i in range(5)], axis=0
            )
            bands = [
                jnp.max(extra_ref[16 + block * KB + s : 17 + block * KB + s, 0:LANES]).astype(jnp.int32)
                for s in range(KB)
            ]
            weight, moment = block_terms(base, padded, bands, lane32)
            quality = jnp.concatenate(
                [extra_ref[rows, c * LANES : (c + 1) * LANES] for c in range(4)], axis=0
            )
            weight, moment = weight * quality, moment * quality
            if trace == 1:
                target_ref[block] = moment
            fields.append((weight, moment))
        padded_fields = []
        for f in range(2):
            for h in range(2):
                value = fields[h][f]
                turned = [roll(value[c * 8 : c * 8 + 8], 8, 1) for c in range(4)]
                sides = [zero] + turned + [zero]
                padded_fields.append([jnp.where(lane < 8, sides[i], sides[i + 1]) for i in range(5)])
        for piece in range(N_PLANE):
            part, offset = piece // 8, 16 * (piece % 8)
            packed = None
            for g, vregs in enumerate(padded_fields):
                shift = (32 * g - offset) % LANES
                value = roll(vregs[part], shift, 1)
                if piece % 8 == 7:
                    value = jnp.where(lane < 32 * g + 16, value, roll(vregs[part + 1], shift, 1))
                packed = value if packed is None else jnp.where(lane < 32 * g, packed, value)
            out_ref[piece, trace * 8 : trace * 8 + 8, :] = packed


def beside(values, lane, row):
    low, high = values
    next_low, next_high = roll(low, 7, 1), roll(high, 7, 1)
    turn_low, turn_high = roll(next_low, 96, 2), roll(next_high, 96, 2)
    last = row == 7
    up_low = jnp.where(last, jnp.where(lane < 96, turn_low, turn_high), next_low)
    up_high = jnp.where(last, jnp.where(lane < 96, turn_high, 0.0), next_high)
    prev_low, prev_high = roll(low, 1, 1), roll(high, 1, 1)
    turn_low, turn_high = roll(prev_low, 32, 2), roll(prev_high, 32, 2)
    first = row == 0
    down_low = jnp.where(first, jnp.where(lane < 32, 0.0, turn_low), prev_low)
    down_high = jnp.where(first, jnp.where(lane < 32, turn_low, turn_high), prev_high)
    return up_low + down_low, up_high + down_high


CHUNK = 2


def powers(recv_ref, out_ref, diag_ref, basis_ref):
    group = lax.axis_index("zh") * 8 + lax.axis_index("core") * 4 + lax.axis_index("zl")
    slab = lax.axis_index("y") * 4 + lax.axis_index("x")
    lane, row = lane_ids(), row_ids()
    tau = lane & 31
    time = slab * 16 - 8 + tau
    inside = ((time >= 0) & (time < 512)).astype(F32)
    shares = [
        inside * (group > 0).astype(F32),
        inside,
        inside * (group < N_GROUP - 1).astype(F32),
    ]
    space = [share * (2.0 * smooth_space / CENTRE) for share in shares]
    along = [share * (2.0 * smooth_time / CENTRE) for share in shares]
    for inline in range(DEPTH):
        trace, y = inline // 8, inline % 8
        for v in range(2):
            even = recv_ref[y * 4 + 2 * v, trace * 8 : trace * 8 + 8, :]
            odd = recv_ref[y * 4 + 2 * v + 1, trace * 8 : trace * 8 + 8, :]
            weight = jnp.where(lane < 64, even, roll(odd, 64, 1))
            target = jnp.where(lane < 64, roll(even, 64, 1), odd)
            centre = weight + (4.0 * smooth_space + 2.0 * smooth_time - CENTRE)
            diag_ref[v, inline] = centre * (shares[trace] * (2.0 / CENTRE))
            basis_ref[0, v, inline] = target
    lane3 = lax.broadcasted_iota(jnp.int32, (CHUNK, SUB, LANES), 2)
    row3 = lax.broadcasted_iota(jnp.int32, (CHUNK, SUB, LANES), 1)
    own = (tau >= 8) & (tau < 24)
    tile = jnp.zeros((SUB, LANES), F32)
    for level in range(ITERS):
        square = jnp.zeros((CHUNK, SUB, LANES), F32)
        cross = jnp.zeros((CHUNK, SUB, LANES), F32)
        begin = level + 1 + ((level + 1) % CHUNK and -1)
        for inline in range(begin, DEPTH - begin, CHUNK):
            region = inline // 8
            here = slice(inline, inline + CHUNK)
            centre = [basis_ref[level, v, here] for v in range(2)]
            sides = beside(centre, lane3, row3)
            for v in range(2):
                if inline == 0:
                    inlines = jnp.concatenate([jnp.zeros((1, SUB, LANES), F32), basis_ref[level, v, 0 : CHUNK - 1]], axis=0)
                else:
                    inlines = basis_ref[level, v, inline - 1 : inline - 1 + CHUNK]
                if inline + CHUNK == DEPTH:
                    inlines = inlines + jnp.concatenate(
                        [basis_ref[level, v, inline + 1 : DEPTH], jnp.zeros((1, SUB, LANES), F32)], axis=0
                    )
                else:
                    inlines = inlines + basis_ref[level, v, inline + 1 : inline + 1 + CHUNK]
                times = roll(centre[v], 1, 2) + roll(centre[v], LANES - 1, 2)
                image = (
                    diag_ref[v, here] * centre[v]
                    - space[region] * (inlines + sides[v])
                    - along[region] * times
                )
                image = 0.5 * image if level == 0 else image - basis_ref[level - 1, v, here]
                basis_ref[level + 1, v, here] = image
                if region == 1:
                    square += centre[v] * centre[v]
                    cross += centre[v] * image
        sums = []
        for value in (square, cross):
            value = jnp.where(own, jnp.sum(value, axis=0), 0.0)
            for shift in (4, 2, 1):
                value = value + roll(value, shift, 0)
            sums.append(value + roll(value, 64, 1))
        tile = jnp.where(row == level, jnp.where(lane < 64, sums[0], sums[1]), tile)
    for y in range(8):
        for v in range(2):
            pairs = []
            for k in range(1, 9, 2):
                pairs.append(
                    jnp.where(
                        tau < 16,
                        roll(basis_ref[k, v, 8 + y], 120, 1),
                        roll(basis_ref[k + 1, v, 8 + y], 8, 1),
                    )
                )
            turned = [roll(pair, 64, 1) for pair in pairs]
            for half in range(2):
                low, high = (pairs, turned) if half == 0 else (turned, pairs)
                piece = y * 4 + 2 * v + half
                for part in range(2):
                    out_ref[piece, part * 8 : part * 8 + 8, :] = jnp.where(
                        lane < 64, low[2 * part], high[2 * part + 1]
                    )
                out_ref[piece, 16:24, :] = tile


def spread_sums(recv_ref, out_ref):
    total = recv_ref[0, 16:24, :]
    for piece in range(1, N_PLANE):
        total = total + recv_ref[piece, 16:24, :]
    for group in range(N_GROUP):
        out_ref[group] = total


def two_sum(a, b):
    total = a + b
    part = total - a
    return total, (a - (total - part)) + (b - part)


def split(a):
    scaled = 4097.0 * a
    high = scaled - (scaled - a)
    return high, a - high


def across(tile, k):
    return jnp.broadcast_to(tile[k : k + 1], (SUB, LANES))


def lift(pair, turn):
    return tuple(turn(part) for part in pair)


def choose(mask, first, second):
    return tuple(jnp.where(mask, a, b) for a, b in zip(first, second))


def add_pairs(first, second):
    total, error = two_sum(first[0], second[0])
    return two_sum(total, error + (first[1] + second[1]))


def solve(total, row, turn):
    zero = jnp.zeros((SUB, LANES), F32)
    fold = total
    for amount in (96, 112, 120, 124, 126, 127):
        fold = add_pairs(fold, lift(fold, lambda part: turn(part, amount, 1)))
    squares = lift(fold, lambda part: jnp.broadcast_to(part[:, 0:1], (SUB, LANES)))
    crosses = lift(fold, lambda part: jnp.broadcast_to(part[:, 64:65], (SUB, LANES)))
    moments = [None] * (2 * ITERS)
    for parity, pair in enumerate((squares, crosses)):
        start = lift(pair, lambda part: across(part, 0))
        doubled = add_pairs(lift(pair, lambda part: 2.0 * part), lift(start, lambda part: -part))
        for k in range(ITERS):
            moments[2 * k + parity] = lift(doubled, lambda part: across(part, k))

    def column(values):
        out = values[0]
        for k in range(1, SUB):
            out = choose(row < k, out, values[k])
        return out

    ahead, beyond, behind = column(moments[:8]), column(moments[8:]), column(moments[8:0:-1])
    gram = []
    for k in range(ITERS + 1):
        later = choose(
            row < 8 - k,
            lift(ahead, lambda part: turn(part, (8 - k) % 8, 0)),
            lift(beyond, lambda part: turn(part, (8 - k) % 8, 0)),
        )
        earlier = choose(
            row < k,
            lift(behind, lambda part: turn(part, k % 8, 0)),
            lift(ahead, lambda part: turn(part, k % 8, 0)),
        )
        gram.append(add_pairs(later, earlier))
    inverse = [gram[k][0] + 0.5 * (gram[k + 1][0] + gram[abs(k - 1)][0]) for k in range(ITERS)]
    for k in range(ITERS):
        reciprocal = 1.0 / across(inverse[k], k)
        pivot = inverse[k]
        for j in range(ITERS):
            if j != k:
                share = across(inverse[j], k) * reciprocal
                inverse[j] = jnp.where(row == k, share, inverse[j] - pivot * share)
        inverse[k] = jnp.where(row == k, reciprocal, -pivot * reciprocal)

    def apply_inverse(right):
        terms = [inverse[k] * across(right, k) for k in range(ITERS)]
        while len(terms) > 1:
            terms = [terms[k] + terms[k + 1] for k in range(0, len(terms), 2)]
        return terms[0]

    def remainder(series):
        def lower(part):
            return jnp.where(row == 0, 0.0, jnp.where(row == 1, 1.0, 0.5) * turn(part, 1, 0))

        def upper(part):
            return jnp.where(row == 7, 0.0, 0.5 * turn(part, 7, 0))

        image = add_pairs(add_pairs(lift(series, lower), lift(series, upper)), series)
        start = (jnp.where(row == 0, 1.0, 0.0), zero)
        return add_pairs(start, lift(image, lambda part: -part)), lift(series, lambda part: -0.5 * across(part, 7))

    parts = [split(pair[0]) for pair in gram]
    series = (apply_inverse(gram[0][0]), zero)
    steps = []
    for _ in range(2):
        body, top = remainder(series)
        high, low = zero, zero
        for k in range(ITERS + 1):
            a, a_low = lift(body, lambda part: across(part, k)) if k < ITERS else top
            b, b_low = gram[k]
            (a0, a1), (b0, b1) = split(a), parts[k]
            product = a * b
            error = (((a0 * b0 - product) + a0 * b1) + a1 * b0) + a1 * b1
            high, rest = two_sum(high, product)
            low = low + (rest + (error + (a * b_low + a_low * b)))
        change = apply_inverse(high + low)
        steps.append(change)
        series = two_sum(series[0], series[1] + change)
    body, top = remainder(series)
    return (series[0] + series[1]) * (1.0 / CENTRE), body[0] + body[1], top[0] + top[1], steps, series[0]


def combine(basis_ref, sums_ref, target_ref, shift_ref, residual_ref, again_ref):
    lane, row = lane_ids(), row_ids()
    zero = jnp.zeros((SUB, LANES), F32)
    total = (sums_ref[0], zero)
    for group in range(1, N_GROUP):
        high, error = two_sum(total[0], sums_ref[group])
        total = (high, total[1] + error)
    shift, residual, last, steps, series = solve(total, row, roll)
    fine = jnp.max(jnp.abs(steps[0])) <= TRUST * jnp.max(jnp.abs(series))
    again_ref[0] = 1 - fine.astype(jnp.int32)
    first = (lane & 31) < 16
    for body, top, out_ref in ((shift, zero, shift_ref), (residual, last, residual_ref)):
        terms = [across(body, k) for k in range(ITERS)] + [top]
        low, high = (
            jnp.where(
                lane < 64,
                jnp.where(first, terms[k], terms[k + 1]),
                jnp.where(first, terms[k + 2], terms[k + 3]),
            )
            for k in (1, 5)
        )
        for part in range(4):
            packed = [None, None]
            for step in range(8):
                piece = part * 8 + step
                value = low * basis_ref[piece, 0:8, :] + high * basis_ref[piece, 8:16, :]
                value = value + roll(value, 64, 1)
                value = value + roll(value, 112, 1)
                for h in range(2):
                    turned = roll(value, (16 * step - 32 * h) % LANES, 1)
                    packed[h] = turned if step == 0 else jnp.where(lane < 16 * step, packed[h], turned)
            for h in range(2):
                out_ref[0, 0, h * 8 : h * 8 + 8, part * LANES : (part + 1) * LANES] = (
                    packed[h] + terms[0] * target_ref[h, part * 8 : part * 8 + 8, :]
                )


def limit(mebibytes):
    return pltpu.CompilerParams(vmem_limit_bytes=mebibytes * 1024 * 1024)


def arrays(*shapes):
    return [jax.ShapeDtypeStruct(shape, F32) for shape in shapes]


def padded_2(value, sides, width):
    for axis, dim in sides:
        size, length = (lax.axis_size(axis), value.shape[dim])
        up = [(i, (i + 1) % size) for i in range(size - 1)]
        down = [(j, i) for i, j in up]
        last = lax.slice_in_dim(value, length - width, length, axis=dim)
        first = lax.slice_in_dim(value, 0, width, axis=dim)
        before = lax.ppermute(last, axis, up)
        after = lax.ppermute(first, axis, down)
        value = jnp.concatenate([before, value, after], axis=dim)
    return value


def slot_window(block, band):
    start = band * BAND
    return lax.dynamic_slice(
        block, (jnp.int32(0), start), (block.shape[0], block.shape[1] - LAGS + BAND)
    )


def lag_table(band_list):
    steps = jnp.arange(BAND, dtype=jnp.float32)
    return (band_list.astype(jnp.float32)[..., None] * BAND + steps - HALF) / HALF


def moments(errors, lags):
    likeness = 1.0 / (1.0 + errors.astype(jnp.float32))
    weight_sum = jnp.sum(likeness, axis=(3, 4)) / (KB * BAND)
    moment_sum = jnp.sum(lags[..., None, None] * likeness, axis=(3, 4)) / (KB * BAND)
    return (weight_sum, moment_sum)


def operate(field, weight):
    padded = padded_2(field, ((FILT + IL, 0), ("x", 1)), 1)
    centre = padded[1:-1, 1:-1, :]
    across = (
        4.0 * centre
        - padded[2:, 1:-1, :]
        - padded[:-2, 1:-1, :]
        - padded[1:-1, 2:, :]
        - padded[1:-1, :-2, :]
    )
    timed = jnp.pad(field, ((0, 0), (0, 0), (1, 1)))
    along = 2.0 * field - timed[:, :, 2:] - timed[:, :, :-2]
    return weight * field + smooth_space * across + smooth_time * along


def squares(residual):
    return lax.psum(jnp.sum(residual * residual), FILT + IL + ("x",))


def step_by_step(baseline, monitor, band_ids, quality):
    quarters, inline_rows, cross_rows, samples = baseline.shape
    cross_blocks = cross_rows // BXL
    extended = padded_2(monitor, ((FILT, 3),), HALF)
    ext_blocks = extended.reshape(quarters, inline_rows, cross_blocks, BXL, samples + LAGS)
    base_blocks = baseline.reshape(quarters, inline_rows, cross_blocks, BXL, samples)
    per_slot = jax.vmap(slot_window, in_axes=(None, 0))
    windows = jax.vmap(jax.vmap(jax.vmap(per_slot)))(ext_blocks, band_ids)
    errors = jnp.stack(
        [
            jnp.square(
                base_blocks[:, :, :, None] - windows[..., lag_step : lag_step + samples]
            ).astype(jnp.bfloat16)
            for lag_step in range(BAND)
        ],
        axis=4,
    )
    local_weight, local_moment = moments(errors, lag_table(band_ids))
    weight_raw, moment_raw = (
        lax.all_to_all(local_weight, FILT, split_axis=0, concat_axis=4, tiled=True),
        lax.all_to_all(local_moment, FILT, split_axis=0, concat_axis=4, tiled=True),
    )
    total_time = weight_raw.shape[-1]
    quality_grid = quality.reshape(inline_rows, cross_rows, total_time)
    weight = quality_grid * weight_raw.reshape(inline_rows, cross_rows, total_time)
    target = quality_grid * moment_raw.reshape(inline_rows, cross_rows, total_time)
    shift = jnp.zeros_like(target)
    residual = target
    direction = target
    norm_now = squares(residual)
    for iteration in range(ITERS):
        image = operate(direction, weight)
        alpha = norm_now / lax.psum(jnp.sum(direction * image), FILT + IL + ("x",))
        shift = shift + alpha * direction
        residual = residual - alpha * image
        norm_next = squares(residual)
        direction = residual + norm_next / norm_now * direction
        norm_now = norm_next
    out_shape = (1, inline_rows, cross_rows, total_time)
    return (shift.reshape(out_shape), residual.reshape(out_shape))


def kernel(body, out_shape, mebibytes, **options):
    return pl.pallas_call(
        body, out_shape=out_shape, compiler_params=limit(mebibytes), name=body.__name__, **options
    )


def per_device(baseline, monitor, band_ids, quality):
    pieces, extra = pl.pallas_call(
        pack_inputs,
        out_shape=arrays((N_GROUP, 32, LANES), (DEPTH, 512)),
        in_specs=[VMEM, VMEM, SMEM, VMEM],
        name="pack_inputs",
    )(baseline, monitor, band_ids.transpose(1, 2, 3, 0), quality)
    below = lax.ppermute(extra, GROUP, [(i, i + 1) for i in range(N_GROUP - 1)])
    above = lax.ppermute(extra, GROUP, [(i + 1, i) for i in range(N_GROUP - 1)])
    pieces = lax.all_to_all(pieces, GROUP, 0, 0, tiled=True)
    pieces, target = kernel(make_fields, arrays((N_PLANE, 8 * TRACES, LANES), (2, 32, LANES)), 8)(
        pieces, below, extra, above
    )
    pieces = lax.all_to_all(pieces, PLANE, 0, 0, tiled=True)
    (pieces,) = kernel(
        powers,
        arrays((N_PLANE, 24, LANES)),
        8,
        scratch_shapes=[
            pltpu.VMEM((2, DEPTH, SUB, LANES), F32),
            pltpu.VMEM((ITERS + 1, 2, DEPTH, SUB, LANES), F32),
        ],
    )(pieces)
    pieces = lax.all_to_all(pieces, PLANE, 0, 0, tiled=True)
    (sums,) = kernel(spread_sums, arrays((N_GROUP, SUB, LANES)), 4)(pieces)
    sums = lax.all_to_all(sums, GROUP, 0, 0, tiled=True)
    shift, residual, again = kernel(
        combine,
        arrays((1, 1, 16, 512), (1, 1, 16, 512)) + [jax.ShapeDtypeStruct((1,), jnp.int32)],
        4,
        out_specs=[VMEM, VMEM, SMEM],
    )(pieces, sums, target)

    def unsettled(state):
        return state[2][0] != 0

    def apart(state):
        return step_by_step(baseline, monitor, band_ids, quality) + (jnp.zeros((1,), jnp.int32),)

    return lax.while_loop(unsettled, apart, (shift, residual, again))[:2]


def solution(mesh):
    fine = Mesh(mesh.devices.reshape(2, 2, 4, 8, 4), ("zh", "core", "zl", "y", "x"))
    outs = P(FILT, IL, "x", None)
    in_specs = (P(None, IL, "x", FILT), P(None, IL, "x", FILT), P(None, IL, "x", None), outs)
    return jax.shard_map(
        per_device, mesh=fine, in_specs=in_specs, out_specs=(outs, outs), check_vma=False
    )
```

```python
import jax
import jax.numpy as jnp
from jax import lax
from jax.experimental import pallas as pl
from jax.experimental.pallas import tpu as pltpu
from jax.sharding import Mesh, PartitionSpec as P

BAND = 8
KB = 2
BXL = 8
HALF = 64
ITERS = 8
LANES = 128
SUB = 8

smooth_space = 4.0
smooth_time = 1.0
CENTRE = 19.0

GROUP = ("zh", "core", "zl")
PLANE = ("y", "x")
N_GROUP = 16
N_PLANE = 32
ROWS = 17
FIXED = 2.0**29
DEPTH = 24
FILT, IL = ("zh", "core"), ("zl", "y")
LAGS = 128
TRUST = 3e-4
VMEM = pl.BlockSpec(memory_space=pltpu.VMEM)
SMEM = pl.BlockSpec(memory_space=pltpu.SMEM)
F32 = jnp.float32


def lane_ids():
    return lax.broadcasted_iota(jnp.int32, (SUB, LANES), 1)


def row_ids():
    return lax.broadcasted_iota(jnp.int32, (SUB, LANES), 0)


def roll(value, amount, axis):
    return pltpu.roll(value, amount, axis) if amount else value


def pack_inputs(base_ref, mon_ref, bands_ref, quality_ref, out_ref, extra_ref):
    zl = lax.axis_index("zl")
    quarter = lax.axis_index("zh") * 2 + lax.axis_index("core")
    for group in range(N_GROUP):
        offset = ((zl - group % 4 + 1) & 3) - 1
        source = jnp.clip(group + offset, 0, N_GROUP - 1) >> 2
        out_ref[group, 0:16, :] = base_ref[source, 0]
        out_ref[group, 16:32, :] = mon_ref[source, 0]
    extra_ref[0:16, :] = quality_ref[0, 0]
    rows = lax.broadcasted_iota(jnp.int32, (SUB, 512), 0)
    bands = jnp.zeros((SUB, 512), F32)
    for block in range(2):
        for slot in range(KB):
            band = bands_ref[0, block, slot, quarter].astype(F32)
            bands = jnp.where(rows == block * KB + slot, band, bands)
    extra_ref[16:24, :] = bands


def block_terms(base, padded, bands, lane):
    weight = jnp.zeros(base.shape, F32)
    moment = jnp.zeros(base.shape, F32)
    for band in bands:
        like_sum = jnp.zeros(base.shape, F32)
        step_sum = jnp.zeros(base.shape, F32)
        for quad in range(BAND // 4):
            terms = []
            for step in range(quad * 4, quad * 4 + 4):
                start = band * BAND + step
                turned = pltpu.roll(padded, (LANES - start) & (LANES - 1), 1)
                window = jnp.where(lane < LANES - start, turned[0:32], turned[8:40])
                difference = base - window
                misfit = (difference * difference).astype(jnp.bfloat16)
                terms.append(1.0 + misfit.astype(F32))
            a, b, c, d = terms
            left, right = a * b, c * d
            inverse = pl.reciprocal(left * right, approx=False)
            first, second = right * inverse, left * inverse
            low, high = (a + b) * first, (c + d) * second
            like_sum += low + high
            step_sum += a * first + c * second + 2.0 * high
            if quad:
                step_sum += (4.0 * quad) * (low + high)
        lag = (band * BAND - HALF).astype(F32)
        weight += like_sum
        moment += (lag * like_sum + step_sum) * (1.0 / HALF)
    scale = 1.0 / (KB * BAND)
    return weight * scale, moment * scale


def spread(value, lane, zero):
    turned = [roll(value[c * 8 : c * 8 + 8], 8, 1) for c in range(4)]
    sides = [zero] + turned + [zero]
    return [jnp.where(lane < 8, sides[i], sides[i + 1]) for i in range(5)]


def code(weight, target):
    high = (jnp.sqrt(weight * 0.5) * 65535.0 + 0.5).astype(jnp.int32)
    low = (jnp.sqrt(jnp.sqrt(jnp.abs(target) * 0.5)) * 32767.0 + 0.5).astype(jnp.int32)
    low = jnp.where(target < 0.0, -low, low)
    return (high << 16) | (low & 65535)


def decode(coded):
    high = lax.shift_right_logical(coded, 16).astype(F32) * (2.0**0.5 / 65535.0)
    low = ((coded << 16) >> 16).astype(F32) * (2.0**0.25 / 32767.0)
    return high * high, low * jnp.abs(low) * (low * low)


def make_fields(recv_ref, below_ref, own_ref, above_ref, out_ref, target_ref):
    zl = lax.axis_index("zl")
    lane32 = lax.broadcasted_iota(jnp.int32, (32, LANES), 1)
    lane = lane_ids()
    zero = jnp.zeros((SUB, LANES), F32)
    empty = jnp.zeros((SUB, LANES), jnp.int32)
    exact, coded = [None] * 4, []
    for trace, extra_ref in enumerate((below_ref, own_ref, above_ref)):
        slot0 = (zl + trace - 1) & 3
        for block in range(2):
            rows = slice(block * 8, block * 8 + 8)
            mon_rows = slice(16 + block * 8, 24 + block * 8)
            base = jnp.concatenate([recv_ref[4 * c + slot0, rows, :] for c in range(4)], axis=0)
            turned = [roll(recv_ref[4 * c + slot0, mon_rows, :], 64, 1) for c in range(4)]
            sides = [zero] + turned + [zero]
            padded = jnp.concatenate(
                [jnp.where(lane < 64, sides[i], sides[i + 1]) for i in range(5)], axis=0
            )
            bands = [
                jnp.max(extra_ref[16 + block * KB + s : 17 + block * KB + s, 0:LANES]).astype(jnp.int32)
                for s in range(KB)
            ]
            weight, moment = block_terms(base, padded, bands, lane32)
            quality = jnp.concatenate(
                [extra_ref[rows, c * LANES : (c + 1) * LANES] for c in range(4)], axis=0
            )
            weight, moment = weight * quality, moment * quality
            if trace == 1:
                target_ref[block] = moment
                exact[block] = spread((weight * FIXED).astype(jnp.int32), lane, empty)
                exact[2 + block] = spread((moment * FIXED).astype(jnp.int32), lane, empty)
            else:
                coded.append(spread(code(weight, moment), lane, empty))
    for at, fields in enumerate((exact, coded)):
        for piece in range(N_PLANE):
            part, offset = piece // 8, 16 * (piece % 8)
            packed = None
            for g, vregs in enumerate(fields):
                shift = (32 * g - offset) % LANES
                value = roll(vregs[part], shift, 1)
                if piece % 8 == 7:
                    value = jnp.where(lane < 32 * g + 16, value, roll(vregs[part + 1], shift, 1))
                packed = value if packed is None else jnp.where(lane < 32 * g, packed, value)
            out_ref[piece, at * 8 : at * 8 + 8, :] = packed


def beside(values, lane, row):
    low, high = values
    next_low, next_high = roll(low, 7, 1), roll(high, 7, 1)
    turn_low, turn_high = roll(next_low, 96, 2), roll(next_high, 96, 2)
    last = row == 7
    up_low = jnp.where(last, jnp.where(lane < 96, turn_low, turn_high), next_low)
    up_high = jnp.where(last, jnp.where(lane < 96, turn_high, 0.0), next_high)
    prev_low, prev_high = roll(low, 1, 1), roll(high, 1, 1)
    turn_low, turn_high = roll(prev_low, 32, 2), roll(prev_high, 32, 2)
    first = row == 0
    down_low = jnp.where(first, jnp.where(lane < 32, 0.0, turn_low), prev_low)
    down_high = jnp.where(first, jnp.where(lane < 32, turn_low, turn_high), prev_high)
    return up_low + down_low, up_high + down_high


CHUNK = 2


def powers(recv_ref, out_ref, diag_ref, basis_ref):
    group = lax.axis_index("zh") * 8 + lax.axis_index("core") * 4 + lax.axis_index("zl")
    slab = lax.axis_index("y") * 4 + lax.axis_index("x")
    lane, row = lane_ids(), row_ids()
    tau = lane & 31
    time = slab * 16 - 8 + tau
    inside = ((time >= 0) & (time < 512)).astype(F32)
    shares = [
        inside * (group > 0).astype(F32),
        inside,
        inside * (group < N_GROUP - 1).astype(F32),
    ]
    space = [share * (2.0 * smooth_space / CENTRE) for share in shares]
    along = [share * (2.0 * smooth_time / CENTRE) for share in shares]
    def place(inline, weight, target):
        centre = weight + (4.0 * smooth_space + 2.0 * smooth_time - CENTRE)
        diag_ref[v, inline] = centre * (shares[inline // 8] * (2.0 / CENTRE))
        basis_ref[0, v, inline] = target

    for y in range(8):
        for v in range(2):
            joined = []
            for at in range(2):
                even = recv_ref[y * 4 + 2 * v, at * 8 : at * 8 + 8, :]
                odd = recv_ref[y * 4 + 2 * v + 1, at * 8 : at * 8 + 8, :]
                joined.append(jnp.where(lane < 64, even, roll(odd, 64, 1)))
                joined.append(jnp.where(lane < 64, roll(even, 64, 1), odd))
            place(8 + y, joined[0].astype(F32) * (1.0 / FIXED), joined[1].astype(F32) * (1.0 / FIXED))
            place(y, *decode(joined[2]))
            place(16 + y, *decode(joined[3]))
    lane3 = lax.broadcasted_iota(jnp.int32, (CHUNK, SUB, LANES), 2)
    row3 = lax.broadcasted_iota(jnp.int32, (CHUNK, SUB, LANES), 1)
    own = (tau >= 8) & (tau < 24)
    squares, crosses = [], []
    for level in range(ITERS):
        square = jnp.zeros((CHUNK, SUB, LANES), F32)
        cross = jnp.zeros((CHUNK, SUB, LANES), F32)
        begin = level + 1 + ((level + 1) % CHUNK and -1)
        for inline in range(begin, DEPTH - begin, CHUNK):
            region = inline // 8
            here = slice(inline, inline + CHUNK)
            centre = [basis_ref[level, v, here] for v in range(2)]
            sides = beside(centre, lane3, row3)
            for v in range(2):
                if inline == 0:
                    inlines = jnp.concatenate([jnp.zeros((1, SUB, LANES), F32), basis_ref[level, v, 0 : CHUNK - 1]], axis=0)
                else:
                    inlines = basis_ref[level, v, inline - 1 : inline - 1 + CHUNK]
                if inline + CHUNK == DEPTH:
                    inlines = inlines + jnp.concatenate(
                        [basis_ref[level, v, inline + 1 : DEPTH], jnp.zeros((1, SUB, LANES), F32)], axis=0
                    )
                else:
                    inlines = inlines + basis_ref[level, v, inline + 1 : inline + 1 + CHUNK]
                times = roll(centre[v], 1, 2) + roll(centre[v], LANES - 1, 2)
                image = (
                    diag_ref[v, here] * centre[v]
                    - space[region] * (inlines + sides[v])
                    - along[region] * times
                )
                image = 0.5 * image if level == 0 else image - basis_ref[level - 1, v, here]
                basis_ref[level + 1, v, here] = image
                if region == 1:
                    square += centre[v] * centre[v]
                    cross += centre[v] * image
        squares.append(jnp.where(own, jnp.sum(square, axis=0), 0.0))
        crosses.append(jnp.where(own, jnp.sum(cross, axis=0), 0.0))
    tiles = []
    for values in (squares, crosses):
        for amount in (4, 2, 1):
            values = [
                jnp.where(
                    (row & amount) == 0, a + roll(a, 8 - amount, 0), b + roll(b, amount, 0)
                )
                for a, b in zip(values[:amount], values[amount:])
            ]
        tile = values[0]
        for amount in (64, 32, 16, 8):
            tile = tile + roll(tile, amount, 1)
        tiles.append(tile)
    tile = jnp.where(((lane >> 3) & 7) == row, jnp.where(lane < 64, tiles[0], tiles[1]), 0.0)
    for amount in (4, 2, 1):
        tile = tile + roll(tile, amount, 0)
    for y in range(8):
        for v in range(2):
            pairs = []
            for k in range(1, 9, 2):
                pairs.append(
                    jnp.where(
                        tau < 16,
                        roll(basis_ref[k, v, 8 + y], 120, 1),
                        roll(basis_ref[k + 1, v, 8 + y], 8, 1),
                    )
                )
            turned = [roll(pair, 64, 1) for pair in pairs]
            for half in range(2):
                low, high = (pairs, turned) if half == 0 else (turned, pairs)
                piece = y * 4 + 2 * v + half
                for part in range(2):
                    at = piece * ROWS + part * 8
                    out_ref[at : at + 8, :] = jnp.where(
                        lane < 64, low[2 * part], high[2 * part + 1]
                    )
                out_ref[piece * ROWS + 16 : piece * ROWS + 17, :] = tile[0:1]


def spread_sums(recv_ref, out_ref):
    terms = [recv_ref[piece * ROWS + 16 : piece * ROWS + 17, :] for piece in range(N_PLANE)]
    while len(terms) > 1:
        terms = [terms[k] + terms[k + 1] for k in range(0, len(terms), 2)]
    out_ref[...] = jnp.broadcast_to(terms[0], (N_GROUP, LANES))


def two_sum(a, b):
    total = a + b
    part = total - a
    return total, (a - (total - part)) + (b - part)


def split(a):
    scaled = 4097.0 * a
    high = scaled - (scaled - a)
    return high, a - high


def across(tile, k):
    return jnp.broadcast_to(tile[k : k + 1], (SUB, LANES))


def lift(pair, turn):
    return tuple(turn(part) for part in pair)


def choose(mask, first, second):
    return tuple(jnp.where(mask, a, b) for a, b in zip(first, second))


def add_pairs(first, second):
    total, error = two_sum(first[0], second[0])
    return two_sum(total, error + (first[1] + second[1]))


def solve(total, lane, row, turn):
    zero = jnp.zeros((SUB, LANES), F32)
    fold = total
    for amount in (4, 2, 1):
        fold = add_pairs(fold, lift(fold, lambda part: turn(part, amount, 0)))
    for amount in (124, 126, 127):
        fold = add_pairs(fold, lift(fold, lambda part: turn(part, amount, 1)))

    def at_lane(pair, k):
        return lift(pair, lambda part: jnp.broadcast_to(part[:, k : k + 1], (SUB, LANES)))

    start = choose(lane < 64, at_lane(fold, 0), at_lane(fold, 64))
    doubled = add_pairs(lift(fold, lambda part: 2.0 * part), lift(start, lambda part: -part))
    moments = [at_lane(doubled, 64 * (k % 2) + 8 * (k // 2)) for k in range(2 * ITERS)]

    def column(values):
        out = values[0]
        for k in range(1, SUB):
            out = choose(row < k, out, values[k])
        return out

    ahead, beyond, behind = column(moments[:8]), column(moments[8:]), column(moments[8:0:-1])
    gram = []
    for k in range(ITERS + 1):
        later = choose(
            row < 8 - k,
            lift(ahead, lambda part: turn(part, (8 - k) % 8, 0)),
            lift(beyond, lambda part: turn(part, (8 - k) % 8, 0)),
        )
        earlier = choose(
            row < k,
            lift(behind, lambda part: turn(part, k % 8, 0)),
            lift(ahead, lambda part: turn(part, k % 8, 0)),
        )
        gram.append(add_pairs(later, earlier))
    inverse = [gram[k][0] + 0.5 * (gram[k + 1][0] + gram[abs(k - 1)][0]) for k in range(ITERS)]
    for k in range(ITERS):
        reciprocal = 1.0 / across(inverse[k], k)
        pivot = inverse[k]
        for j in range(ITERS):
            if j != k:
                share = across(inverse[j], k) * reciprocal
                inverse[j] = jnp.where(row == k, share, inverse[j] - pivot * share)
        inverse[k] = jnp.where(row == k, reciprocal, -pivot * reciprocal)

    def apply_inverse(right):
        terms = [inverse[k] * across(right, k) for k in range(ITERS)]
        while len(terms) > 1:
            terms = [terms[k] + terms[k + 1] for k in range(0, len(terms), 2)]
        return terms[0]

    def remainder(series):
        def lower(part):
            return jnp.where(row == 0, 0.0, jnp.where(row == 1, 1.0, 0.5) * turn(part, 1, 0))

        def upper(part):
            return jnp.where(row == 7, 0.0, 0.5 * turn(part, 7, 0))

        image = add_pairs(add_pairs(lift(series, lower), lift(series, upper)), series)
        start = (jnp.where(row == 0, 1.0, 0.0), zero)
        return add_pairs(start, lift(image, lambda part: -part)), lift(series, lambda part: -0.5 * across(part, 7))

    parts = [split(pair[0]) for pair in gram]
    series = (apply_inverse(gram[0][0]), zero)
    steps = []
    for _ in range(2):
        body, top = remainder(series)
        high, low = zero, zero
        for k in range(ITERS + 1):
            a, a_low = lift(body, lambda part: across(part, k)) if k < ITERS else top
            b, b_low = gram[k]
            (a0, a1), (b0, b1) = split(a), parts[k]
            product = a * b
            error = (((a0 * b0 - product) + a0 * b1) + a1 * b0) + a1 * b1
            high, rest = two_sum(high, product)
            low = low + (rest + (error + (a * b_low + a_low * b)))
        change = apply_inverse(high + low)
        steps.append(change)
        series = two_sum(series[0], series[1] + change)
    body, top = remainder(series)
    return (series[0] + series[1]) * (1.0 / CENTRE), body[0] + body[1], top[0] + top[1], steps, series[0]


def combine(basis_ref, sums_ref, target_ref, shift_ref, residual_ref, again_ref):
    lane, row = lane_ids(), row_ids()
    zero = jnp.zeros((SUB, LANES), F32)
    total = two_sum(sums_ref[0:8, :], sums_ref[8:16, :])
    shift, residual, last, steps, series = solve(total, lane, row, roll)
    fine = jnp.max(jnp.abs(steps[0])) <= TRUST * jnp.max(jnp.abs(series))
    again_ref[0] = 1 - fine.astype(jnp.int32)
    first = (lane & 31) < 16
    for body, top, out_ref in ((shift, zero, shift_ref), (residual, last, residual_ref)):
        terms = [across(body, k) for k in range(ITERS)] + [top]
        low, high = (
            jnp.where(
                lane < 64,
                jnp.where(first, terms[k], terms[k + 1]),
                jnp.where(first, terms[k + 2], terms[k + 3]),
            )
            for k in (1, 5)
        )
        for part in range(4):
            packed = [None, None]
            for step in range(8):
                piece = part * 8 + step
                at = piece * ROWS
                value = low * basis_ref[at : at + 8, :] + high * basis_ref[at + 8 : at + 16, :]
                value = value + roll(value, 64, 1)
                value = value + roll(value, 112, 1)
                for h in range(2):
                    turned = roll(value, (16 * step - 32 * h) % LANES, 1)
                    packed[h] = turned if step == 0 else jnp.where(lane < 16 * step, packed[h], turned)
            for h in range(2):
                out_ref[0, 0, h * 8 : h * 8 + 8, part * LANES : (part + 1) * LANES] = (
                    packed[h] + terms[0] * target_ref[h, part * 8 : part * 8 + 8, :]
                )


def limit(mebibytes):
    return pltpu.CompilerParams(vmem_limit_bytes=mebibytes * 1024 * 1024)


def arrays(*shapes):
    return [jax.ShapeDtypeStruct(shape, F32) for shape in shapes]


def padded_2(value, sides, width):
    for axis, dim in sides:
        size, length = (lax.axis_size(axis), value.shape[dim])
        up = [(i, (i + 1) % size) for i in range(size - 1)]
        down = [(j, i) for i, j in up]
        last = lax.slice_in_dim(value, length - width, length, axis=dim)
        first = lax.slice_in_dim(value, 0, width, axis=dim)
        before = lax.ppermute(last, axis, up)
        after = lax.ppermute(first, axis, down)
        value = jnp.concatenate([before, value, after], axis=dim)
    return value


def slot_window(block, band):
    start = band * BAND
    return lax.dynamic_slice(
        block, (jnp.int32(0), start), (block.shape[0], block.shape[1] - LAGS + BAND)
    )


def lag_table(band_list):
    steps = jnp.arange(BAND, dtype=jnp.float32)
    return (band_list.astype(jnp.float32)[..., None] * BAND + steps - HALF) / HALF


def moments(errors, lags):
    likeness = 1.0 / (1.0 + errors.astype(jnp.float32))
    weight_sum = jnp.sum(likeness, axis=(3, 4)) / (KB * BAND)
    moment_sum = jnp.sum(lags[..., None, None] * likeness, axis=(3, 4)) / (KB * BAND)
    return (weight_sum, moment_sum)


def operate(field, weight):
    padded = padded_2(field, ((FILT + IL, 0), ("x", 1)), 1)
    centre = padded[1:-1, 1:-1, :]
    across = (
        4.0 * centre
        - padded[2:, 1:-1, :]
        - padded[:-2, 1:-1, :]
        - padded[1:-1, 2:, :]
        - padded[1:-1, :-2, :]
    )
    timed = jnp.pad(field, ((0, 0), (0, 0), (1, 1)))
    along = 2.0 * field - timed[:, :, 2:] - timed[:, :, :-2]
    return weight * field + smooth_space * across + smooth_time * along


def squares(residual):
    return lax.psum(jnp.sum(residual * residual), FILT + IL + ("x",))


def step_by_step(baseline, monitor, band_ids, quality):
    quarters, inline_rows, cross_rows, samples = baseline.shape
    cross_blocks = cross_rows // BXL
    extended = padded_2(monitor, ((FILT, 3),), HALF)
    ext_blocks = extended.reshape(quarters, inline_rows, cross_blocks, BXL, samples + LAGS)
    base_blocks = baseline.reshape(quarters, inline_rows, cross_blocks, BXL, samples)
    per_slot = jax.vmap(slot_window, in_axes=(None, 0))
    windows = jax.vmap(jax.vmap(jax.vmap(per_slot)))(ext_blocks, band_ids)
    errors = jnp.stack(
        [
            jnp.square(
                base_blocks[:, :, :, None] - windows[..., lag_step : lag_step + samples]
            ).astype(jnp.bfloat16)
            for lag_step in range(BAND)
        ],
        axis=4,
    )
    local_weight, local_moment = moments(errors, lag_table(band_ids))
    weight_raw, moment_raw = (
        lax.all_to_all(local_weight, FILT, split_axis=0, concat_axis=4, tiled=True),
        lax.all_to_all(local_moment, FILT, split_axis=0, concat_axis=4, tiled=True),
    )
    total_time = weight_raw.shape[-1]
    quality_grid = quality.reshape(inline_rows, cross_rows, total_time)
    weight = quality_grid * weight_raw.reshape(inline_rows, cross_rows, total_time)
    target = quality_grid * moment_raw.reshape(inline_rows, cross_rows, total_time)
    shift = jnp.zeros_like(target)
    residual = target
    direction = target
    norm_now = squares(residual)
    for iteration in range(ITERS):
        image = operate(direction, weight)
        alpha = norm_now / lax.psum(jnp.sum(direction * image), FILT + IL + ("x",))
        shift = shift + alpha * direction
        residual = residual - alpha * image
        norm_next = squares(residual)
        direction = residual + norm_next / norm_now * direction
        norm_now = norm_next
    out_shape = (1, inline_rows, cross_rows, total_time)
    return (shift.reshape(out_shape), residual.reshape(out_shape))


def exchange(rows, axes, count):
    pieces = lax.all_to_all(rows.reshape(-1, count, 1, LANES), axes, 0, 0, tiled=True)
    return pieces.reshape(rows.shape)


def kernel(body, out_shape, mebibytes, **options):
    return pl.pallas_call(
        body, out_shape=out_shape, compiler_params=limit(mebibytes), name=body.__name__, **options
    )


def per_device(baseline, monitor, band_ids, quality):
    pieces, extra = pl.pallas_call(
        pack_inputs,
        out_shape=arrays((N_GROUP, 32, LANES), (DEPTH, 512)),
        in_specs=[VMEM, VMEM, SMEM, VMEM],
        name="pack_inputs",
    )(baseline, monitor, band_ids.transpose(1, 2, 3, 0), quality)
    below = lax.ppermute(extra, GROUP, [(i, i + 1) for i in range(N_GROUP - 1)])
    above = lax.ppermute(extra, GROUP, [(i + 1, i) for i in range(N_GROUP - 1)])
    pieces = lax.all_to_all(pieces, GROUP, 0, 0, tiled=True)
    pieces, target = kernel(
        make_fields,
        [jax.ShapeDtypeStruct((N_PLANE, 16, LANES), jnp.int32)] + arrays((2, 32, LANES)),
        8,
    )(
        pieces, below, extra, above
    )
    pieces = lax.all_to_all(pieces, PLANE, 0, 0, tiled=True)
    (pieces,) = kernel(
        powers,
        arrays((N_PLANE * ROWS, LANES)),
        8,
        scratch_shapes=[
            pltpu.VMEM((2, DEPTH, SUB, LANES), F32),
            pltpu.VMEM((ITERS + 1, 2, DEPTH, SUB, LANES), F32),
        ],
    )(pieces)
    pieces = exchange(pieces, PLANE, ROWS)
    (sums,) = kernel(spread_sums, arrays((N_GROUP, LANES)), 4)(pieces)
    sums = exchange(sums, GROUP, 1)
    shift, residual, again = kernel(
        combine,
        arrays((1, 1, 16, 512), (1, 1, 16, 512)) + [jax.ShapeDtypeStruct((1,), jnp.int32)],
        4,
        out_specs=[VMEM, VMEM, SMEM],
    )(pieces, sums, target)

    def unsettled(state):
        return state[2][0] != 0

    def apart(state):
        return step_by_step(baseline, monitor, band_ids, quality) + (jnp.zeros((1,), jnp.int32),)

    return lax.while_loop(unsettled, apart, (shift, residual, again))[:2]


def solution(mesh):
    fine = Mesh(mesh.devices.reshape(2, 2, 4, 8, 4), ("zh", "core", "zl", "y", "x"))
    outs = P(FILT, IL, "x", None)
    in_specs = (P(None, IL, "x", FILT), P(None, IL, "x", FILT), P(None, IL, "x", None), outs)
    return jax.shard_map(
        per_device, mesh=fine, in_specs=in_specs, out_specs=(outs, outs), check_vma=False
    )
```

```python
import jax
import jax.numpy as jnp
from jax import lax
from jax.experimental import pallas as pl
from jax.experimental.pallas import tpu as pltpu
from jax.sharding import Mesh, PartitionSpec as P

BAND = 8
KB = 2
BXL = 8
HALF = 64
ITERS = 8
LANES = 128
SUB = 8

smooth_space = 4.0
smooth_time = 1.0
CENTRE = 19.0

GROUP = ("zh", "core", "zl")
PLANE = ("y", "x")
N_GROUP = 16
N_PLANE = 32
ROWS = 17
FIXED = 2.0**29
DEPTH = 24
FILT, IL = ("zh", "core"), ("zl", "y")
LAGS = 128
TRUST = 3e-4
HBM = pl.BlockSpec(memory_space=pltpu.HBM)
VMEM = pl.BlockSpec(memory_space=pltpu.VMEM)
SMEM = pl.BlockSpec(memory_space=pltpu.SMEM)
F32 = jnp.float32


def lane_ids():
    return lax.broadcasted_iota(jnp.int32, (SUB, LANES), 1)


def row_ids():
    return lax.broadcasted_iota(jnp.int32, (SUB, LANES), 0)


def roll(value, amount, axis):
    return pltpu.roll(value, amount, axis) if amount else value


def pack_inputs(
    base_hbm, mon_hbm, quality_hbm, bands_hbm, out_ref, extra_ref, base_ref, mon_ref, bands_ref, sems
):
    copies = [
        pltpu.make_async_copy(source, target, sems.at[k])
        for k, (source, target) in enumerate(
            (
                (bands_hbm, bands_ref),
                (base_hbm, base_ref),
                (mon_hbm, mon_ref),
                (quality_hbm.at[0, 0], extra_ref.at[0:16]),
            )
        )
    ]
    for copy in copies:
        copy.start()
    zl = lax.axis_index("zl")
    quarter = lax.axis_index("zh") * 2 + lax.axis_index("core")
    for copy in copies:
        copy.wait()
    for group in range(N_GROUP):
        offset = ((zl - group % 4 + 1) & 3) - 1
        source = jnp.clip(group + offset, 0, N_GROUP - 1) >> 2
        out_ref[group, 0:16, :] = base_ref[source, 0]
        out_ref[group, 16:32, :] = mon_ref[source, 0]
    rows = lax.broadcasted_iota(jnp.int32, (SUB, 512), 0)
    bands = jnp.zeros((SUB, 512), F32)
    for block in range(2):
        for slot in range(KB):
            band = bands_ref[0, block, slot, quarter].astype(F32)
            bands = jnp.where(rows == block * KB + slot, band, bands)
    extra_ref[16:24, :] = bands


def block_terms(base, padded, bands, lane):
    weight = jnp.zeros(base.shape, F32)
    moment = jnp.zeros(base.shape, F32)
    for band in bands:
        like_sum = jnp.zeros(base.shape, F32)
        step_sum = jnp.zeros(base.shape, F32)
        for quad in range(BAND // 4):
            terms = []
            for step in range(quad * 4, quad * 4 + 4):
                start = band * BAND + step
                turned = pltpu.roll(padded, (LANES - start) & (LANES - 1), 1)
                window = jnp.where(lane < LANES - start, turned[0:32], turned[8:40])
                difference = base - window
                misfit = (difference * difference).astype(jnp.bfloat16)
                terms.append(1.0 + misfit.astype(F32))
            a, b, c, d = terms
            left, right = a * b, c * d
            inverse = pl.reciprocal(left * right, approx=False)
            first, second = right * inverse, left * inverse
            low, high = (a + b) * first, (c + d) * second
            like_sum += low + high
            step_sum += a * first + c * second + 2.0 * high
            if quad:
                step_sum += (4.0 * quad) * (low + high)
        lag = (band * BAND - HALF).astype(F32)
        weight += like_sum
        moment += (lag * like_sum + step_sum) * (1.0 / HALF)
    scale = 1.0 / (KB * BAND)
    return weight * scale, moment * scale


def spread(value, lane, zero):
    turned = [roll(value[c * 8 : c * 8 + 8], 8, 1) for c in range(4)]
    sides = [zero] + turned + [zero]
    return [jnp.where(lane < 8, sides[i], sides[i + 1]) for i in range(5)]


def code(weight, target):
    high = (jnp.sqrt(weight * 0.5) * 65535.0 + 0.5).astype(jnp.int32)
    low = (jnp.sqrt(jnp.sqrt(jnp.abs(target) * 0.5)) * 32767.0 + 0.5).astype(jnp.int32)
    low = jnp.where(target < 0.0, -low, low)
    return (high << 16) | (low & 65535)


def decode(coded):
    high = lax.shift_right_logical(coded, 16).astype(F32) * (2.0**0.5 / 65535.0)
    low = ((coded << 16) >> 16).astype(F32) * (2.0**0.25 / 32767.0)
    return high * high, low * jnp.abs(low) * (low * low)


def make_fields(recv_ref, below_ref, own_ref, above_ref, out_ref, target_ref):
    zl = lax.axis_index("zl")
    lane32 = lax.broadcasted_iota(jnp.int32, (32, LANES), 1)
    lane = lane_ids()
    zero = jnp.zeros((SUB, LANES), F32)
    empty = jnp.zeros((SUB, LANES), jnp.int32)
    exact, coded = [None] * 4, []
    for trace, extra_ref in enumerate((below_ref, own_ref, above_ref)):
        slot0 = (zl + trace - 1) & 3
        for block in range(2):
            rows = slice(block * 8, block * 8 + 8)
            mon_rows = slice(16 + block * 8, 24 + block * 8)
            base = jnp.concatenate([recv_ref[4 * c + slot0, rows, :] for c in range(4)], axis=0)
            turned = [roll(recv_ref[4 * c + slot0, mon_rows, :], 64, 1) for c in range(4)]
            sides = [zero] + turned + [zero]
            padded = jnp.concatenate(
                [jnp.where(lane < 64, sides[i], sides[i + 1]) for i in range(5)], axis=0
            )
            bands = [
                jnp.max(extra_ref[16 + block * KB + s : 17 + block * KB + s, 0:LANES]).astype(jnp.int32)
                for s in range(KB)
            ]
            weight, moment = block_terms(base, padded, bands, lane32)
            quality = jnp.concatenate(
                [extra_ref[rows, c * LANES : (c + 1) * LANES] for c in range(4)], axis=0
            )
            weight, moment = weight * quality, moment * quality
            if trace == 1:
                target_ref[block] = moment
                exact[block] = spread((weight * FIXED).astype(jnp.int32), lane, empty)
                exact[2 + block] = spread((moment * FIXED).astype(jnp.int32), lane, empty)
            else:
                coded.append(spread(code(weight, moment), lane, empty))
    for at, fields in enumerate((exact, coded)):
        for piece in range(N_PLANE):
            part, offset = piece // 8, 16 * (piece % 8)
            packed = None
            for g, vregs in enumerate(fields):
                shift = (32 * g - offset) % LANES
                value = roll(vregs[part], shift, 1)
                if piece % 8 == 7:
                    value = jnp.where(lane < 32 * g + 16, value, roll(vregs[part + 1], shift, 1))
                packed = value if packed is None else jnp.where(lane < 32 * g, packed, value)
            out_ref[piece, at * 8 : at * 8 + 8, :] = packed


def swap_halves(low, high, lane):
    turned = roll(jnp.where(lane < 64, high, low), 64, 1)
    return jnp.where(lane < 64, low, turned), jnp.where(lane < 64, turned, high)


def beside(values, lane, row):
    low, high = values
    next_low, next_high = roll(low, 7, 1), roll(high, 7, 1)
    turn_low, turn_high = roll(next_low, 96, 2), roll(next_high, 96, 2)
    last = row == 7
    up_low = jnp.where(last, jnp.where(lane < 96, turn_low, turn_high), next_low)
    up_high = jnp.where(last, jnp.where(lane < 96, turn_high, 0.0), next_high)
    prev_low, prev_high = roll(low, 1, 1), roll(high, 1, 1)
    turn_low, turn_high = roll(prev_low, 32, 2), roll(prev_high, 32, 2)
    first = row == 0
    down_low = jnp.where(first, jnp.where(lane < 32, 0.0, turn_low), prev_low)
    down_high = jnp.where(first, jnp.where(lane < 32, turn_low, turn_high), prev_high)
    return up_low + down_low, up_high + down_high


CHUNK = 2


def chunks(begin, end):
    out = []
    while begin < end:
        stop = min(end, begin + CHUNK, (begin // 8 + 1) * 8)
        out.append((begin, stop))
        begin = stop
    return out


def powers(recv_ref, out_ref, diag_ref, basis_ref):
    group = lax.axis_index("zh") * 8 + lax.axis_index("core") * 4 + lax.axis_index("zl")
    slab = lax.axis_index("y") * 4 + lax.axis_index("x")
    lane, row = lane_ids(), row_ids()
    tau = lane & 31
    time = slab * 16 - 8 + tau
    inside = ((time >= 0) & (time < 512)).astype(F32)
    shares = [
        inside * (group > 0).astype(F32),
        inside,
        inside * (group < N_GROUP - 1).astype(F32),
    ]
    space = [share * (2.0 * smooth_space / CENTRE) for share in shares]
    along = [share * (2.0 * smooth_time / CENTRE) for share in shares]
    def place(inline, weight, target):
        centre = weight + (4.0 * smooth_space + 2.0 * smooth_time - CENTRE)
        diag_ref[v, inline] = centre * (shares[inline // 8] * (2.0 / CENTRE))
        basis_ref[0, v, inline] = target

    for y in range(8):
        for v in range(2):
            joined = []
            for at in range(2):
                even = recv_ref[y * 4 + 2 * v, at * 8 : at * 8 + 8, :]
                odd = recv_ref[y * 4 + 2 * v + 1, at * 8 : at * 8 + 8, :]
                joined += swap_halves(even, odd, lane)
            place(8 + y, joined[0].astype(F32) * (1.0 / FIXED), joined[1].astype(F32) * (1.0 / FIXED))
            place(y, *decode(joined[2]))
            place(16 + y, *decode(joined[3]))
    own = (tau >= 8) & (tau < 24)
    squares, crosses = [], []
    for level in range(ITERS):
        square = jnp.zeros((SUB, LANES), F32)
        cross = jnp.zeros((SUB, LANES), F32)
        for begin, end in chunks(level + 1, DEPTH - 1 - level):
            region, here = begin // 8, slice(begin, end)
            centre = [basis_ref[level, v, here] for v in range(2)]
            sides = beside(centre, lane[None], row[None])
            for v in range(2):
                inlines = basis_ref[level, v, begin - 1 : end - 1] + basis_ref[level, v, begin + 1 : end + 1]
                times = roll(centre[v], 1, 2) + roll(centre[v], LANES - 1, 2)
                image = (
                    diag_ref[v, here] * centre[v]
                    - space[region] * (inlines + sides[v])
                    - along[region] * times
                )
                image = 0.5 * image if level == 0 else image - basis_ref[level - 1, v, here]
                basis_ref[level + 1, v, here] = image
                if region == 1:
                    square += jnp.sum(centre[v] * centre[v], axis=0)
                    cross += jnp.sum(centre[v] * image, axis=0)
        squares.append(jnp.where(own, square, 0.0))
        crosses.append(jnp.where(own, cross, 0.0))
    tiles = []
    for values in (squares, crosses):
        for amount in (4, 2, 1):
            values = [
                jnp.where(
                    (row & amount) == 0, a + roll(a, 8 - amount, 0), b + roll(b, amount, 0)
                )
                for a, b in zip(values[:amount], values[amount:])
            ]
        tile = values[0]
        for amount in (64, 32, 16, 8):
            tile = tile + roll(tile, amount, 1)
        tiles.append(tile)
    tile = jnp.where(((lane >> 3) & 7) == row, jnp.where(lane < 64, tiles[0], tiles[1]), 0.0)
    for amount in (4, 2, 1):
        tile = tile + roll(tile, amount, 0)
    for y in range(8):
        for v in range(2):
            pairs = []
            for k in range(1, 9, 2):
                pairs.append(
                    jnp.where(
                        tau < 16,
                        roll(basis_ref[k, v, 8 + y], 120, 1),
                        roll(basis_ref[k + 1, v, 8 + y], 8, 1),
                    )
                )
            for part in range(2):
                for half, tile_half in enumerate(swap_halves(*pairs[2 * part : 2 * part + 2], lane)):
                    at = (y * 4 + 2 * v + half) * ROWS + part * 8
                    out_ref[at : at + 8, :] = tile_half
    for piece in range(N_PLANE):
        out_ref[piece * ROWS + 16 : piece * ROWS + 17, :] = tile[0:1]


def spread_sums(recv_ref, out_ref):
    terms = [recv_ref[piece * ROWS + 16 : piece * ROWS + 17, :] for piece in range(N_PLANE)]
    while len(terms) > 1:
        terms = [terms[k] + terms[k + 1] for k in range(0, len(terms), 2)]
    out_ref[...] = jnp.broadcast_to(terms[0], (N_GROUP, LANES))


def two_sum(a, b):
    total = a + b
    part = total - a
    return total, (a - (total - part)) + (b - part)


def split(a):
    scaled = 4097.0 * a
    high = scaled - (scaled - a)
    return high, a - high


def across(tile, k):
    return jnp.broadcast_to(tile[k : k + 1], (SUB, LANES))


def lift(pair, turn):
    return tuple(turn(part) for part in pair)


def choose(mask, first, second):
    return tuple(jnp.where(mask, a, b) for a, b in zip(first, second))


def add_pairs(first, second):
    total, error = two_sum(first[0], second[0])
    return two_sum(total, error + (first[1] + second[1]))


def solve(total, lane, row, turn):
    zero = jnp.zeros((SUB, LANES), F32)
    fold = total
    for amount in (4, 2, 1):
        fold = add_pairs(fold, lift(fold, lambda part: turn(part, amount, 0)))
    for amount in (124, 126, 127):
        fold = add_pairs(fold, lift(fold, lambda part: turn(part, amount, 1)))

    def at_lane(pair, k):
        return lift(pair, lambda part: jnp.broadcast_to(part[:, k : k + 1], (SUB, LANES)))

    start = choose(lane < 64, at_lane(fold, 0), at_lane(fold, 64))
    doubled = add_pairs(lift(fold, lambda part: 2.0 * part), lift(start, lambda part: -part))
    moments = [at_lane(doubled, 64 * (k % 2) + 8 * (k // 2)) for k in range(2 * ITERS)]

    def column(values):
        out = values[0]
        for k in range(1, SUB):
            out = choose(row < k, out, values[k])
        return out

    ahead, beyond, behind = column(moments[:8]), column(moments[8:]), column(moments[8:0:-1])
    gram = []
    for k in range(ITERS + 1):
        later = choose(
            row < 8 - k,
            lift(ahead, lambda part: turn(part, (8 - k) % 8, 0)),
            lift(beyond, lambda part: turn(part, (8 - k) % 8, 0)),
        )
        earlier = choose(
            row < k,
            lift(behind, lambda part: turn(part, k % 8, 0)),
            lift(ahead, lambda part: turn(part, k % 8, 0)),
        )
        gram.append(add_pairs(later, earlier))
    inverse = [gram[k][0] + 0.5 * (gram[k + 1][0] + gram[abs(k - 1)][0]) for k in range(ITERS)]
    for k in range(ITERS):
        reciprocal = 1.0 / across(inverse[k], k)
        pivot = inverse[k]
        for j in range(ITERS):
            if j != k:
                share = across(inverse[j], k) * reciprocal
                inverse[j] = jnp.where(row == k, share, inverse[j] - pivot * share)
        inverse[k] = jnp.where(row == k, reciprocal, -pivot * reciprocal)

    def apply_inverse(right):
        terms = [inverse[k] * across(right, k) for k in range(ITERS)]
        while len(terms) > 1:
            terms = [terms[k] + terms[k + 1] for k in range(0, len(terms), 2)]
        return terms[0]

    def remainder(series):
        def lower(part):
            return jnp.where(row == 0, 0.0, jnp.where(row == 1, 1.0, 0.5) * turn(part, 1, 0))

        def upper(part):
            return jnp.where(row == 7, 0.0, 0.5 * turn(part, 7, 0))

        image = add_pairs(add_pairs(lift(series, lower), lift(series, upper)), series)
        start = (jnp.where(row == 0, 1.0, 0.0), zero)
        return add_pairs(start, lift(image, lambda part: -part)), lift(series, lambda part: -0.5 * across(part, 7))

    parts = [split(pair[0]) for pair in gram]
    series = (apply_inverse(gram[0][0]), zero)
    steps = []
    for _ in range(2):
        body, top = remainder(series)
        high, low = zero, zero
        for k in range(ITERS + 1):
            a, a_low = lift(body, lambda part: across(part, k)) if k < ITERS else top
            b, b_low = gram[k]
            (a0, a1), (b0, b1) = split(a), parts[k]
            product = a * b
            error = (((a0 * b0 - product) + a0 * b1) + a1 * b0) + a1 * b1
            high, rest = two_sum(high, product)
            low = low + (rest + (error + (a * b_low + a_low * b)))
        change = apply_inverse(high + low)
        steps.append(change)
        series = two_sum(series[0], series[1] + change)
    body, top = remainder(series)
    return (series[0] + series[1]) * (1.0 / CENTRE), body[0] + body[1], top[0] + top[1], steps, series[0]


def combine(basis_ref, sums_ref, target_ref, shift_ref, residual_ref, again_ref):
    lane, row = lane_ids(), row_ids()
    zero = jnp.zeros((SUB, LANES), F32)
    total = two_sum(sums_ref[0:8, :], sums_ref[8:16, :])
    shift, residual, last, steps, series = solve(total, lane, row, roll)
    fine = jnp.max(jnp.abs(steps[0])) <= TRUST * jnp.max(jnp.abs(series))
    again_ref[0] = 1 - fine.astype(jnp.int32)
    first = (lane & 31) < 16
    for body, top, out_ref in ((shift, zero, shift_ref), (residual, last, residual_ref)):
        terms = [across(body, k) for k in range(ITERS)] + [top]
        low, high = (
            jnp.where(
                lane < 64,
                jnp.where(first, terms[k], terms[k + 1]),
                jnp.where(first, terms[k + 2], terms[k + 3]),
            )
            for k in (1, 5)
        )
        for part in range(4):
            def piece(step):
                at = (part * 8 + step) * ROWS
                return low * basis_ref[at : at + 8, :] + high * basis_ref[at + 8 : at + 16, :]

            def quad(step):
                halves = []
                for near in (step, step + 1):
                    a, b = piece(near), piece(near + 4)
                    halves.append(jnp.where(lane < 64, a, b) + roll(jnp.where(lane < 64, b, a), 64, 1))
                a, b = halves
                return jnp.where(first, a + roll(a, 112, 1), b + roll(b, 16, 1))

            even, odd = quad(0), quad(2)
            lower = (lane & 32) == 0
            blocks = (
                jnp.where(lower, even, roll(odd, 32, 1)),
                jnp.where(lower, roll(even, 96, 1), odd),
            )
            for h in range(2):
                out_ref[0, 0, h * 8 : h * 8 + 8, part * LANES : (part + 1) * LANES] = (
                    blocks[h] + terms[0] * target_ref[h, part * 8 : part * 8 + 8, :]
                )


def limit(mebibytes):
    return pltpu.CompilerParams(vmem_limit_bytes=mebibytes * 1024 * 1024)


def arrays(*shapes):
    return [jax.ShapeDtypeStruct(shape, F32) for shape in shapes]


def padded_2(value, sides, width):
    for axis, dim in sides:
        size, length = (lax.axis_size(axis), value.shape[dim])
        up = [(i, (i + 1) % size) for i in range(size - 1)]
        down = [(j, i) for i, j in up]
        last = lax.slice_in_dim(value, length - width, length, axis=dim)
        first = lax.slice_in_dim(value, 0, width, axis=dim)
        before = lax.ppermute(last, axis, up)
        after = lax.ppermute(first, axis, down)
        value = jnp.concatenate([before, value, after], axis=dim)
    return value


def slot_window(block, band):
    start = band * BAND
    return lax.dynamic_slice(
        block, (jnp.int32(0), start), (block.shape[0], block.shape[1] - LAGS + BAND)
    )


def lag_table(band_list):
    steps = jnp.arange(BAND, dtype=jnp.float32)
    return (band_list.astype(jnp.float32)[..., None] * BAND + steps - HALF) / HALF


def moments(errors, lags):
    likeness = 1.0 / (1.0 + errors.astype(jnp.float32))
    weight_sum = jnp.sum(likeness, axis=(3, 4)) / (KB * BAND)
    moment_sum = jnp.sum(lags[..., None, None] * likeness, axis=(3, 4)) / (KB * BAND)
    return (weight_sum, moment_sum)


def operate(field, weight):
    padded = padded_2(field, ((FILT + IL, 0), ("x", 1)), 1)
    centre = padded[1:-1, 1:-1, :]
    across = (
        4.0 * centre
        - padded[2:, 1:-1, :]
        - padded[:-2, 1:-1, :]
        - padded[1:-1, 2:, :]
        - padded[1:-1, :-2, :]
    )
    timed = jnp.pad(field, ((0, 0), (0, 0), (1, 1)))
    along = 2.0 * field - timed[:, :, 2:] - timed[:, :, :-2]
    return weight * field + smooth_space * across + smooth_time * along


def squares(residual):
    return lax.psum(jnp.sum(residual * residual), FILT + IL + ("x",))


def step_by_step(baseline, monitor, band_ids, quality):
    quarters, inline_rows, cross_rows, samples = baseline.shape
    cross_blocks = cross_rows // BXL
    extended = padded_2(monitor, ((FILT, 3),), HALF)
    ext_blocks = extended.reshape(quarters, inline_rows, cross_blocks, BXL, samples + LAGS)
    base_blocks = baseline.reshape(quarters, inline_rows, cross_blocks, BXL, samples)
    per_slot = jax.vmap(slot_window, in_axes=(None, 0))
    windows = jax.vmap(jax.vmap(jax.vmap(per_slot)))(ext_blocks, band_ids)
    errors = jnp.stack(
        [
            jnp.square(
                base_blocks[:, :, :, None] - windows[..., lag_step : lag_step + samples]
            ).astype(jnp.bfloat16)
            for lag_step in range(BAND)
        ],
        axis=4,
    )
    local_weight, local_moment = moments(errors, lag_table(band_ids))
    weight_raw, moment_raw = (
        lax.all_to_all(local_weight, FILT, split_axis=0, concat_axis=4, tiled=True),
        lax.all_to_all(local_moment, FILT, split_axis=0, concat_axis=4, tiled=True),
    )
    total_time = weight_raw.shape[-1]
    quality_grid = quality.reshape(inline_rows, cross_rows, total_time)
    weight = quality_grid * weight_raw.reshape(inline_rows, cross_rows, total_time)
    target = quality_grid * moment_raw.reshape(inline_rows, cross_rows, total_time)
    shift = jnp.zeros_like(target)
    residual = target
    direction = target
    norm_now = squares(residual)
    for iteration in range(ITERS):
        image = operate(direction, weight)
        alpha = norm_now / lax.psum(jnp.sum(direction * image), FILT + IL + ("x",))
        shift = shift + alpha * direction
        residual = residual - alpha * image
        norm_next = squares(residual)
        direction = residual + norm_next / norm_now * direction
        norm_now = norm_next
    out_shape = (1, inline_rows, cross_rows, total_time)
    return (shift.reshape(out_shape), residual.reshape(out_shape))


def exchange(rows, axes, count):
    pieces = lax.all_to_all(rows.reshape(-1, count, 1, LANES), axes, 0, 0, tiled=True)
    return pieces.reshape(rows.shape)


def kernel(body, out_shape, mebibytes, **options):
    return pl.pallas_call(
        body, out_shape=out_shape, compiler_params=limit(mebibytes), name=body.__name__, **options
    )


def per_device(baseline, monitor, band_ids, quality):
    pieces, extra = kernel(
        pack_inputs,
        arrays((N_GROUP, 32, LANES), (24, 512)),
        4,
        in_specs=[HBM] * 4,
        scratch_shapes=[
            pltpu.VMEM((4, 1, 16, LANES), F32),
            pltpu.VMEM((4, 1, 16, LANES), F32),
            pltpu.SMEM((1, 2, KB, 4), jnp.int32),
            pltpu.SemaphoreType.DMA((4,)),
        ],
    )(baseline, monitor, quality, band_ids.transpose(1, 2, 3, 0))
    below = lax.ppermute(extra, GROUP, [(i, i + 1) for i in range(N_GROUP - 1)])
    above = lax.ppermute(extra, GROUP, [(i + 1, i) for i in range(N_GROUP - 1)])
    pieces = lax.all_to_all(pieces, GROUP, 0, 0, tiled=True)
    pieces, target = kernel(
        make_fields,
        [jax.ShapeDtypeStruct((N_PLANE, 16, LANES), jnp.int32)] + arrays((2, 32, LANES)),
        8,
    )(
        pieces, below, extra, above
    )
    pieces = lax.all_to_all(pieces, PLANE, 0, 0, tiled=True)
    (pieces,) = kernel(
        powers,
        arrays((N_PLANE * ROWS, LANES)),
        8,
        scratch_shapes=[
            pltpu.VMEM((2, DEPTH, SUB, LANES), F32),
            pltpu.VMEM((ITERS + 1, 2, DEPTH, SUB, LANES), F32),
        ],
    )(pieces)
    pieces = exchange(pieces, PLANE, ROWS)
    (sums,) = kernel(spread_sums, arrays((N_GROUP, LANES)), 4)(pieces)
    sums = exchange(sums, GROUP, 1)
    shift, residual, again = kernel(
        combine,
        arrays((1, 1, 16, 512), (1, 1, 16, 512)) + [jax.ShapeDtypeStruct((1,), jnp.int32)],
        4,
        out_specs=[VMEM, VMEM, SMEM],
    )(pieces, sums, target)

    def unsettled(state):
        return state[2][0] != 0

    def apart(state):
        return step_by_step(baseline, monitor, band_ids, quality) + (jnp.zeros((1,), jnp.int32),)

    return lax.while_loop(unsettled, apart, (shift, residual, again))[:2]


def solution(mesh):
    fine = Mesh(mesh.devices.reshape(2, 2, 4, 8, 4), ("zh", "core", "zl", "y", "x"))
    outs = P(FILT, IL, "x", None)
    in_specs = (P(None, IL, "x", FILT), P(None, IL, "x", FILT), P(None, IL, "x", None), outs)
    return jax.shard_map(
        per_device, mesh=fine, in_specs=in_specs, out_specs=(outs, outs), check_vma=False
    )
```

```python
import jax
import jax.numpy as jnp
from jax import lax
from jax.experimental import pallas as pl
from jax.experimental.pallas import tpu as pltpu
from jax.sharding import Mesh, PartitionSpec as P

BAND = 8
KB = 2
BXL = 8
HALF = 64
ITERS = 8
LANES = 128
SUB = 8

smooth_space = 4.0
smooth_time = 1.0
CENTRE = 19.0

GROUP = ("zh", "core", "zl")
PLANE = ("y", "x")
N_GROUP = 16
N_PLANE = 32
ROWS = 17
DEPTH = 24
FILT, IL = ("zh", "core"), ("zl", "y")
LAGS = 128
TRUST = 1e-4
HBM = pl.BlockSpec(memory_space=pltpu.HBM)
VMEM = pl.BlockSpec(memory_space=pltpu.VMEM)
SMEM = pl.BlockSpec(memory_space=pltpu.SMEM)
F32 = jnp.float32


def lane_ids():
    return lax.broadcasted_iota(jnp.int32, (SUB, LANES), 1)


def row_ids():
    return lax.broadcasted_iota(jnp.int32, (SUB, LANES), 0)


def roll(value, amount, axis):
    return pltpu.roll(value, amount, axis) if amount else value


def pack_inputs(
    base_hbm, mon_hbm, quality_hbm, bands_hbm, out_ref, extra_ref, base_ref, mon_ref, bands_ref, sems
):
    copies = [
        pltpu.make_async_copy(source, target, sems.at[k])
        for k, (source, target) in enumerate(
            (
                (bands_hbm, bands_ref),
                (base_hbm, base_ref),
                (mon_hbm, mon_ref),
                (quality_hbm.at[0, 0], extra_ref.at[0:16]),
            )
        )
    ]
    for copy in copies:
        copy.start()
    zl = lax.axis_index("zl")
    quarter = lax.axis_index("zh") * 2 + lax.axis_index("core")
    for copy in copies:
        copy.wait()
    for group in range(N_GROUP):
        offset = ((zl - group % 4 + 1) & 3) - 1
        source = jnp.clip(group + offset, 0, N_GROUP - 1) >> 2
        out_ref[group, 0:16, :] = base_ref[source, 0]
        out_ref[group, 16:32, :] = mon_ref[source, 0]
    rows = lax.broadcasted_iota(jnp.int32, (SUB, 512), 0)
    bands = jnp.zeros((SUB, 512), F32)
    for block in range(2):
        for slot in range(KB):
            band = bands_ref[0, block, slot, quarter].astype(F32)
            bands = jnp.where(rows == block * KB + slot, band, bands)
    extra_ref[16:24, :] = bands


def block_terms(base, padded, bands, lane):
    weight = jnp.zeros(base.shape, F32)
    moment = jnp.zeros(base.shape, F32)
    for band in bands:
        like_sum = jnp.zeros(base.shape, F32)
        step_sum = jnp.zeros(base.shape, F32)
        for quad in range(BAND // 4):
            terms = []
            for step in range(quad * 4, quad * 4 + 4):
                start = band * BAND + step
                turned = pltpu.roll(padded, (LANES - start) & (LANES - 1), 1)
                window = jnp.where(lane < LANES - start, turned[0:32], turned[8:40])
                difference = base - window
                misfit = (difference * difference).astype(jnp.bfloat16)
                terms.append(1.0 + misfit.astype(F32))
            a, b, c, d = terms
            left, right = a * b, c * d
            inverse = pl.reciprocal(left * right, approx=False)
            first, second = right * inverse, left * inverse
            low, high = (a + b) * first, (c + d) * second
            like_sum += low + high
            step_sum += a * first + c * second + 2.0 * high
            if quad:
                step_sum += (4.0 * quad) * (low + high)
        lag = (band * BAND - HALF).astype(F32)
        weight += like_sum
        moment += (lag * like_sum + step_sum) * (1.0 / HALF)
    scale = 1.0 / (KB * BAND)
    return weight * scale, moment * scale


def spread(value, lane, zero):
    turned = [roll(value[c * 8 : c * 8 + 8], 8, 1) for c in range(4)]
    sides = [zero] + turned + [zero]
    return [jnp.where(lane < 8, sides[i], sides[i + 1]) for i in range(5)]


def make_fields(recv_ref, below_ref, own_ref, above_ref, out_ref, target_ref):
    zl = lax.axis_index("zl")
    lane32 = lax.broadcasted_iota(jnp.int32, (32, LANES), 1)
    lane = lane_ids()
    zero = jnp.zeros((SUB, LANES), F32)
    for trace, extra_ref in enumerate((below_ref, own_ref, above_ref)):
        slot0 = (zl + trace - 1) & 3
        fields = [None] * 4
        for block in range(2):
            rows = slice(block * 8, block * 8 + 8)
            mon_rows = slice(16 + block * 8, 24 + block * 8)
            base = jnp.concatenate([recv_ref[4 * c + slot0, rows, :] for c in range(4)], axis=0)
            turned = [roll(recv_ref[4 * c + slot0, mon_rows, :], 64, 1) for c in range(4)]
            sides = [zero] + turned + [zero]
            padded = jnp.concatenate(
                [jnp.where(lane < 64, sides[i], sides[i + 1]) for i in range(5)], axis=0
            )
            bands = [
                jnp.max(extra_ref[16 + block * KB + s : 17 + block * KB + s, 0:LANES]).astype(jnp.int32)
                for s in range(KB)
            ]
            weight, moment = block_terms(base, padded, bands, lane32)
            quality = jnp.concatenate(
                [extra_ref[rows, c * LANES : (c + 1) * LANES] for c in range(4)], axis=0
            )
            weight, moment = weight * quality, moment * quality
            if trace == 1:
                target_ref[block] = moment
            fields[block] = spread(weight, lane, zero)
            fields[2 + block] = spread(moment, lane, zero)
        for piece in range(N_PLANE):
            part, offset = piece // 8, 16 * (piece % 8)
            packed = None
            for g, vregs in enumerate(fields):
                shift = (32 * g - offset) % LANES
                value = roll(vregs[part], shift, 1)
                if piece % 8 == 7:
                    value = jnp.where(lane < 32 * g + 16, value, roll(vregs[part + 1], shift, 1))
                packed = value if packed is None else jnp.where(lane < 32 * g, packed, value)
            out_ref[piece, trace * 8 : trace * 8 + 8, :] = packed


def swap_halves(low, high, lane):
    turned = roll(jnp.where(lane < 64, high, low), 64, 1)
    return jnp.where(lane < 64, low, turned), jnp.where(lane < 64, turned, high)


def beside(values, lane, row):
    low, high = values
    next_low, next_high = roll(low, 7, 1), roll(high, 7, 1)
    turn_low, turn_high = roll(next_low, 96, 2), roll(next_high, 96, 2)
    last = row == 7
    up_low = jnp.where(last, jnp.where(lane < 96, turn_low, turn_high), next_low)
    up_high = jnp.where(last, jnp.where(lane < 96, turn_high, 0.0), next_high)
    prev_low, prev_high = roll(low, 1, 1), roll(high, 1, 1)
    turn_low, turn_high = roll(prev_low, 32, 2), roll(prev_high, 32, 2)
    first = row == 0
    down_low = jnp.where(first, jnp.where(lane < 32, 0.0, turn_low), prev_low)
    down_high = jnp.where(first, jnp.where(lane < 32, turn_low, turn_high), prev_high)
    return up_low + down_low, up_high + down_high


CHUNK = 2


def chunks(begin, end):
    out = []
    while begin < end:
        stop = min(end, begin + CHUNK, (begin // 8 + 1) * 8)
        out.append((begin, stop))
        begin = stop
    return out


def powers(recv_ref, out_ref, diag_ref, basis_ref):
    group = lax.axis_index("zh") * 8 + lax.axis_index("core") * 4 + lax.axis_index("zl")
    slab = lax.axis_index("y") * 4 + lax.axis_index("x")
    lane, row = lane_ids(), row_ids()
    tau = lane & 31
    time = slab * 16 - 8 + tau
    inside = ((time >= 0) & (time < 512)).astype(F32)
    shares = [
        inside * (group > 0).astype(F32),
        inside,
        inside * (group < N_GROUP - 1).astype(F32),
    ]
    space = [share * (2.0 * smooth_space / CENTRE) for share in shares]
    along = [share * (2.0 * smooth_time / CENTRE) for share in shares]
    for inline in range(DEPTH):
        rows = slice(inline // 8 * 8, inline // 8 * 8 + 8)
        for v in range(2):
            piece = inline % 8 * 4 + 2 * v
            weight, target = swap_halves(recv_ref[piece, rows, :], recv_ref[piece + 1, rows, :], lane)
            centre = weight + (4.0 * smooth_space + 2.0 * smooth_time - CENTRE)
            diag_ref[v, inline] = centre * (shares[inline // 8] * (2.0 / CENTRE))
            basis_ref[0, v, inline] = target
    own = (tau >= 8) & (tau < 24)
    squares, crosses = [], []
    for level in range(ITERS):
        square = jnp.zeros((SUB, LANES), F32)
        cross = jnp.zeros((SUB, LANES), F32)
        for begin, end in chunks(level + 1, DEPTH - 1 - level):
            region, here = begin // 8, slice(begin, end)
            centre = [basis_ref[level, v, here] for v in range(2)]
            sides = beside(centre, lane[None], row[None])
            for v in range(2):
                inlines = basis_ref[level, v, begin - 1 : end - 1] + basis_ref[level, v, begin + 1 : end + 1]
                times = roll(centre[v], 1, 2) + roll(centre[v], LANES - 1, 2)
                image = (
                    diag_ref[v, here] * centre[v]
                    - space[region] * (inlines + sides[v])
                    - along[region] * times
                )
                image = 0.5 * image if level == 0 else image - basis_ref[level - 1, v, here]
                basis_ref[level + 1, v, here] = image
                if region == 1:
                    square += jnp.sum(centre[v] * centre[v], axis=0)
                    cross += jnp.sum(centre[v] * image, axis=0)
        squares.append(jnp.where(own, square, 0.0))
        crosses.append(jnp.where(own, cross, 0.0))
    tiles = []
    for values in (squares, crosses):
        for amount in (4, 2, 1):
            values = [
                jnp.where(
                    (row & amount) == 0, a + roll(a, 8 - amount, 0), b + roll(b, amount, 0)
                )
                for a, b in zip(values[:amount], values[amount:])
            ]
        tile = values[0]
        for amount in (64, 32, 16, 8):
            tile = tile + roll(tile, amount, 1)
        tiles.append(tile)
    tile = jnp.where(((lane >> 3) & 7) == row, jnp.where(lane < 64, tiles[0], tiles[1]), 0.0)
    for amount in (4, 2, 1):
        tile = tile + roll(tile, amount, 0)
    for y in range(8):
        for v in range(2):
            pairs = []
            for k in range(1, 9, 2):
                pairs.append(
                    jnp.where(
                        tau < 16,
                        roll(basis_ref[k, v, 8 + y], 120, 1),
                        roll(basis_ref[k + 1, v, 8 + y], 8, 1),
                    )
                )
            for part in range(2):
                for half, tile_half in enumerate(swap_halves(*pairs[2 * part : 2 * part + 2], lane)):
                    at = (y * 4 + 2 * v + half) * ROWS + part * 8
                    out_ref[at : at + 8, :] = tile_half
    for piece in range(N_PLANE):
        out_ref[piece * ROWS + 16 : piece * ROWS + 17, :] = tile[0:1]


def spread_sums(recv_ref, out_ref):
    terms = [recv_ref[piece * ROWS + 16 : piece * ROWS + 17, :] for piece in range(N_PLANE)]
    while len(terms) > 1:
        terms = [terms[k] + terms[k + 1] for k in range(0, len(terms), 2)]
    out_ref[...] = jnp.broadcast_to(terms[0], (N_GROUP, LANES))


def two_sum(a, b):
    total = a + b
    part = total - a
    return total, (a - (total - part)) + (b - part)


def split(a):
    scaled = 4097.0 * a
    high = scaled - (scaled - a)
    return high, a - high


def across(tile, k):
    return jnp.broadcast_to(tile[k : k + 1], (SUB, LANES))


def lift(pair, turn):
    return tuple(turn(part) for part in pair)


def choose(mask, first, second):
    return tuple(jnp.where(mask, a, b) for a, b in zip(first, second))


def add_pairs(first, second):
    total, error = two_sum(first[0], second[0])
    return two_sum(total, error + (first[1] + second[1]))


def solve(total, lane, row, turn):
    zero = jnp.zeros((SUB, LANES), F32)
    fold = total
    for amount in (4, 2, 1):
        fold = add_pairs(fold, lift(fold, lambda part: turn(part, amount, 0)))
    for amount in (124, 126, 127):
        fold = add_pairs(fold, lift(fold, lambda part: turn(part, amount, 1)))

    def at_lane(pair, k):
        return lift(pair, lambda part: jnp.broadcast_to(part[:, k : k + 1], (SUB, LANES)))

    start = choose(lane < 64, at_lane(fold, 0), at_lane(fold, 64))
    doubled = add_pairs(lift(fold, lambda part: 2.0 * part), lift(start, lambda part: -part))
    moments = [at_lane(doubled, 64 * (k % 2) + 8 * (k // 2)) for k in range(2 * ITERS)]

    def column(values):
        out = values[0]
        for k in range(1, SUB):
            out = choose(row < k, out, values[k])
        return out

    ahead, beyond, behind = column(moments[:8]), column(moments[8:]), column(moments[8:0:-1])
    gram = []
    for k in range(ITERS + 1):
        later = choose(
            row < 8 - k,
            lift(ahead, lambda part: turn(part, (8 - k) % 8, 0)),
            lift(beyond, lambda part: turn(part, (8 - k) % 8, 0)),
        )
        earlier = choose(
            row < k,
            lift(behind, lambda part: turn(part, k % 8, 0)),
            lift(ahead, lambda part: turn(part, k % 8, 0)),
        )
        gram.append(add_pairs(later, earlier))
    inverse = [gram[k][0] + 0.5 * (gram[k + 1][0] + gram[abs(k - 1)][0]) for k in range(ITERS)]
    for k in range(ITERS):
        reciprocal = 1.0 / across(inverse[k], k)
        pivot = inverse[k]
        for j in range(ITERS):
            if j != k:
                share = across(inverse[j], k) * reciprocal
                inverse[j] = jnp.where(row == k, share, inverse[j] - pivot * share)
        inverse[k] = jnp.where(row == k, reciprocal, -pivot * reciprocal)

    def apply_inverse(right):
        terms = [inverse[k] * across(right, k) for k in range(ITERS)]
        while len(terms) > 1:
            terms = [terms[k] + terms[k + 1] for k in range(0, len(terms), 2)]
        return terms[0]

    def remainder(series):
        def lower(part):
            return jnp.where(row == 0, 0.0, jnp.where(row == 1, 1.0, 0.5) * turn(part, 1, 0))

        def upper(part):
            return jnp.where(row == 7, 0.0, 0.5 * turn(part, 7, 0))

        image = add_pairs(add_pairs(lift(series, lower), lift(series, upper)), series)
        start = (jnp.where(row == 0, 1.0, 0.0), zero)
        return add_pairs(start, lift(image, lambda part: -part)), lift(series, lambda part: -0.5 * across(part, 7))

    parts = [split(pair[0]) for pair in gram]
    series = (apply_inverse(gram[0][0]), zero)
    steps = []
    for _ in range(1):
        body, top = remainder(series)
        high, low = zero, zero
        for k in range(ITERS + 1):
            a, a_low = lift(body, lambda part: across(part, k)) if k < ITERS else top
            b, b_low = gram[k]
            (a0, a1), (b0, b1) = split(a), parts[k]
            product = a * b
            error = (((a0 * b0 - product) + a0 * b1) + a1 * b0) + a1 * b1
            high, rest = two_sum(high, product)
            low = low + (rest + (error + (a * b_low + a_low * b)))
        change = apply_inverse(high + low)
        steps.append(change)
        series = two_sum(series[0], series[1] + change)
    body, top = remainder(series)
    return (series[0] + series[1]) * (1.0 / CENTRE), body[0] + body[1], top[0] + top[1], steps, series[0]


def combine(basis_ref, sums_ref, target_ref, shift_ref, residual_ref, again_ref):
    lane, row = lane_ids(), row_ids()
    zero = jnp.zeros((SUB, LANES), F32)
    total = two_sum(sums_ref[0:8, :], sums_ref[8:16, :])
    shift, residual, last, steps, series = solve(total, lane, row, roll)
    fine = jnp.max(jnp.abs(steps[0])) <= TRUST * jnp.max(jnp.abs(series))
    again_ref[0] = 1 - fine.astype(jnp.int32)
    first = (lane & 31) < 16
    for body, top, out_ref in ((shift, zero, shift_ref), (residual, last, residual_ref)):
        terms = [across(body, k) for k in range(ITERS)] + [top]
        low, high = (
            jnp.where(
                lane < 64,
                jnp.where(first, terms[k], terms[k + 1]),
                jnp.where(first, terms[k + 2], terms[k + 3]),
            )
            for k in (1, 5)
        )
        for part in range(4):
            def piece(step):
                at = (part * 8 + step) * ROWS
                return low * basis_ref[at : at + 8, :] + high * basis_ref[at + 8 : at + 16, :]

            def quad(step):
                halves = []
                for near in (step, step + 1):
                    a, b = piece(near), piece(near + 4)
                    halves.append(jnp.where(lane < 64, a, b) + roll(jnp.where(lane < 64, b, a), 64, 1))
                a, b = halves
                return jnp.where(first, a + roll(a, 112, 1), b + roll(b, 16, 1))

            even, odd = quad(0), quad(2)
            lower = (lane & 32) == 0
            blocks = (
                jnp.where(lower, even, roll(odd, 32, 1)),
                jnp.where(lower, roll(even, 96, 1), odd),
            )
            for h in range(2):
                out_ref[0, 0, h * 8 : h * 8 + 8, part * LANES : (part + 1) * LANES] = (
                    blocks[h] + terms[0] * target_ref[h, part * 8 : part * 8 + 8, :]
                )


def limit(mebibytes):
    return pltpu.CompilerParams(vmem_limit_bytes=mebibytes * 1024 * 1024)


def arrays(*shapes):
    return [jax.ShapeDtypeStruct(shape, F32) for shape in shapes]


def padded_2(value, sides, width):
    for axis, dim in sides:
        size, length = (lax.axis_size(axis), value.shape[dim])
        up = [(i, (i + 1) % size) for i in range(size - 1)]
        down = [(j, i) for i, j in up]
        last = lax.slice_in_dim(value, length - width, length, axis=dim)
        first = lax.slice_in_dim(value, 0, width, axis=dim)
        before = lax.ppermute(last, axis, up)
        after = lax.ppermute(first, axis, down)
        value = jnp.concatenate([before, value, after], axis=dim)
    return value


def slot_window(block, band):
    start = band * BAND
    return lax.dynamic_slice(
        block, (jnp.int32(0), start), (block.shape[0], block.shape[1] - LAGS + BAND)
    )


def lag_table(band_list):
    steps = jnp.arange(BAND, dtype=jnp.float32)
    return (band_list.astype(jnp.float32)[..., None] * BAND + steps - HALF) / HALF


def moments(errors, lags):
    likeness = 1.0 / (1.0 + errors.astype(jnp.float32))
    weight_sum = jnp.sum(likeness, axis=(3, 4)) / (KB * BAND)
    moment_sum = jnp.sum(lags[..., None, None] * likeness, axis=(3, 4)) / (KB * BAND)
    return (weight_sum, moment_sum)


def operate(field, weight):
    padded = padded_2(field, ((FILT + IL, 0), ("x", 1)), 1)
    centre = padded[1:-1, 1:-1, :]
    across = (
        4.0 * centre
        - padded[2:, 1:-1, :]
        - padded[:-2, 1:-1, :]
        - padded[1:-1, 2:, :]
        - padded[1:-1, :-2, :]
    )
    timed = jnp.pad(field, ((0, 0), (0, 0), (1, 1)))
    along = 2.0 * field - timed[:, :, 2:] - timed[:, :, :-2]
    return weight * field + smooth_space * across + smooth_time * along


def squares(residual):
    return lax.psum(jnp.sum(residual * residual), FILT + IL + ("x",))


def step_by_step(baseline, monitor, band_ids, quality):
    quarters, inline_rows, cross_rows, samples = baseline.shape
    cross_blocks = cross_rows // BXL
    extended = padded_2(monitor, ((FILT, 3),), HALF)
    ext_blocks = extended.reshape(quarters, inline_rows, cross_blocks, BXL, samples + LAGS)
    base_blocks = baseline.reshape(quarters, inline_rows, cross_blocks, BXL, samples)
    per_slot = jax.vmap(slot_window, in_axes=(None, 0))
    windows = jax.vmap(jax.vmap(jax.vmap(per_slot)))(ext_blocks, band_ids)
    errors = jnp.stack(
        [
            jnp.square(
                base_blocks[:, :, :, None] - windows[..., lag_step : lag_step + samples]
            ).astype(jnp.bfloat16)
            for lag_step in range(BAND)
        ],
        axis=4,
    )
    local_weight, local_moment = moments(errors, lag_table(band_ids))
    weight_raw, moment_raw = (
        lax.all_to_all(local_weight, FILT, split_axis=0, concat_axis=4, tiled=True),
        lax.all_to_all(local_moment, FILT, split_axis=0, concat_axis=4, tiled=True),
    )
    total_time = weight_raw.shape[-1]
    quality_grid = quality.reshape(inline_rows, cross_rows, total_time)
    weight = quality_grid * weight_raw.reshape(inline_rows, cross_rows, total_time)
    target = quality_grid * moment_raw.reshape(inline_rows, cross_rows, total_time)
    shift = jnp.zeros_like(target)
    residual = target
    direction = target
    norm_now = squares(residual)
    for iteration in range(ITERS):
        image = operate(direction, weight)
        alpha = norm_now / lax.psum(jnp.sum(direction * image), FILT + IL + ("x",))
        shift = shift + alpha * direction
        residual = residual - alpha * image
        norm_next = squares(residual)
        direction = residual + norm_next / norm_now * direction
        norm_now = norm_next
    out_shape = (1, inline_rows, cross_rows, total_time)
    return (shift.reshape(out_shape), residual.reshape(out_shape))


def exchange(rows, axes, count):
    pieces = lax.all_to_all(rows.reshape(-1, count, 1, LANES), axes, 0, 0, tiled=True)
    return pieces.reshape(rows.shape)


def kernel(body, out_shape, mebibytes, **options):
    return pl.pallas_call(
        body, out_shape=out_shape, compiler_params=limit(mebibytes), name=body.__name__, **options
    )


def per_device(baseline, monitor, band_ids, quality):
    pieces, extra = kernel(
        pack_inputs,
        arrays((N_GROUP, 32, LANES), (24, 512)),
        4,
        in_specs=[HBM] * 4,
        scratch_shapes=[
            pltpu.VMEM((4, 1, 16, LANES), F32),
            pltpu.VMEM((4, 1, 16, LANES), F32),
            pltpu.SMEM((1, 2, KB, 4), jnp.int32),
            pltpu.SemaphoreType.DMA((4,)),
        ],
    )(baseline, monitor, quality, band_ids.transpose(1, 2, 3, 0))
    below = lax.ppermute(extra, GROUP, [(i, i + 1) for i in range(N_GROUP - 1)])
    above = lax.ppermute(extra, GROUP, [(i + 1, i) for i in range(N_GROUP - 1)])
    pieces = lax.all_to_all(pieces, GROUP, 0, 0, tiled=True)
    pieces, target = kernel(
        make_fields,
        arrays((N_PLANE, DEPTH, LANES), (2, 32, LANES)),
        8,
    )(
        pieces, below, extra, above
    )
    pieces = lax.all_to_all(pieces, PLANE, 0, 0, tiled=True)
    (pieces,) = kernel(
        powers,
        arrays((N_PLANE * ROWS, LANES)),
        8,
        scratch_shapes=[
            pltpu.VMEM((2, DEPTH, SUB, LANES), F32),
            pltpu.VMEM((ITERS + 1, 2, DEPTH, SUB, LANES), F32),
        ],
    )(pieces)
    pieces = exchange(pieces, PLANE, ROWS)
    (sums,) = kernel(spread_sums, arrays((N_GROUP, LANES)), 4)(pieces)
    sums = exchange(sums, GROUP, 1)
    shift, residual, again = kernel(
        combine,
        arrays((1, 1, 16, 512), (1, 1, 16, 512)) + [jax.ShapeDtypeStruct((1,), jnp.int32)],
        4,
        out_specs=[VMEM, VMEM, SMEM],
    )(pieces, sums, target)

    def unsettled(state):
        return state[2][0] != 0

    def apart(state):
        return step_by_step(baseline, monitor, band_ids, quality) + (jnp.zeros((1,), jnp.int32),)

    return lax.while_loop(unsettled, apart, (shift, residual, again))[:2]


def solution(mesh):
    fine = Mesh(mesh.devices.reshape(2, 2, 4, 8, 4), ("zh", "core", "zl", "y", "x"))
    outs = P(FILT, IL, "x", None)
    in_specs = (P(None, IL, "x", FILT), P(None, IL, "x", FILT), P(None, IL, "x", None), outs)
    return jax.shard_map(
        per_device, mesh=fine, in_specs=in_specs, out_specs=(outs, outs), check_vma=False
    )
```

```python
import jax
import jax.numpy as jnp
from jax import lax
from jax.experimental import pallas as pl
from jax.experimental.pallas import tpu as pltpu
from jax.sharding import Mesh, PartitionSpec as P

BAND = 8
KB = 2
BXL = 8
HALF = 64
ITERS = 8
LANES = 128
SUB = 8

smooth_space = 4.0
smooth_time = 1.0
CENTRE = 19.0

GROUP = ("zh", "core", "zl")
PLANE = ("y", "x")
N_GROUP = 16
N_PLANE = 32
ROWS = 17
STEPS = 2.0**20 - 1.0
DEPTH = 24
FILT, IL = ("zh", "core"), ("zl", "y")
LAGS = 128
TRUST = 5e-5
HBM = pl.BlockSpec(memory_space=pltpu.HBM)
VMEM = pl.BlockSpec(memory_space=pltpu.VMEM)
SMEM = pl.BlockSpec(memory_space=pltpu.SMEM)
F32 = jnp.float32


def lane_ids():
    return lax.broadcasted_iota(jnp.int32, (SUB, LANES), 1)


def row_ids():
    return lax.broadcasted_iota(jnp.int32, (SUB, LANES), 0)


def roll(value, amount, axis):
    return pltpu.roll(value, amount, axis) if amount else value


def pack_inputs(
    base_hbm, mon_hbm, quality_hbm, bands_hbm, out_ref, extra_ref, base_ref, mon_ref, bands_ref, sems
):
    copies = [
        pltpu.make_async_copy(source, target, sems.at[k])
        for k, (source, target) in enumerate(
            (
                (bands_hbm, bands_ref),
                (base_hbm, base_ref),
                (mon_hbm, mon_ref),
                (quality_hbm.at[0, 0], extra_ref.at[0:16]),
            )
        )
    ]
    for copy in copies:
        copy.start()
    zl = lax.axis_index("zl")
    quarter = lax.axis_index("zh") * 2 + lax.axis_index("core")
    for copy in copies:
        copy.wait()
    for group in range(N_GROUP):
        offset = ((zl - group % 4 + 1) & 3) - 1
        source = jnp.clip(group + offset, 0, N_GROUP - 1) >> 2
        out_ref[group, 0:16, :] = base_ref[source, 0]
        out_ref[group, 16:32, :] = mon_ref[source, 0]
    rows = lax.broadcasted_iota(jnp.int32, (SUB, 512), 0)
    bands = jnp.zeros((SUB, 512), F32)
    for block in range(2):
        for slot in range(KB):
            band = bands_ref[0, block, slot, quarter].astype(F32)
            bands = jnp.where(rows == block * KB + slot, band, bands)
    extra_ref[16:24, :] = bands


def block_terms(base, padded, bands, lane):
    weight = jnp.zeros(base.shape, F32)
    moment = jnp.zeros(base.shape, F32)
    for band in bands:
        like_sum = jnp.zeros(base.shape, F32)
        step_sum = jnp.zeros(base.shape, F32)
        for quad in range(BAND // 4):
            terms = []
            for step in range(quad * 4, quad * 4 + 4):
                start = band * BAND + step
                turned = pltpu.roll(padded, (LANES - start) & (LANES - 1), 1)
                window = jnp.where(lane < LANES - start, turned[0:32], turned[8:40])
                difference = base - window
                misfit = (difference * difference).astype(jnp.bfloat16)
                terms.append(1.0 + misfit.astype(F32))
            a, b, c, d = terms
            left, right = a * b, c * d
            inverse = pl.reciprocal(left * right, approx=False)
            first, second = right * inverse, left * inverse
            low, high = (a + b) * first, (c + d) * second
            like_sum += low + high
            step_sum += a * first + c * second + 2.0 * high
            if quad:
                step_sum += (4.0 * quad) * (low + high)
        lag = (band * BAND - HALF).astype(F32)
        weight += like_sum
        moment += (lag * like_sum + step_sum) * (1.0 / HALF)
    scale = 1.0 / (KB * BAND)
    return weight * scale, moment * scale


def spread(value, lane, zero):
    turned = [roll(value[c * 8 : c * 8 + 8], 8, 1) for c in range(4)]
    sides = [zero] + turned + [zero]
    return [jnp.where(lane < 8, sides[i], sides[i + 1]) for i in range(5)]


def words_of(fields):
    weights = [(weight * STEPS + 0.5).astype(jnp.int32) for weight, _ in fields]
    targets = []
    for _, target in fields:
        size = (jnp.sqrt(jnp.abs(target) * 0.5) * STEPS + 0.5).astype(jnp.int32)
        targets.append(jnp.where(target < 0.0, -size, size))
    words = []
    for low, own, high in (weights, targets):
        words += [(low << 11) | ((high >> 10) & 2047), (own << 11) | (high & 1023)]
    return words


def fields_of(words):
    a, b, c, d = words
    weights = [lax.shift_right_logical(part, 11) for part in (a, b)]
    weights.append(((a & 2047) << 10) | (b & 1023))
    targets = [c >> 11, d >> 11]
    targets.append(((((c & 2047) << 10) | (d & 1023)) << 11) >> 11)
    out = []
    for weight, target in zip(weights, targets):
        root = target.astype(F32) * (2.0**0.5 / STEPS)
        out.append((weight.astype(F32) * (1.0 / STEPS), root * jnp.abs(root)))
    return out


def make_fields(recv_ref, below_ref, own_ref, above_ref, out_ref, target_ref):
    zl = lax.axis_index("zl")
    lane32 = lax.broadcasted_iota(jnp.int32, (32, LANES), 1)
    lane = lane_ids()
    zero = jnp.zeros((SUB, LANES), F32)
    empty = jnp.zeros((SUB, LANES), jnp.int32)
    fields = [[], []]
    for trace, extra_ref in enumerate((below_ref, own_ref, above_ref)):
        slot0 = (zl + trace - 1) & 3
        for block in range(2):
            rows = slice(block * 8, block * 8 + 8)
            mon_rows = slice(16 + block * 8, 24 + block * 8)
            base = jnp.concatenate([recv_ref[4 * c + slot0, rows, :] for c in range(4)], axis=0)
            turned = [roll(recv_ref[4 * c + slot0, mon_rows, :], 64, 1) for c in range(4)]
            sides = [zero] + turned + [zero]
            padded = jnp.concatenate(
                [jnp.where(lane < 64, sides[i], sides[i + 1]) for i in range(5)], axis=0
            )
            bands = [
                jnp.max(extra_ref[16 + block * KB + s : 17 + block * KB + s, 0:LANES]).astype(jnp.int32)
                for s in range(KB)
            ]
            weight, moment = block_terms(base, padded, bands, lane32)
            quality = jnp.concatenate(
                [extra_ref[rows, c * LANES : (c + 1) * LANES] for c in range(4)], axis=0
            )
            weight, moment = weight * quality, moment * quality
            if trace == 1:
                target_ref[block] = moment
            fields[block].append((weight, moment))
    words = [[spread(word, lane, empty) for word in words_of(part)] for part in fields]
    for at in range(2):
        groups = [words[h][2 * at + k] for k in range(2) for h in range(2)]
        for piece in range(N_PLANE):
            part, offset = piece // 8, 16 * (piece % 8)
            packed = None
            for g, vregs in enumerate(groups):
                shift = (32 * g - offset) % LANES
                value = roll(vregs[part], shift, 1)
                if piece % 8 == 7:
                    value = jnp.where(lane < 32 * g + 16, value, roll(vregs[part + 1], shift, 1))
                packed = value if packed is None else jnp.where(lane < 32 * g, packed, value)
            out_ref[piece, at * 8 : at * 8 + 8, :] = packed


def swap_halves(low, high, lane):
    turned = roll(jnp.where(lane < 64, high, low), 64, 1)
    return jnp.where(lane < 64, low, turned), jnp.where(lane < 64, turned, high)


def beside(values, lane, row):
    low, high = values
    next_low, next_high = roll(low, 7, 1), roll(high, 7, 1)
    turn_low, turn_high = roll(next_low, 96, 2), roll(next_high, 96, 2)
    last = row == 7
    up_low = jnp.where(last, jnp.where(lane < 96, turn_low, turn_high), next_low)
    up_high = jnp.where(last, jnp.where(lane < 96, turn_high, 0.0), next_high)
    prev_low, prev_high = roll(low, 1, 1), roll(high, 1, 1)
    turn_low, turn_high = roll(prev_low, 32, 2), roll(prev_high, 32, 2)
    first = row == 0
    down_low = jnp.where(first, jnp.where(lane < 32, 0.0, turn_low), prev_low)
    down_high = jnp.where(first, jnp.where(lane < 32, turn_low, turn_high), prev_high)
    return up_low + down_low, up_high + down_high


CHUNK = 2


def chunks(begin, end):
    out = []
    while begin < end:
        stop = min(end, begin + CHUNK, (begin // 8 + 1) * 8)
        out.append((begin, stop))
        begin = stop
    return out


def powers(recv_ref, out_ref, diag_ref, basis_ref):
    group = lax.axis_index("zh") * 8 + lax.axis_index("core") * 4 + lax.axis_index("zl")
    slab = lax.axis_index("y") * 4 + lax.axis_index("x")
    lane, row = lane_ids(), row_ids()
    tau = lane & 31
    time = slab * 16 - 8 + tau
    inside = ((time >= 0) & (time < 512)).astype(F32)
    shares = [
        inside * (group > 0).astype(F32),
        inside,
        inside * (group < N_GROUP - 1).astype(F32),
    ]
    space = [share * (2.0 * smooth_space / CENTRE) for share in shares]
    along = [share * (2.0 * smooth_time / CENTRE) for share in shares]
    for y in range(8):
        for v in range(2):
            piece = y * 4 + 2 * v
            words = []
            for rows in (slice(0, 8), slice(8, 16)):
                words += swap_halves(recv_ref[piece, rows, :], recv_ref[piece + 1, rows, :], lane)
            for trace, (weight, target) in enumerate(fields_of(words)):
                centre = weight + (4.0 * smooth_space + 2.0 * smooth_time - CENTRE)
                diag_ref[v, trace * 8 + y] = centre * (shares[trace] * (2.0 / CENTRE))
                basis_ref[0, v, trace * 8 + y] = target
    own = (tau >= 8) & (tau < 24)
    squares, crosses = [], []
    for level in range(ITERS):
        square = jnp.zeros((SUB, LANES), F32)
        cross = jnp.zeros((SUB, LANES), F32)
        for begin, end in chunks(level + 1, DEPTH - 1 - level):
            region, here = begin // 8, slice(begin, end)
            centre = [basis_ref[level, v, here] for v in range(2)]
            sides = beside(centre, lane[None], row[None])
            for v in range(2):
                inlines = basis_ref[level, v, begin - 1 : end - 1] + basis_ref[level, v, begin + 1 : end + 1]
                times = roll(centre[v], 1, 2) + roll(centre[v], LANES - 1, 2)
                image = (
                    diag_ref[v, here] * centre[v]
                    - space[region] * (inlines + sides[v])
                    - along[region] * times
                )
                image = 0.5 * image if level == 0 else image - basis_ref[level - 1, v, here]
                basis_ref[level + 1, v, here] = image
                if region == 1:
                    square += jnp.sum(centre[v] * centre[v], axis=0)
                    cross += jnp.sum(centre[v] * image, axis=0)
        squares.append(jnp.where(own, square, 0.0))
        crosses.append(jnp.where(own, cross, 0.0))
    tiles = []
    for values in (squares, crosses):
        for amount in (4, 2, 1):
            values = [
                jnp.where(
                    (row & amount) == 0, a + roll(a, 8 - amount, 0), b + roll(b, amount, 0)
                )
                for a, b in zip(values[:amount], values[amount:])
            ]
        tile = values[0]
        for amount in (64, 32, 16, 8):
            tile = tile + roll(tile, amount, 1)
        tiles.append(tile)
    tile = jnp.where(((lane >> 3) & 7) == row, jnp.where(lane < 64, tiles[0], tiles[1]), 0.0)
    for amount in (4, 2, 1):
        tile = tile + roll(tile, amount, 0)
    for y in range(8):
        for v in range(2):
            pairs = []
            for k in range(1, 9, 2):
                pairs.append(
                    jnp.where(
                        tau < 16,
                        roll(basis_ref[k, v, 8 + y], 120, 1),
                        roll(basis_ref[k + 1, v, 8 + y], 8, 1),
                    )
                )
            for part in range(2):
                for half, tile_half in enumerate(swap_halves(*pairs[2 * part : 2 * part + 2], lane)):
                    at = (y * 4 + 2 * v + half) * ROWS + part * 8
                    out_ref[at : at + 8, :] = tile_half
    for piece in range(N_PLANE):
        out_ref[piece * ROWS + 16 : piece * ROWS + 17, :] = tile[0:1]


def spread_sums(recv_ref, out_ref):
    terms = [recv_ref[piece * ROWS + 16 : piece * ROWS + 17, :] for piece in range(N_PLANE)]
    while len(terms) > 1:
        terms = [terms[k] + terms[k + 1] for k in range(0, len(terms), 2)]
    out_ref[...] = jnp.broadcast_to(terms[0], (N_GROUP, LANES))


def two_sum(a, b):
    total = a + b
    part = total - a
    return total, (a - (total - part)) + (b - part)


def split(a):
    scaled = 4097.0 * a
    high = scaled - (scaled - a)
    return high, a - high


def across(tile, k):
    return jnp.broadcast_to(tile[k : k + 1], (SUB, LANES))


def lift(pair, turn):
    return tuple(turn(part) for part in pair)


def choose(mask, first, second):
    return tuple(jnp.where(mask, a, b) for a, b in zip(first, second))


def add_pairs(first, second):
    total, error = two_sum(first[0], second[0])
    return two_sum(total, error + (first[1] + second[1]))


def solve(total, lane, row, turn):
    zero = jnp.zeros((SUB, LANES), F32)
    fold = total
    for amount in (4, 2, 1):
        fold = add_pairs(fold, lift(fold, lambda part: turn(part, amount, 0)))
    for amount in (124, 126, 127):
        fold = add_pairs(fold, lift(fold, lambda part: turn(part, amount, 1)))

    def at_lane(pair, k):
        return lift(pair, lambda part: jnp.broadcast_to(part[:, k : k + 1], (SUB, LANES)))

    start = choose(lane < 64, at_lane(fold, 0), at_lane(fold, 64))
    doubled = add_pairs(lift(fold, lambda part: 2.0 * part), lift(start, lambda part: -part))
    moments = [at_lane(doubled, 64 * (k % 2) + 8 * (k // 2)) for k in range(2 * ITERS)]

    def column(values):
        out = values[0]
        for k in range(1, SUB):
            out = choose(row < k, out, values[k])
        return out

    ahead, beyond, behind = column(moments[:8]), column(moments[8:]), column(moments[8:0:-1])
    gram = []
    for k in range(ITERS + 1):
        later = choose(
            row < 8 - k,
            lift(ahead, lambda part: turn(part, (8 - k) % 8, 0)),
            lift(beyond, lambda part: turn(part, (8 - k) % 8, 0)),
        )
        earlier = choose(
            row < k,
            lift(behind, lambda part: turn(part, k % 8, 0)),
            lift(ahead, lambda part: turn(part, k % 8, 0)),
        )
        gram.append(add_pairs(later, earlier))
    inverse = [gram[k][0] + 0.5 * (gram[k + 1][0] + gram[abs(k - 1)][0]) for k in range(ITERS)]
    for k in range(ITERS):
        reciprocal = 1.0 / across(inverse[k], k)
        pivot = inverse[k]
        for j in range(ITERS):
            if j != k:
                share = across(inverse[j], k) * reciprocal
                inverse[j] = jnp.where(row == k, share, inverse[j] - pivot * share)
        inverse[k] = jnp.where(row == k, reciprocal, -pivot * reciprocal)

    def apply_inverse(right):
        terms = [inverse[k] * across(right, k) for k in range(ITERS)]
        while len(terms) > 1:
            terms = [terms[k] + terms[k + 1] for k in range(0, len(terms), 2)]
        return terms[0]

    def remainder(series):
        def lower(part):
            return jnp.where(row == 0, 0.0, jnp.where(row == 1, 1.0, 0.5) * turn(part, 1, 0))

        def upper(part):
            return jnp.where(row == 7, 0.0, 0.5 * turn(part, 7, 0))

        image = add_pairs(add_pairs(lift(series, lower), lift(series, upper)), series)
        start = (jnp.where(row == 0, 1.0, 0.0), zero)
        return add_pairs(start, lift(image, lambda part: -part)), lift(series, lambda part: -0.5 * across(part, 7))

    parts = [split(pair[0]) for pair in gram]
    series = (apply_inverse(gram[0][0]), zero)
    steps = []
    for _ in range(1):
        body, top = remainder(series)
        high, low = zero, zero
        for k in range(ITERS + 1):
            a, a_low = lift(body, lambda part: across(part, k)) if k < ITERS else top
            b, b_low = gram[k]
            (a0, a1), (b0, b1) = split(a), parts[k]
            product = a * b
            error = (((a0 * b0 - product) + a0 * b1) + a1 * b0) + a1 * b1
            high, rest = two_sum(high, product)
            low = low + (rest + (error + (a * b_low + a_low * b)))
        change = apply_inverse(high + low)
        steps.append(change)
        series = two_sum(series[0], series[1] + change)
    body, top = remainder(series)
    return (series[0] + series[1]) * (1.0 / CENTRE), body[0] + body[1], top[0] + top[1], steps, series[0]


def combine(basis_ref, sums_ref, target_ref, shift_ref, residual_ref, again_ref):
    lane, row = lane_ids(), row_ids()
    zero = jnp.zeros((SUB, LANES), F32)
    total = two_sum(sums_ref[0:8, :], sums_ref[8:16, :])
    shift, residual, last, steps, series = solve(total, lane, row, roll)
    fine = jnp.max(jnp.abs(steps[0])) <= TRUST * jnp.max(jnp.abs(series))
    again_ref[0] = 1 - fine.astype(jnp.int32)
    first = (lane & 31) < 16
    for body, top, out_ref in ((shift, zero, shift_ref), (residual, last, residual_ref)):
        terms = [across(body, k) for k in range(ITERS)] + [top]
        low, high = (
            jnp.where(
                lane < 64,
                jnp.where(first, terms[k], terms[k + 1]),
                jnp.where(first, terms[k + 2], terms[k + 3]),
            )
            for k in (1, 5)
        )
        for part in range(4):
            def piece(step):
                at = (part * 8 + step) * ROWS
                return low * basis_ref[at : at + 8, :] + high * basis_ref[at + 8 : at + 16, :]

            def quad(step):
                halves = []
                for near in (step, step + 1):
                    a, b = piece(near), piece(near + 4)
                    halves.append(jnp.where(lane < 64, a, b) + roll(jnp.where(lane < 64, b, a), 64, 1))
                a, b = halves
                return jnp.where(first, a + roll(a, 112, 1), b + roll(b, 16, 1))

            even, odd = quad(0), quad(2)
            lower = (lane & 32) == 0
            blocks = (
                jnp.where(lower, even, roll(odd, 32, 1)),
                jnp.where(lower, roll(even, 96, 1), odd),
            )
            for h in range(2):
                out_ref[0, 0, h * 8 : h * 8 + 8, part * LANES : (part + 1) * LANES] = (
                    blocks[h] + terms[0] * target_ref[h, part * 8 : part * 8 + 8, :]
                )


def limit(mebibytes):
    return pltpu.CompilerParams(vmem_limit_bytes=mebibytes * 1024 * 1024)


def arrays(*shapes):
    return [jax.ShapeDtypeStruct(shape, F32) for shape in shapes]


def padded_2(value, sides, width):
    for axis, dim in sides:
        size, length = (lax.axis_size(axis), value.shape[dim])
        up = [(i, (i + 1) % size) for i in range(size - 1)]
        down = [(j, i) for i, j in up]
        last = lax.slice_in_dim(value, length - width, length, axis=dim)
        first = lax.slice_in_dim(value, 0, width, axis=dim)
        before = lax.ppermute(last, axis, up)
        after = lax.ppermute(first, axis, down)
        value = jnp.concatenate([before, value, after], axis=dim)
    return value


def slot_window(block, band):
    start = band * BAND
    return lax.dynamic_slice(
        block, (jnp.int32(0), start), (block.shape[0], block.shape[1] - LAGS + BAND)
    )


def lag_table(band_list):
    steps = jnp.arange(BAND, dtype=jnp.float32)
    return (band_list.astype(jnp.float32)[..., None] * BAND + steps - HALF) / HALF


def moments(errors, lags):
    likeness = 1.0 / (1.0 + errors.astype(jnp.float32))
    weight_sum = jnp.sum(likeness, axis=(3, 4)) / (KB * BAND)
    moment_sum = jnp.sum(lags[..., None, None] * likeness, axis=(3, 4)) / (KB * BAND)
    return (weight_sum, moment_sum)


def operate(field, weight):
    padded = padded_2(field, ((FILT + IL, 0), ("x", 1)), 1)
    centre = padded[1:-1, 1:-1, :]
    across = (
        4.0 * centre
        - padded[2:, 1:-1, :]
        - padded[:-2, 1:-1, :]
        - padded[1:-1, 2:, :]
        - padded[1:-1, :-2, :]
    )
    timed = jnp.pad(field, ((0, 0), (0, 0), (1, 1)))
    along = 2.0 * field - timed[:, :, 2:] - timed[:, :, :-2]
    return weight * field + smooth_space * across + smooth_time * along


def squares(residual):
    return lax.psum(jnp.sum(residual * residual), FILT + IL + ("x",))


def step_by_step(baseline, monitor, band_ids, quality):
    quarters, inline_rows, cross_rows, samples = baseline.shape
    cross_blocks = cross_rows // BXL
    extended = padded_2(monitor, ((FILT, 3),), HALF)
    ext_blocks = extended.reshape(quarters, inline_rows, cross_blocks, BXL, samples + LAGS)
    base_blocks = baseline.reshape(quarters, inline_rows, cross_blocks, BXL, samples)
    per_slot = jax.vmap(slot_window, in_axes=(None, 0))
    windows = jax.vmap(jax.vmap(jax.vmap(per_slot)))(ext_blocks, band_ids)
    errors = jnp.stack(
        [
            jnp.square(
                base_blocks[:, :, :, None] - windows[..., lag_step : lag_step + samples]
            ).astype(jnp.bfloat16)
            for lag_step in range(BAND)
        ],
        axis=4,
    )
    local_weight, local_moment = moments(errors, lag_table(band_ids))
    weight_raw, moment_raw = (
        lax.all_to_all(local_weight, FILT, split_axis=0, concat_axis=4, tiled=True),
        lax.all_to_all(local_moment, FILT, split_axis=0, concat_axis=4, tiled=True),
    )
    total_time = weight_raw.shape[-1]
    quality_grid = quality.reshape(inline_rows, cross_rows, total_time)
    weight = quality_grid * weight_raw.reshape(inline_rows, cross_rows, total_time)
    target = quality_grid * moment_raw.reshape(inline_rows, cross_rows, total_time)
    shift = jnp.zeros_like(target)
    residual = target
    direction = target
    norm_now = squares(residual)
    for iteration in range(ITERS):
        image = operate(direction, weight)
        alpha = norm_now / lax.psum(jnp.sum(direction * image), FILT + IL + ("x",))
        shift = shift + alpha * direction
        residual = residual - alpha * image
        norm_next = squares(residual)
        direction = residual + norm_next / norm_now * direction
        norm_now = norm_next
    out_shape = (1, inline_rows, cross_rows, total_time)
    return (shift.reshape(out_shape), residual.reshape(out_shape))


def exchange(rows, axes, count):
    pieces = lax.all_to_all(rows.reshape(-1, count, 1, LANES), axes, 0, 0, tiled=True)
    return pieces.reshape(rows.shape)


def kernel(body, out_shape, mebibytes, **options):
    return pl.pallas_call(
        body, out_shape=out_shape, compiler_params=limit(mebibytes), name=body.__name__, **options
    )


def per_device(baseline, monitor, band_ids, quality):
    pieces, extra = kernel(
        pack_inputs,
        arrays((N_GROUP, 32, LANES), (24, 512)),
        4,
        in_specs=[HBM] * 4,
        scratch_shapes=[
            pltpu.VMEM((4, 1, 16, LANES), F32),
            pltpu.VMEM((4, 1, 16, LANES), F32),
            pltpu.SMEM((1, 2, KB, 4), jnp.int32),
            pltpu.SemaphoreType.DMA((4,)),
        ],
    )(baseline, monitor, quality, band_ids.transpose(1, 2, 3, 0))
    below = lax.ppermute(extra, GROUP, [(i, i + 1) for i in range(N_GROUP - 1)])
    above = lax.ppermute(extra, GROUP, [(i + 1, i) for i in range(N_GROUP - 1)])
    pieces = lax.all_to_all(pieces, GROUP, 0, 0, tiled=True)
    pieces, target = kernel(
        make_fields,
        [jax.ShapeDtypeStruct((N_PLANE, 16, LANES), jnp.int32)] + arrays((2, 32, LANES)),
        8,
    )(
        pieces, below, extra, above
    )
    pieces = lax.all_to_all(pieces, PLANE, 0, 0, tiled=True)
    (pieces,) = kernel(
        powers,
        arrays((N_PLANE * ROWS, LANES)),
        8,
        scratch_shapes=[
            pltpu.VMEM((2, DEPTH, SUB, LANES), F32),
            pltpu.VMEM((ITERS + 1, 2, DEPTH, SUB, LANES), F32),
        ],
    )(pieces)
    pieces = exchange(pieces, PLANE, ROWS)
    (sums,) = kernel(spread_sums, arrays((N_GROUP, LANES)), 4)(pieces)
    sums = exchange(sums, GROUP, 1)
    shift, residual, again = kernel(
        combine,
        arrays((1, 1, 16, 512), (1, 1, 16, 512)) + [jax.ShapeDtypeStruct((1,), jnp.int32)],
        4,
        out_specs=[VMEM, VMEM, SMEM],
    )(pieces, sums, target)

    def unsettled(state):
        return state[2][0] != 0

    def apart(state):
        return step_by_step(baseline, monitor, band_ids, quality) + (jnp.zeros((1,), jnp.int32),)

    return lax.while_loop(unsettled, apart, (shift, residual, again))[:2]


def solution(mesh):
    fine = Mesh(mesh.devices.reshape(2, 2, 4, 8, 4), ("zh", "core", "zl", "y", "x"))
    outs = P(FILT, IL, "x", None)
    in_specs = (P(None, IL, "x", FILT), P(None, IL, "x", FILT), P(None, IL, "x", None), outs)
    return jax.shard_map(
        per_device, mesh=fine, in_specs=in_specs, out_specs=(outs, outs), check_vma=False
    )
```

```python
import jax
import jax.numpy as jnp
from jax import lax
from jax.experimental import pallas as pl
from jax.experimental.pallas import tpu as pltpu
from jax.sharding import Mesh, PartitionSpec as P

BAND = 8
KB = 2
BXL = 8
HALF = 64
ITERS = 8
LANES = 128
SUB = 8

smooth_space = 4.0
smooth_time = 1.0
CENTRE = 19.0

GROUP = ("zh", "core", "zl")
PLANE = ("y", "x")
N_GROUP = 16
N_PLANE = 32
ROWS = 17
STEPS = 2.0**20 - 1.0
DEPTH = 24
FILT, IL = ("zh", "core"), ("zl", "y")
LAGS = 128
TRUST = 5e-5
HBM = pl.BlockSpec(memory_space=pltpu.HBM)
VMEM = pl.BlockSpec(memory_space=pltpu.VMEM)
SMEM = pl.BlockSpec(memory_space=pltpu.SMEM)
F32 = jnp.float32


def lane_ids():
    return lax.broadcasted_iota(jnp.int32, (SUB, LANES), 1)


def row_ids():
    return lax.broadcasted_iota(jnp.int32, (SUB, LANES), 0)


def roll(value, amount, axis):
    return pltpu.roll(value, amount, axis) if amount else value


def pack_inputs(
    base_hbm, mon_hbm, quality_hbm, bands_hbm, out_ref, extra_ref, base_ref, mon_ref, bands_ref, sems
):
    copies = [
        pltpu.make_async_copy(source, target, sems.at[k])
        for k, (source, target) in enumerate(
            (
                (bands_hbm, bands_ref),
                (base_hbm, base_ref),
                (mon_hbm, mon_ref),
                (quality_hbm.at[0, 0], extra_ref.at[0:16]),
            )
        )
    ]
    for copy in copies:
        copy.start()
    zl = lax.axis_index("zl")
    quarter = lax.axis_index("zh") * 2 + lax.axis_index("core")
    for copy in copies:
        copy.wait()
    for group in range(N_GROUP):
        offset = ((zl - group % 4 + 1) & 3) - 1
        source = jnp.clip(group + offset, 0, N_GROUP - 1) >> 2
        out_ref[group, 0:16, :] = base_ref[source, 0]
        out_ref[group, 16:32, :] = mon_ref[source, 0]
    rows = lax.broadcasted_iota(jnp.int32, (SUB, 512), 0)
    bands = jnp.zeros((SUB, 512), F32)
    for block in range(2):
        for slot in range(KB):
            band = bands_ref[0, block, slot, quarter].astype(F32)
            bands = jnp.where(rows == block * KB + slot, band, bands)
    extra_ref[16:24, :] = bands


def block_terms(base, padded, bands, lane):
    weight = jnp.zeros(base.shape, F32)
    moment = jnp.zeros(base.shape, F32)
    for band in bands:
        like_sum = jnp.zeros(base.shape, F32)
        step_sum = jnp.zeros(base.shape, F32)
        for quad in range(BAND // 4):
            terms = []
            for step in range(quad * 4, quad * 4 + 4):
                start = band * BAND + step
                turned = pltpu.roll(padded, (LANES - start) & (LANES - 1), 1)
                window = jnp.where(lane < LANES - start, turned[0:32], turned[8:40])
                difference = base - window
                misfit = (difference * difference).astype(jnp.bfloat16)
                terms.append(1.0 + misfit.astype(F32))
            a, b, c, d = terms
            left, right = a * b, c * d
            inverse = pl.reciprocal(left * right, approx=False)
            first, second = right * inverse, left * inverse
            low, high = (a + b) * first, (c + d) * second
            like_sum += low + high
            step_sum += a * first + c * second + 2.0 * high
            if quad:
                step_sum += (4.0 * quad) * (low + high)
        lag = (band * BAND - HALF).astype(F32)
        weight += like_sum
        moment += (lag * like_sum + step_sum) * (1.0 / HALF)
    scale = 1.0 / (KB * BAND)
    return weight * scale, moment * scale


def spread(value, lane, zero):
    turned = [roll(value[c * 8 : c * 8 + 8], 8, 1) for c in range(4)]
    sides = [zero] + turned + [zero]
    return [jnp.where(lane < 8, sides[i], sides[i + 1]) for i in range(5)]


def words_of(fields):
    weights = [(weight * STEPS + 0.5).astype(jnp.int32) for weight, _ in fields]
    targets = []
    for _, target in fields:
        size = (jnp.sqrt(jnp.abs(target) * 0.5) * STEPS + 0.5).astype(jnp.int32)
        targets.append(jnp.where(target < 0.0, -size, size))
    words = []
    for low, own, high in (weights, targets):
        words += [(low << 11) | ((high >> 10) & 2047), (own << 11) | (high & 1023)]
    return words


def fields_of(words):
    a, b, c, d = words
    weights = [lax.shift_right_logical(part, 11) for part in (a, b)]
    weights.append(((a & 2047) << 10) | (b & 1023))
    targets = [c >> 11, d >> 11]
    targets.append(((((c & 2047) << 10) | (d & 1023)) << 11) >> 11)
    out = []
    for weight, target in zip(weights, targets):
        root = target.astype(F32) * (2.0**0.5 / STEPS)
        out.append((weight.astype(F32) * (1.0 / STEPS), root * jnp.abs(root)))
    return out


def make_fields(recv_ref, below_ref, own_ref, above_ref, out_ref, target_ref):
    zl = lax.axis_index("zl")
    lane32 = lax.broadcasted_iota(jnp.int32, (32, LANES), 1)
    lane = lane_ids()
    zero = jnp.zeros((SUB, LANES), F32)
    empty = jnp.zeros((SUB, LANES), jnp.int32)
    fields = [[], []]
    for trace, extra_ref in enumerate((below_ref, own_ref, above_ref)):
        slot0 = (zl + trace - 1) & 3
        for block in range(2):
            rows = slice(block * 8, block * 8 + 8)
            mon_rows = slice(16 + block * 8, 24 + block * 8)
            base = jnp.concatenate([recv_ref[4 * c + slot0, rows, :] for c in range(4)], axis=0)
            turned = [roll(recv_ref[4 * c + slot0, mon_rows, :], 64, 1) for c in range(4)]
            sides = [zero] + turned + [zero]
            padded = jnp.concatenate(
                [jnp.where(lane < 64, sides[i], sides[i + 1]) for i in range(5)], axis=0
            )
            bands = [
                jnp.max(extra_ref[16 + block * KB + s : 17 + block * KB + s, 0:LANES]).astype(jnp.int32)
                for s in range(KB)
            ]
            weight, moment = block_terms(base, padded, bands, lane32)
            quality = jnp.concatenate(
                [extra_ref[rows, c * LANES : (c + 1) * LANES] for c in range(4)], axis=0
            )
            weight, moment = weight * quality, moment * quality
            if trace == 1:
                target_ref[block] = moment
            fields[block].append((weight, moment))
    words = [[spread(word, lane, empty) for word in words_of(part)] for part in fields]
    for at in range(2):
        groups = [words[h][2 * at + k] for k in range(2) for h in range(2)]
        for piece in range(N_PLANE):
            part, offset = piece // 8, 16 * (piece % 8)
            packed = None
            for g, vregs in enumerate(groups):
                shift = (32 * g - offset) % LANES
                value = roll(vregs[part], shift, 1)
                if piece % 8 == 7:
                    value = jnp.where(lane < 32 * g + 16, value, roll(vregs[part + 1], shift, 1))
                packed = value if packed is None else jnp.where(lane < 32 * g, packed, value)
            out_ref[piece, at * 8 : at * 8 + 8, :] = packed


def swap_halves(low, high, lane):
    turned = roll(jnp.where(lane < 64, high, low), 64, 1)
    return jnp.where(lane < 64, low, turned), jnp.where(lane < 64, turned, high)


def beside(values, lane, row):
    low, high = values
    next_low, next_high = roll(low, 7, 1), roll(high, 7, 1)
    turn_low, turn_high = roll(next_low, 96, 2), roll(next_high, 96, 2)
    last = row == 7
    up_low = jnp.where(last, jnp.where(lane < 96, turn_low, turn_high), next_low)
    up_high = jnp.where(last, jnp.where(lane < 96, turn_high, 0.0), next_high)
    prev_low, prev_high = roll(low, 1, 1), roll(high, 1, 1)
    turn_low, turn_high = roll(prev_low, 32, 2), roll(prev_high, 32, 2)
    first = row == 0
    down_low = jnp.where(first, jnp.where(lane < 32, 0.0, turn_low), prev_low)
    down_high = jnp.where(first, jnp.where(lane < 32, turn_low, turn_high), prev_high)
    return up_low + down_low, up_high + down_high


CHUNK = 2


def chunks(begin, end):
    out = []
    while begin < end:
        stop = min(end, begin + CHUNK, (begin // 8 + 1) * 8)
        out.append((begin, stop))
        begin = stop
    return out


def powers(recv_ref, out_ref, diag_ref, basis_ref):
    group = lax.axis_index("zh") * 8 + lax.axis_index("core") * 4 + lax.axis_index("zl")
    slab = lax.axis_index("y") * 4 + lax.axis_index("x")
    lane, row = lane_ids(), row_ids()
    tau = lane & 31
    time = slab * 16 - 8 + tau
    inside = ((time >= 0) & (time < 512)).astype(F32)
    shares = [
        inside * (group > 0).astype(F32),
        inside,
        inside * (group < N_GROUP - 1).astype(F32),
    ]
    space = [share * (2.0 * smooth_space / CENTRE) for share in shares]
    along = [share * (2.0 * smooth_time / CENTRE) for share in shares]
    for y in range(8):
        for v in range(2):
            piece = y * 4 + 2 * v
            words = []
            for rows in (slice(0, 8), slice(8, 16)):
                words += swap_halves(recv_ref[piece, rows, :], recv_ref[piece + 1, rows, :], lane)
            for trace, (weight, target) in enumerate(fields_of(words)):
                centre = weight + (4.0 * smooth_space + 2.0 * smooth_time - CENTRE)
                diag_ref[v, trace * 8 + y] = centre * (shares[trace] * (2.0 / CENTRE))
                basis_ref[0, v, trace * 8 + y] = target
    own = (tau >= 8) & (tau < 24)
    squares, crosses = [], []
    for level in range(ITERS):
        square = jnp.zeros((SUB, LANES), F32)
        cross = jnp.zeros((SUB, LANES), F32)
        for begin, end in chunks(level + 1, DEPTH - 1 - level):
            region, here = begin // 8, slice(begin, end)
            centre = [basis_ref[level, v, here] for v in range(2)]
            sides = beside(centre, lane[None], row[None])
            for v in range(2):
                inlines = basis_ref[level, v, begin - 1 : end - 1] + basis_ref[level, v, begin + 1 : end + 1]
                times = roll(centre[v], 1, 2) + roll(centre[v], LANES - 1, 2)
                image = (
                    diag_ref[v, here] * centre[v]
                    - space[region] * (inlines + sides[v])
                    - along[region] * times
                )
                image = 0.5 * image if level == 0 else image - basis_ref[level - 1, v, here]
                basis_ref[level + 1, v, here] = image
                if region == 1:
                    square += jnp.sum(centre[v] * centre[v], axis=0)
                    cross += jnp.sum(centre[v] * image, axis=0)
        squares.append(jnp.where(own, square, 0.0))
        crosses.append(jnp.where(own, cross, 0.0))
    tiles = []
    for values in (squares, crosses):
        for amount in (4, 2, 1):
            values = [
                jnp.where(
                    (row & amount) == 0, a + roll(a, 8 - amount, 0), b + roll(b, amount, 0)
                )
                for a, b in zip(values[:amount], values[amount:])
            ]
        tile = values[0]
        for amount in (64, 32, 16, 8):
            tile = tile + roll(tile, amount, 1)
        tiles.append(tile)
    tile = jnp.where(((lane >> 3) & 7) == row, jnp.where(lane < 64, tiles[0], tiles[1]), 0.0)
    for amount in (4, 2, 1):
        tile = tile + roll(tile, amount, 0)
    for y in range(8):
        for v in range(2):
            pairs = []
            for k in range(1, 9, 2):
                pairs.append(
                    jnp.where(own, basis_ref[k, v, 8 + y], roll(basis_ref[k + 1, v, 8 + y], 16, 1))
                )
            for part in range(2):
                for half, tile_half in enumerate(swap_halves(*pairs[2 * part : 2 * part + 2], (lane - 8) & 127)):
                    at = (y * 4 + 2 * v + half) * ROWS + part * 8
                    out_ref[at : at + 8, :] = tile_half
    for piece in range(N_PLANE):
        out_ref[piece * ROWS + 16 : piece * ROWS + 17, :] = tile[0:1]


def spread_sums(recv_ref, out_ref):
    terms = [recv_ref[piece * ROWS + 16 : piece * ROWS + 17, :] for piece in range(N_PLANE)]
    while len(terms) > 1:
        terms = [terms[k] + terms[k + 1] for k in range(0, len(terms), 2)]
    out_ref[...] = jnp.broadcast_to(terms[0], (N_GROUP, LANES))


def two_sum(a, b):
    total = a + b
    part = total - a
    return total, (a - (total - part)) + (b - part)


def split(a):
    scaled = 4097.0 * a
    high = scaled - (scaled - a)
    return high, a - high


def across(tile, k):
    return jnp.broadcast_to(tile[k : k + 1], (SUB, LANES))


def lift(pair, turn):
    return tuple(turn(part) for part in pair)


def choose(mask, first, second):
    return tuple(jnp.where(mask, a, b) for a, b in zip(first, second))


def add_pairs(first, second):
    total, error = two_sum(first[0], second[0])
    return two_sum(total, error + (first[1] + second[1]))


def solve(total, lane, row, turn):
    zero = jnp.zeros((SUB, LANES), F32)
    fold = total
    for amount in (4, 2, 1):
        fold = add_pairs(fold, lift(fold, lambda part: turn(part, amount, 0)))
    for amount in (124, 126, 127):
        fold = add_pairs(fold, lift(fold, lambda part: turn(part, amount, 1)))

    def at_lane(pair, k):
        return lift(pair, lambda part: jnp.broadcast_to(part[:, k : k + 1], (SUB, LANES)))

    start = choose(lane < 64, at_lane(fold, 0), at_lane(fold, 64))
    doubled = add_pairs(lift(fold, lambda part: 2.0 * part), lift(start, lambda part: -part))
    moments = [at_lane(doubled, 64 * (k % 2) + 8 * (k // 2)) for k in range(2 * ITERS)]

    def column(values):
        out = values[0]
        for k in range(1, SUB):
            out = choose(row < k, out, values[k])
        return out

    ahead, beyond, behind = column(moments[:8]), column(moments[8:]), column(moments[8:0:-1])
    gram = []
    for k in range(ITERS + 1):
        later = choose(
            row < 8 - k,
            lift(ahead, lambda part: turn(part, (8 - k) % 8, 0)),
            lift(beyond, lambda part: turn(part, (8 - k) % 8, 0)),
        )
        earlier = choose(
            row < k,
            lift(behind, lambda part: turn(part, k % 8, 0)),
            lift(ahead, lambda part: turn(part, k % 8, 0)),
        )
        gram.append(add_pairs(later, earlier))
    inverse = [gram[k][0] + 0.5 * (gram[k + 1][0] + gram[abs(k - 1)][0]) for k in range(ITERS)]
    for k in range(ITERS):
        reciprocal = 1.0 / across(inverse[k], k)
        pivot = inverse[k]
        for j in range(ITERS):
            if j != k:
                share = across(inverse[j], k) * reciprocal
                inverse[j] = jnp.where(row == k, share, inverse[j] - pivot * share)
        inverse[k] = jnp.where(row == k, reciprocal, -pivot * reciprocal)

    def apply_inverse(right):
        terms = [inverse[k] * across(right, k) for k in range(ITERS)]
        while len(terms) > 1:
            terms = [terms[k] + terms[k + 1] for k in range(0, len(terms), 2)]
        return terms[0]

    def remainder(series):
        def lower(part):
            return jnp.where(row == 0, 0.0, jnp.where(row == 1, 1.0, 0.5) * turn(part, 1, 0))

        def upper(part):
            return jnp.where(row == 7, 0.0, 0.5 * turn(part, 7, 0))

        image = add_pairs(add_pairs(lift(series, lower), lift(series, upper)), series)
        start = (jnp.where(row == 0, 1.0, 0.0), zero)
        return add_pairs(start, lift(image, lambda part: -part)), lift(series, lambda part: -0.5 * across(part, 7))

    parts = [split(pair[0]) for pair in gram]
    series = (apply_inverse(gram[0][0]), zero)
    steps = []
    for _ in range(1):
        body, top = remainder(series)
        high, low = zero, zero
        for k in range(ITERS + 1):
            a, a_low = lift(body, lambda part: across(part, k)) if k < ITERS else top
            b, b_low = gram[k]
            (a0, a1), (b0, b1) = split(a), parts[k]
            product = a * b
            error = (((a0 * b0 - product) + a0 * b1) + a1 * b0) + a1 * b1
            high, rest = two_sum(high, product)
            low = low + (rest + (error + (a * b_low + a_low * b)))
        change = apply_inverse(high + low)
        steps.append(change)
        series = two_sum(series[0], series[1] + change)
    body, top = remainder(series)
    return (series[0] + series[1]) * (1.0 / CENTRE), body[0] + body[1], top[0] + top[1], steps, series[0]


def combine(basis_ref, sums_ref, target_ref, shift_ref, residual_ref, again_ref):
    lane, row = lane_ids(), row_ids()
    zero = jnp.zeros((SUB, LANES), F32)
    total = two_sum(sums_ref[0:8, :], sums_ref[8:16, :])
    shift, residual, last, steps, series = solve(total, lane, row, roll)
    fine = jnp.max(jnp.abs(steps[0])) <= TRUST * jnp.max(jnp.abs(series))
    again_ref[0] = 1 - fine.astype(jnp.int32)
    lane = (lane - 8) & 127
    first = (lane & 31) < 16
    for body, top, out_ref in ((shift, zero, shift_ref), (residual, last, residual_ref)):
        terms = [across(body, k) for k in range(ITERS)] + [top]
        low, high = (
            jnp.where(
                lane < 64,
                jnp.where(first, terms[k], terms[k + 1]),
                jnp.where(first, terms[k + 2], terms[k + 3]),
            )
            for k in (1, 5)
        )
        for part in range(4):
            def piece(step):
                at = (part * 8 + step) * ROWS
                return low * basis_ref[at : at + 8, :] + high * basis_ref[at + 8 : at + 16, :]

            def quad(step):
                halves = []
                for near in (step, step + 1):
                    a, b = piece(near), piece(near + 4)
                    halves.append(jnp.where(lane < 64, a, b) + roll(jnp.where(lane < 64, b, a), 64, 1))
                a, b = halves
                return jnp.where(first, a + roll(a, 112, 1), b + roll(b, 16, 1))

            even, odd = quad(0), quad(2)
            lower = (lane & 32) == 0
            blocks = (
                jnp.where(lower, even, roll(odd, 32, 1)),
                jnp.where(lower, roll(even, 96, 1), odd),
            )
            for h in range(2):
                out_ref[0, 0, h * 8 : h * 8 + 8, part * LANES : (part + 1) * LANES] = (
                    roll(blocks[h], 120, 1) + terms[0] * target_ref[h, part * 8 : part * 8 + 8, :]
                )


def limit(mebibytes):
    return pltpu.CompilerParams(vmem_limit_bytes=mebibytes * 1024 * 1024)


def arrays(*shapes):
    return [jax.ShapeDtypeStruct(shape, F32) for shape in shapes]


def padded_2(value, sides, width):
    for axis, dim in sides:
        size, length = (lax.axis_size(axis), value.shape[dim])
        up = [(i, (i + 1) % size) for i in range(size - 1)]
        down = [(j, i) for i, j in up]
        last = lax.slice_in_dim(value, length - width, length, axis=dim)
        first = lax.slice_in_dim(value, 0, width, axis=dim)
        before = lax.ppermute(last, axis, up)
        after = lax.ppermute(first, axis, down)
        value = jnp.concatenate([before, value, after], axis=dim)
    return value


def slot_window(block, band):
    start = band * BAND
    return lax.dynamic_slice(
        block, (jnp.int32(0), start), (block.shape[0], block.shape[1] - LAGS + BAND)
    )


def lag_table(band_list):
    steps = jnp.arange(BAND, dtype=jnp.float32)
    return (band_list.astype(jnp.float32)[..., None] * BAND + steps - HALF) / HALF


def moments(errors, lags):
    likeness = 1.0 / (1.0 + errors.astype(jnp.float32))
    weight_sum = jnp.sum(likeness, axis=(3, 4)) / (KB * BAND)
    moment_sum = jnp.sum(lags[..., None, None] * likeness, axis=(3, 4)) / (KB * BAND)
    return (weight_sum, moment_sum)


def operate(field, weight):
    padded = padded_2(field, ((FILT + IL, 0), ("x", 1)), 1)
    centre = padded[1:-1, 1:-1, :]
    across = (
        4.0 * centre
        - padded[2:, 1:-1, :]
        - padded[:-2, 1:-1, :]
        - padded[1:-1, 2:, :]
        - padded[1:-1, :-2, :]
    )
    timed = jnp.pad(field, ((0, 0), (0, 0), (1, 1)))
    along = 2.0 * field - timed[:, :, 2:] - timed[:, :, :-2]
    return weight * field + smooth_space * across + smooth_time * along


def squares(residual):
    return lax.psum(jnp.sum(residual * residual), FILT + IL + ("x",))


def step_by_step(baseline, monitor, band_ids, quality):
    quarters, inline_rows, cross_rows, samples = baseline.shape
    cross_blocks = cross_rows // BXL
    extended = padded_2(monitor, ((FILT, 3),), HALF)
    ext_blocks = extended.reshape(quarters, inline_rows, cross_blocks, BXL, samples + LAGS)
    base_blocks = baseline.reshape(quarters, inline_rows, cross_blocks, BXL, samples)
    per_slot = jax.vmap(slot_window, in_axes=(None, 0))
    windows = jax.vmap(jax.vmap(jax.vmap(per_slot)))(ext_blocks, band_ids)
    errors = jnp.stack(
        [
            jnp.square(
                base_blocks[:, :, :, None] - windows[..., lag_step : lag_step + samples]
            ).astype(jnp.bfloat16)
            for lag_step in range(BAND)
        ],
        axis=4,
    )
    local_weight, local_moment = moments(errors, lag_table(band_ids))
    weight_raw, moment_raw = (
        lax.all_to_all(local_weight, FILT, split_axis=0, concat_axis=4, tiled=True),
        lax.all_to_all(local_moment, FILT, split_axis=0, concat_axis=4, tiled=True),
    )
    total_time = weight_raw.shape[-1]
    quality_grid = quality.reshape(inline_rows, cross_rows, total_time)
    weight = quality_grid * weight_raw.reshape(inline_rows, cross_rows, total_time)
    target = quality_grid * moment_raw.reshape(inline_rows, cross_rows, total_time)
    shift = jnp.zeros_like(target)
    residual = target
    direction = target
    norm_now = squares(residual)
    for iteration in range(ITERS):
        image = operate(direction, weight)
        alpha = norm_now / lax.psum(jnp.sum(direction * image), FILT + IL + ("x",))
        shift = shift + alpha * direction
        residual = residual - alpha * image
        norm_next = squares(residual)
        direction = residual + norm_next / norm_now * direction
        norm_now = norm_next
    out_shape = (1, inline_rows, cross_rows, total_time)
    return (shift.reshape(out_shape), residual.reshape(out_shape))


def exchange(rows, axes, count):
    pieces = lax.all_to_all(rows.reshape(-1, count, 1, LANES), axes, 0, 0, tiled=True)
    return pieces.reshape(rows.shape)


def kernel(body, out_shape, mebibytes, **options):
    return pl.pallas_call(
        body, out_shape=out_shape, compiler_params=limit(mebibytes), name=body.__name__, **options
    )


def per_device(baseline, monitor, band_ids, quality):
    pieces, extra = kernel(
        pack_inputs,
        arrays((N_GROUP, 32, LANES), (24, 512)),
        4,
        in_specs=[HBM] * 4,
        scratch_shapes=[
            pltpu.VMEM((4, 1, 16, LANES), F32),
            pltpu.VMEM((4, 1, 16, LANES), F32),
            pltpu.SMEM((1, 2, KB, 4), jnp.int32),
            pltpu.SemaphoreType.DMA((4,)),
        ],
    )(baseline, monitor, quality, band_ids.transpose(1, 2, 3, 0))
    below = lax.ppermute(extra, GROUP, [(i, i + 1) for i in range(N_GROUP - 1)])
    above = lax.ppermute(extra, GROUP, [(i + 1, i) for i in range(N_GROUP - 1)])
    pieces = lax.all_to_all(pieces, GROUP, 0, 0, tiled=True)
    pieces, target = kernel(
        make_fields,
        [jax.ShapeDtypeStruct((N_PLANE, 16, LANES), jnp.int32)] + arrays((2, 32, LANES)),
        8,
    )(
        pieces, below, extra, above
    )
    pieces = lax.all_to_all(pieces, PLANE, 0, 0, tiled=True)
    (pieces,) = kernel(
        powers,
        arrays((N_PLANE * ROWS, LANES)),
        8,
        scratch_shapes=[
            pltpu.VMEM((2, DEPTH, SUB, LANES), F32),
            pltpu.VMEM((ITERS + 1, 2, DEPTH, SUB, LANES), F32),
        ],
    )(pieces)
    pieces = exchange(pieces, PLANE, ROWS)
    (sums,) = kernel(spread_sums, arrays((N_GROUP, LANES)), 4)(pieces)
    sums = exchange(sums, GROUP, 1)
    shift, residual, again = kernel(
        combine,
        arrays((1, 1, 16, 512), (1, 1, 16, 512)) + [jax.ShapeDtypeStruct((1,), jnp.int32)],
        4,
        out_specs=[VMEM, VMEM, SMEM],
    )(pieces, sums, target)

    def unsettled(state):
        return state[2][0] != 0

    def apart(state):
        return step_by_step(baseline, monitor, band_ids, quality) + (jnp.zeros((1,), jnp.int32),)

    return lax.while_loop(unsettled, apart, (shift, residual, again))[:2]


def solution(mesh):
    fine = Mesh(mesh.devices.reshape(2, 2, 4, 8, 4), ("zh", "core", "zl", "y", "x"))
    outs = P(FILT, IL, "x", None)
    in_specs = (P(None, IL, "x", FILT), P(None, IL, "x", FILT), P(None, IL, "x", None), outs)
    return jax.shard_map(
        per_device, mesh=fine, in_specs=in_specs, out_specs=(outs, outs), check_vma=False
    )
```

```python
import jax
import jax.numpy as jnp
from jax import lax
from jax.experimental import pallas as pl
from jax.experimental.pallas import tpu as pltpu
from jax.sharding import Mesh, PartitionSpec as P

BAND = 8
KB = 2
BXL = 8
HALF = 64
ITERS = 8
LANES = 128
SUB = 8

smooth_space = 4.0
smooth_time = 1.0
CENTRE = 19.0

GROUP = ("zh", "core", "zl")
PLANE = ("y", "x")
N_GROUP = 16
N_PLANE = 32
ROWS = 17
STEPS = 2.0**20 - 1.0
DEPTH = 24
FILT, IL = ("zh", "core"), ("zl", "y")
LAGS = 128
TRUST = 5e-5
HBM = pl.BlockSpec(memory_space=pltpu.HBM)
VMEM = pl.BlockSpec(memory_space=pltpu.VMEM)
SMEM = pl.BlockSpec(memory_space=pltpu.SMEM)
F32 = jnp.float32


def lane_ids():
    return lax.broadcasted_iota(jnp.int32, (SUB, LANES), 1)


def row_ids():
    return lax.broadcasted_iota(jnp.int32, (SUB, LANES), 0)


def roll(value, amount, axis):
    return pltpu.roll(value, amount, axis) if amount else value


def pack_inputs(
    base_hbm, mon_hbm, quality_hbm, bands_hbm, out_ref, extra_ref, base_ref, mon_ref, bands_ref, sems
):
    copies = [
        pltpu.make_async_copy(source, target, sems.at[k])
        for k, (source, target) in enumerate(
            (
                (bands_hbm, bands_ref),
                (base_hbm, base_ref),
                (mon_hbm, mon_ref),
                (quality_hbm.at[0, 0], extra_ref.at[0:16]),
            )
        )
    ]
    for copy in copies:
        copy.start()
    zl = lax.axis_index("zl")
    quarter = lax.axis_index("zh") * 2 + lax.axis_index("core")
    for copy in copies:
        copy.wait()
    for group in range(N_GROUP):
        offset = ((zl - group % 4 + 1) & 3) - 1
        source = jnp.clip(group + offset, 0, N_GROUP - 1) >> 2
        out_ref[group, 0:16, :] = base_ref[source, 0]
        out_ref[group, 16:32, :] = mon_ref[source, 0]
    rows = lax.broadcasted_iota(jnp.int32, (SUB, 512), 0)
    bands = jnp.zeros((SUB, 512), F32)
    for block in range(2):
        for slot in range(KB):
            band = bands_ref[0, block, slot, quarter].astype(F32)
            bands = jnp.where(rows == block * KB + slot, band, bands)
    extra_ref[16:24, :] = bands


def block_terms(base, padded, bands, lane):
    weight = jnp.zeros(base.shape, F32)
    moment = jnp.zeros(base.shape, F32)
    for band in bands:
        like_sum = jnp.zeros(base.shape, F32)
        step_sum = jnp.zeros(base.shape, F32)
        for quad in range(BAND // 4):
            terms = []
            for step in range(quad * 4, quad * 4 + 4):
                start = band * BAND + step
                turned = pltpu.roll(padded, (LANES - start) & (LANES - 1), 1)
                window = jnp.where(lane < LANES - start, turned[0:32], turned[8:40])
                difference = base - window
                misfit = (difference * difference).astype(jnp.bfloat16)
                terms.append(1.0 + misfit.astype(F32))
            a, b, c, d = terms
            left, right = a * b, c * d
            inverse = pl.reciprocal(left * right, approx=False)
            first, second = right * inverse, left * inverse
            low, high = (a + b) * first, (c + d) * second
            like_sum += low + high
            step_sum += a * first + c * second + 2.0 * high
            if quad:
                step_sum += (4.0 * quad) * (low + high)
        lag = (band * BAND - HALF).astype(F32)
        weight += like_sum
        moment += (lag * like_sum + step_sum) * (1.0 / HALF)
    scale = 1.0 / (KB * BAND)
    return weight * scale, moment * scale


def spread(value, lane, zero):
    turned = [roll(value[c * 8 : c * 8 + 8], 8, 1) for c in range(4)]
    sides = [zero] + turned + [zero]
    return [jnp.where(lane < 8, sides[i], sides[i + 1]) for i in range(5)]


def words_of(fields):
    weights = [(weight * STEPS + 0.5).astype(jnp.int32) for weight, _ in fields]
    targets = []
    for _, target in fields:
        size = (jnp.sqrt(jnp.abs(target) * 0.5) * STEPS + 0.5).astype(jnp.int32)
        targets.append(jnp.where(target < 0.0, -size, size))
    words = []
    for low, own, high in (weights, targets):
        words += [(low << 11) | ((high >> 10) & 2047), (own << 11) | (high & 1023)]
    return words


def fields_of(words):
    a, b, c, d = words
    weights = [lax.shift_right_logical(part, 11) for part in (a, b)]
    weights.append(((a & 2047) << 10) | (b & 1023))
    targets = [c >> 11, d >> 11]
    targets.append(((((c & 2047) << 10) | (d & 1023)) << 11) >> 11)
    out = []
    for weight, target in zip(weights, targets):
        root = target.astype(F32) * (2.0**0.5 / STEPS)
        out.append((weight.astype(F32) * (1.0 / STEPS), root * jnp.abs(root)))
    return out


def make_fields(recv_ref, below_ref, own_ref, above_ref, out_ref, target_ref):
    zl = lax.axis_index("zl")
    lane32 = lax.broadcasted_iota(jnp.int32, (32, LANES), 1)
    lane = lane_ids()
    zero = jnp.zeros((SUB, LANES), F32)
    empty = jnp.zeros((SUB, LANES), jnp.int32)
    fields = [[], []]
    for trace, extra_ref in enumerate((below_ref, own_ref, above_ref)):
        slot0 = (zl + trace - 1) & 3
        for block in range(2):
            rows = slice(block * 8, block * 8 + 8)
            mon_rows = slice(16 + block * 8, 24 + block * 8)
            base = jnp.concatenate([recv_ref[4 * c + slot0, rows, :] for c in range(4)], axis=0)
            turned = [roll(recv_ref[4 * c + slot0, mon_rows, :], 64, 1) for c in range(4)]
            sides = [zero] + turned + [zero]
            padded = jnp.concatenate(
                [jnp.where(lane < 64, sides[i], sides[i + 1]) for i in range(5)], axis=0
            )
            bands = [
                jnp.max(extra_ref[16 + block * KB + s : 17 + block * KB + s, 0:LANES]).astype(jnp.int32)
                for s in range(KB)
            ]
            weight, moment = block_terms(base, padded, bands, lane32)
            quality = jnp.concatenate(
                [extra_ref[rows, c * LANES : (c + 1) * LANES] for c in range(4)], axis=0
            )
            weight, moment = weight * quality, moment * quality
            if trace == 1:
                target_ref[block] = moment
            fields[block].append((weight, moment))
    words = [[spread(word, lane, empty) for word in words_of(part)] for part in fields]
    for at in range(2):
        groups = [words[h][2 * at + k] for k in range(2) for h in range(2)]
        for piece in range(N_PLANE):
            part, offset = piece // 8, 16 * (piece % 8)
            packed = None
            for g, vregs in enumerate(groups):
                shift = (32 * g - offset) % LANES
                value = roll(vregs[part], shift, 1)
                if piece % 8 == 7:
                    value = jnp.where(lane < 32 * g + 16, value, roll(vregs[part + 1], shift, 1))
                packed = value if packed is None else jnp.where(lane < 32 * g, packed, value)
            out_ref[piece, at * 8 : at * 8 + 8, :] = packed


def swap_halves(low, high, lane):
    turned = roll(jnp.where(lane < 64, high, low), 64, 1)
    return jnp.where(lane < 64, low, turned), jnp.where(lane < 64, turned, high)


def beside(values, lane, row):
    low, high = values
    next_low, next_high = roll(low, 7, 1), roll(high, 7, 1)
    turn_low, turn_high = roll(next_low, 96, 2), roll(next_high, 96, 2)
    last = row == 7
    up_low = jnp.where(last, jnp.where(lane < 96, turn_low, turn_high), next_low)
    up_high = jnp.where(last, jnp.where(lane < 96, turn_high, 0.0), next_high)
    prev_low, prev_high = roll(low, 1, 1), roll(high, 1, 1)
    turn_low, turn_high = roll(prev_low, 32, 2), roll(prev_high, 32, 2)
    first = row == 0
    down_low = jnp.where(first, jnp.where(lane < 32, 0.0, turn_low), prev_low)
    down_high = jnp.where(first, jnp.where(lane < 32, turn_low, turn_high), prev_high)
    return up_low + down_low, up_high + down_high


CHUNK = 2


def chunks(begin, end):
    out = []
    while begin < end:
        stop = min(end, begin + CHUNK, (begin // 8 + 1) * 8)
        out.append((begin, stop))
        begin = stop
    return out


def powers(recv_ref, out_ref, diag_ref, basis_ref):
    group = lax.axis_index("zh") * 8 + lax.axis_index("core") * 4 + lax.axis_index("zl")
    slab = lax.axis_index("y") * 4 + lax.axis_index("x")
    lane, row = lane_ids(), row_ids()
    tau = lane & 31
    time = slab * 16 - 8 + tau
    inside = ((time >= 0) & (time < 512)).astype(F32)
    shares = [
        inside * (group > 0).astype(F32),
        inside,
        inside * (group < N_GROUP - 1).astype(F32),
    ]
    space = [share * (2.0 * smooth_space / CENTRE) for share in shares]
    along = [share * (2.0 * smooth_time / CENTRE) for share in shares]
    for y in range(8):
        for v in range(2):
            piece = y * 4 + 2 * v
            words = []
            for rows in (slice(0, 8), slice(8, 16)):
                words += swap_halves(recv_ref[piece, rows, :], recv_ref[piece + 1, rows, :], lane)
            for trace, (weight, target) in enumerate(fields_of(words)):
                centre = weight + (4.0 * smooth_space + 2.0 * smooth_time - CENTRE)
                diag_ref[v, trace * 8 + y] = centre * (shares[trace] * (2.0 / CENTRE))
                basis_ref[0, v, trace * 8 + y] = target
    own = (tau >= 8) & (tau < 24)
    squares, crosses = [], []
    for level in range(ITERS):
        square = jnp.zeros((SUB, LANES), F32)
        cross = jnp.zeros((SUB, LANES), F32)
        for begin, end in chunks(level + 1, DEPTH - 1 - level):
            region, here = begin // 8, slice(begin, end)
            centre = [basis_ref[level, v, here] for v in range(2)]
            sides = beside(centre, lane[None], row[None])
            for v in range(2):
                inlines = basis_ref[level, v, begin - 1 : end - 1] + basis_ref[level, v, begin + 1 : end + 1]
                times = roll(centre[v], 1, 2) + roll(centre[v], LANES - 1, 2)
                image = (
                    diag_ref[v, here] * centre[v]
                    - space[region] * (inlines + sides[v])
                    - along[region] * times
                )
                image = 0.5 * image if level == 0 else image - basis_ref[level - 1, v, here]
                basis_ref[level + 1, v, here] = image
                if region == 1:
                    square += jnp.sum(centre[v] * centre[v], axis=0)
                    cross += jnp.sum(centre[v] * image, axis=0)
        squares.append(jnp.where(own, square, 0.0))
        crosses.append(jnp.where(own, cross, 0.0))
    tiles = []
    for values in (squares, crosses):
        for amount in (4, 2, 1):
            values = [
                jnp.where(
                    (row & amount) == 0, a + roll(a, 8 - amount, 0), b + roll(b, amount, 0)
                )
                for a, b in zip(values[:amount], values[amount:])
            ]
        tile = values[0]
        for amount in (64, 32, 16, 8):
            tile = tile + roll(tile, amount, 1)
        tiles.append(tile)
    tile = jnp.where(((lane >> 3) & 7) == row, jnp.where(lane < 64, tiles[0], tiles[1]), 0.0)
    for amount in (4, 2, 1):
        tile = tile + roll(tile, amount, 0)
    for y in range(8):
        for v in range(2):
            pairs = []
            for k in range(1, 9, 2):
                pairs.append(
                    jnp.where(own, basis_ref[k, v, 8 + y], roll(basis_ref[k + 1, v, 8 + y], 16, 1))
                )
            for part in range(2):
                for half, tile_half in enumerate(swap_halves(*pairs[2 * part : 2 * part + 2], (lane - 8) & 127)):
                    at = (y * 4 + 2 * v + half) * ROWS + part * 8
                    out_ref[at : at + 8, :] = tile_half
    for piece in range(N_PLANE):
        out_ref[piece * ROWS + 16 : piece * ROWS + 17, :] = tile[0:1]


def spread_sums(recv_ref, out_ref):
    terms = [recv_ref[piece * ROWS + 16 : piece * ROWS + 17, :] for piece in range(N_PLANE)]
    while len(terms) > 1:
        terms = [terms[k] + terms[k + 1] for k in range(0, len(terms), 2)]
    out_ref[...] = jnp.broadcast_to(terms[0], (N_GROUP, LANES))


def two_sum(a, b):
    total = a + b
    part = total - a
    return total, (a - (total - part)) + (b - part)


def split(a):
    scaled = 4097.0 * a
    high = scaled - (scaled - a)
    return high, a - high


def across(tile, k):
    return jnp.broadcast_to(tile[k : k + 1], (SUB, LANES))


def lift(pair, turn):
    return tuple(turn(part) for part in pair)


def choose(mask, first, second):
    return tuple(jnp.where(mask, a, b) for a, b in zip(first, second))


def add_pairs(first, second):
    total, error = two_sum(first[0], second[0])
    return two_sum(total, error + (first[1] + second[1]))


def solve(total, lane, row, turn):
    zero = jnp.zeros((SUB, LANES), F32)
    fold = total
    for amount in (4, 2, 1):
        fold = add_pairs(fold, lift(fold, lambda part: turn(part, amount, 0)))
    for amount in (124, 126, 127):
        fold = add_pairs(fold, lift(fold, lambda part: turn(part, amount, 1)))

    def at_lane(pair, k):
        return lift(pair, lambda part: jnp.broadcast_to(part[:, k : k + 1], (SUB, LANES)))

    start = choose(lane < 64, at_lane(fold, 0), at_lane(fold, 64))
    doubled = add_pairs(lift(fold, lambda part: 2.0 * part), lift(start, lambda part: -part))
    moments = [at_lane(doubled, 64 * (k % 2) + 8 * (k // 2)) for k in range(2 * ITERS)]

    def column(values):
        out = values[0]
        for k in range(1, SUB):
            out = choose(row < k, out, values[k])
        return out

    ahead, beyond, behind = column(moments[:8]), column(moments[8:]), column(moments[8:0:-1])
    gram = []
    for k in range(ITERS + 1):
        later = choose(
            row < 8 - k,
            lift(ahead, lambda part: turn(part, (8 - k) % 8, 0)),
            lift(beyond, lambda part: turn(part, (8 - k) % 8, 0)),
        )
        earlier = choose(
            row < k,
            lift(behind, lambda part: turn(part, k % 8, 0)),
            lift(ahead, lambda part: turn(part, k % 8, 0)),
        )
        gram.append(add_pairs(later, earlier))
    inverse = [gram[k][0] + 0.5 * (gram[k + 1][0] + gram[abs(k - 1)][0]) for k in range(ITERS)]
    for k in range(ITERS):
        reciprocal = pl.reciprocal(across(inverse[k], k), approx=False)
        pivot = inverse[k]
        for j in range(ITERS):
            if j != k:
                share = across(inverse[j], k) * reciprocal
                inverse[j] = jnp.where(row == k, share, inverse[j] - pivot * share)
        inverse[k] = jnp.where(row == k, reciprocal, -pivot * reciprocal)

    def apply_inverse(right):
        terms = [inverse[k] * across(right, k) for k in range(ITERS)]
        while len(terms) > 1:
            terms = [terms[k] + terms[k + 1] for k in range(0, len(terms), 2)]
        return terms[0]

    def remainder(series):
        def lower(part):
            return jnp.where(row == 0, 0.0, jnp.where(row == 1, 1.0, 0.5) * turn(part, 1, 0))

        def upper(part):
            return jnp.where(row == 7, 0.0, 0.5 * turn(part, 7, 0))

        image = add_pairs(add_pairs(lift(series, lower), lift(series, upper)), series)
        start = (jnp.where(row == 0, 1.0, 0.0), zero)
        return add_pairs(start, lift(image, lambda part: -part)), lift(series, lambda part: -0.5 * across(part, 7))

    parts = [split(pair[0]) for pair in gram]
    series = (apply_inverse(gram[0][0]), zero)
    steps = []
    for _ in range(1):
        body, top = remainder(series)
        high, low = zero, zero
        for k in range(ITERS + 1):
            a, a_low = lift(body, lambda part: across(part, k)) if k < ITERS else top
            b, b_low = gram[k]
            (a0, a1), (b0, b1) = split(a), parts[k]
            product = a * b
            error = (((a0 * b0 - product) + a0 * b1) + a1 * b0) + a1 * b1
            high, rest = two_sum(high, product)
            low = low + (rest + (error + (a * b_low + a_low * b)))
        change = apply_inverse(high + low)
        steps.append(change)
        series = two_sum(series[0], series[1] + change)
    body, top = remainder(series)
    return (series[0] + series[1]) * (1.0 / CENTRE), body[0] + body[1], top[0] + top[1], steps, series[0]


def combine(basis_ref, sums_ref, target_ref, shift_ref, residual_ref, again_ref):
    lane, row = lane_ids(), row_ids()
    zero = jnp.zeros((SUB, LANES), F32)
    total = two_sum(sums_ref[0:8, :], sums_ref[8:16, :])
    shift, residual, last, steps, series = solve(total, lane, row, roll)
    fine = jnp.max(jnp.abs(steps[0])) <= TRUST * jnp.max(jnp.abs(series))
    again_ref[0] = 1 - fine.astype(jnp.int32)
    lane = (lane - 8) & 127
    first = (lane & 31) < 16
    for body, top, out_ref in ((shift, zero, shift_ref), (residual, last, residual_ref)):
        terms = [across(body, k) for k in range(ITERS)] + [top]
        low, high = (
            jnp.where(
                lane < 64,
                jnp.where(first, terms[k], terms[k + 1]),
                jnp.where(first, terms[k + 2], terms[k + 3]),
            )
            for k in (1, 5)
        )
        for part in range(4):
            def piece(step):
                at = (part * 8 + step) * ROWS
                return low * basis_ref[at : at + 8, :] + high * basis_ref[at + 8 : at + 16, :]

            def quad(step):
                halves = []
                for near in (step, step + 1):
                    a, b = piece(near), piece(near + 4)
                    halves.append(jnp.where(lane < 64, a, b) + roll(jnp.where(lane < 64, b, a), 64, 1))
                a, b = halves
                return jnp.where(first, a + roll(a, 112, 1), b + roll(b, 16, 1))

            even, odd = quad(0), quad(2)
            lower = (lane & 32) == 0
            blocks = (
                jnp.where(lower, even, roll(odd, 32, 1)),
                jnp.where(lower, roll(even, 96, 1), odd),
            )
            for h in range(2):
                out_ref[0, 0, h * 8 : h * 8 + 8, part * LANES : (part + 1) * LANES] = (
                    roll(blocks[h], 120, 1) + terms[0] * target_ref[h, part * 8 : part * 8 + 8, :]
                )


def limit(mebibytes):
    return pltpu.CompilerParams(vmem_limit_bytes=mebibytes * 1024 * 1024)


def arrays(*shapes):
    return [jax.ShapeDtypeStruct(shape, F32) for shape in shapes]


def padded_2(value, sides, width):
    for axis, dim in sides:
        size, length = (lax.axis_size(axis), value.shape[dim])
        up = [(i, (i + 1) % size) for i in range(size - 1)]
        down = [(j, i) for i, j in up]
        last = lax.slice_in_dim(value, length - width, length, axis=dim)
        first = lax.slice_in_dim(value, 0, width, axis=dim)
        before = lax.ppermute(last, axis, up)
        after = lax.ppermute(first, axis, down)
        value = jnp.concatenate([before, value, after], axis=dim)
    return value


def slot_window(block, band):
    start = band * BAND
    return lax.dynamic_slice(
        block, (jnp.int32(0), start), (block.shape[0], block.shape[1] - LAGS + BAND)
    )


def lag_table(band_list):
    steps = jnp.arange(BAND, dtype=jnp.float32)
    return (band_list.astype(jnp.float32)[..., None] * BAND + steps - HALF) / HALF


def moments(errors, lags):
    likeness = 1.0 / (1.0 + errors.astype(jnp.float32))
    weight_sum = jnp.sum(likeness, axis=(3, 4)) / (KB * BAND)
    moment_sum = jnp.sum(lags[..., None, None] * likeness, axis=(3, 4)) / (KB * BAND)
    return (weight_sum, moment_sum)


def operate(field, weight):
    padded = padded_2(field, ((FILT + IL, 0), ("x", 1)), 1)
    centre = padded[1:-1, 1:-1, :]
    across = (
        4.0 * centre
        - padded[2:, 1:-1, :]
        - padded[:-2, 1:-1, :]
        - padded[1:-1, 2:, :]
        - padded[1:-1, :-2, :]
    )
    timed = jnp.pad(field, ((0, 0), (0, 0), (1, 1)))
    along = 2.0 * field - timed[:, :, 2:] - timed[:, :, :-2]
    return weight * field + smooth_space * across + smooth_time * along


def squares(residual):
    return lax.psum(jnp.sum(residual * residual), FILT + IL + ("x",))


def step_by_step(baseline, monitor, band_ids, quality):
    quarters, inline_rows, cross_rows, samples = baseline.shape
    cross_blocks = cross_rows // BXL
    extended = padded_2(monitor, ((FILT, 3),), HALF)
    ext_blocks = extended.reshape(quarters, inline_rows, cross_blocks, BXL, samples + LAGS)
    base_blocks = baseline.reshape(quarters, inline_rows, cross_blocks, BXL, samples)
    per_slot = jax.vmap(slot_window, in_axes=(None, 0))
    windows = jax.vmap(jax.vmap(jax.vmap(per_slot)))(ext_blocks, band_ids)
    errors = jnp.stack(
        [
            jnp.square(
                base_blocks[:, :, :, None] - windows[..., lag_step : lag_step + samples]
            ).astype(jnp.bfloat16)
            for lag_step in range(BAND)
        ],
        axis=4,
    )
    local_weight, local_moment = moments(errors, lag_table(band_ids))
    weight_raw, moment_raw = (
        lax.all_to_all(local_weight, FILT, split_axis=0, concat_axis=4, tiled=True),
        lax.all_to_all(local_moment, FILT, split_axis=0, concat_axis=4, tiled=True),
    )
    total_time = weight_raw.shape[-1]
    quality_grid = quality.reshape(inline_rows, cross_rows, total_time)
    weight = quality_grid * weight_raw.reshape(inline_rows, cross_rows, total_time)
    target = quality_grid * moment_raw.reshape(inline_rows, cross_rows, total_time)
    shift = jnp.zeros_like(target)
    residual = target
    direction = target
    norm_now = squares(residual)
    for iteration in range(ITERS):
        image = operate(direction, weight)
        alpha = norm_now / lax.psum(jnp.sum(direction * image), FILT + IL + ("x",))
        shift = shift + alpha * direction
        residual = residual - alpha * image
        norm_next = squares(residual)
        direction = residual + norm_next / norm_now * direction
        norm_now = norm_next
    out_shape = (1, inline_rows, cross_rows, total_time)
    return (shift.reshape(out_shape), residual.reshape(out_shape))


def exchange(rows, axes, count):
    pieces = lax.all_to_all(rows.reshape(-1, count, 1, LANES), axes, 0, 0, tiled=True)
    return pieces.reshape(rows.shape)


def kernel(body, out_shape, mebibytes, **options):
    return pl.pallas_call(
        body, out_shape=out_shape, compiler_params=limit(mebibytes), name=body.__name__, **options
    )


def per_device(baseline, monitor, band_ids, quality):
    pieces, extra = kernel(
        pack_inputs,
        arrays((N_GROUP, 32, LANES), (24, 512)),
        4,
        in_specs=[HBM] * 4,
        scratch_shapes=[
            pltpu.VMEM((4, 1, 16, LANES), F32),
            pltpu.VMEM((4, 1, 16, LANES), F32),
            pltpu.SMEM((1, 2, KB, 4), jnp.int32),
            pltpu.SemaphoreType.DMA((4,)),
        ],
    )(baseline, monitor, quality, band_ids.transpose(1, 2, 3, 0))
    below = lax.ppermute(extra, GROUP, [(i, i + 1) for i in range(N_GROUP - 1)])
    above = lax.ppermute(extra, GROUP, [(i + 1, i) for i in range(N_GROUP - 1)])
    pieces = lax.all_to_all(pieces, GROUP, 0, 0, tiled=True)
    pieces, target = kernel(
        make_fields,
        [jax.ShapeDtypeStruct((N_PLANE, 16, LANES), jnp.int32)] + arrays((2, 32, LANES)),
        8,
    )(
        pieces, below, extra, above
    )
    pieces = lax.all_to_all(pieces, PLANE, 0, 0, tiled=True)
    (pieces,) = kernel(
        powers,
        arrays((N_PLANE * ROWS, LANES)),
        8,
        scratch_shapes=[
            pltpu.VMEM((2, DEPTH, SUB, LANES), F32),
            pltpu.VMEM((ITERS + 1, 2, DEPTH, SUB, LANES), F32),
        ],
    )(pieces)
    pieces = exchange(pieces, PLANE, ROWS)
    (sums,) = kernel(spread_sums, arrays((N_GROUP, LANES)), 4)(pieces)
    sums = exchange(sums, GROUP, 1)
    shift, residual, again = kernel(
        combine,
        arrays((1, 1, 16, 512), (1, 1, 16, 512)) + [jax.ShapeDtypeStruct((1,), jnp.int32)],
        4,
        out_specs=[VMEM, VMEM, SMEM],
    )(pieces, sums, target)

    def unsettled(state):
        return state[2][0] != 0

    def apart(state):
        return step_by_step(baseline, monitor, band_ids, quality) + (jnp.zeros((1,), jnp.int32),)

    return lax.while_loop(unsettled, apart, (shift, residual, again))[:2]


def solution(mesh):
    fine = Mesh(mesh.devices.reshape(2, 2, 4, 8, 4), ("zh", "core", "zl", "y", "x"))
    outs = P(FILT, IL, "x", None)
    in_specs = (P(None, IL, "x", FILT), P(None, IL, "x", FILT), P(None, IL, "x", None), outs)
    return jax.shard_map(
        per_device, mesh=fine, in_specs=in_specs, out_specs=(outs, outs), check_vma=False
    )
```

```python
import jax
import jax.numpy as jnp
from jax import lax
from jax.experimental import pallas as pl
from jax.experimental.pallas import tpu as pltpu
from jax.sharding import Mesh, PartitionSpec as P

BAND = 8
KB = 2
BXL = 8
HALF = 64
ITERS = 8
LANES = 128
SUB = 8

smooth_space = 4.0
smooth_time = 1.0
CENTRE = 19.0

GROUP = ("zh", "core", "zl")
PLANE = ("y", "x")
N_GROUP = 16
N_PLANE = 32
ROWS = 17
STEPS = 2.0**20 - 1.0
DEPTH = 24
FILT, IL = ("zh", "core"), ("zl", "y")
LAGS = 128
TRUST = 5e-5
HBM = pl.BlockSpec(memory_space=pltpu.HBM)
VMEM = pl.BlockSpec(memory_space=pltpu.VMEM)
SMEM = pl.BlockSpec(memory_space=pltpu.SMEM)
F32 = jnp.float32


def lane_ids():
    return lax.broadcasted_iota(jnp.int32, (SUB, LANES), 1)


def row_ids():
    return lax.broadcasted_iota(jnp.int32, (SUB, LANES), 0)


def roll(value, amount, axis):
    return pltpu.roll(value, amount, axis) if amount else value


def pack_inputs(
    base_hbm, mon_hbm, quality_hbm, bands_hbm, out_ref, extra_ref, base_ref, mon_ref, bands_ref, sems
):
    copies = [
        pltpu.make_async_copy(source, target, sems.at[k])
        for k, (source, target) in enumerate(
            (
                (bands_hbm, bands_ref),
                (base_hbm, base_ref),
                (mon_hbm, mon_ref),
                (quality_hbm.at[0, 0], extra_ref.at[0:16]),
            )
        )
    ]
    for copy in copies:
        copy.start()
    zl = lax.axis_index("zl")
    quarter = lax.axis_index("zh") * 2 + lax.axis_index("core")
    for copy in copies:
        copy.wait()
    for group in range(N_GROUP):
        offset = ((zl - group % 4 + 1) & 3) - 1
        source = jnp.clip(group + offset, 0, N_GROUP - 1) >> 2
        out_ref[group, 0:16, :] = base_ref[source, 0]
        out_ref[group, 16:32, :] = mon_ref[source, 0]
    rows = lax.broadcasted_iota(jnp.int32, (SUB, 512), 0)
    bands = jnp.zeros((SUB, 512), F32)
    for block in range(2):
        for slot in range(KB):
            band = bands_ref[0, block, slot, quarter].astype(F32)
            bands = jnp.where(rows == block * KB + slot, band, bands)
    extra_ref[16:24, :] = bands


def block_terms(base, padded, bands, lane):
    weight = jnp.zeros(base.shape, F32)
    moment = jnp.zeros(base.shape, F32)
    for band in bands:
        like_sum = jnp.zeros(base.shape, F32)
        step_sum = jnp.zeros(base.shape, F32)
        for quad in range(BAND // 4):
            terms = []
            for step in range(quad * 4, quad * 4 + 4):
                start = band * BAND + step
                turned = pltpu.roll(padded, (LANES - start) & (LANES - 1), 1)
                window = jnp.where(lane < LANES - start, turned[0:32], turned[8:40])
                difference = base - window
                misfit = (difference * difference).astype(jnp.bfloat16)
                terms.append(1.0 + misfit.astype(F32))
            a, b, c, d = terms
            left, right = a * b, c * d
            inverse = pl.reciprocal(left * right, approx=False)
            first, second = right * inverse, left * inverse
            low, high = (a + b) * first, (c + d) * second
            like_sum += low + high
            step_sum += a * first + c * second + 2.0 * high
            if quad:
                step_sum += (4.0 * quad) * (low + high)
        lag = (band * BAND - HALF).astype(F32)
        weight += like_sum
        moment += (lag * like_sum + step_sum) * (1.0 / HALF)
    scale = 1.0 / (KB * BAND)
    return weight * scale, moment * scale


def spread(value, lane, zero):
    turned = [roll(value[c * 8 : c * 8 + 8], 8, 1) for c in range(4)]
    sides = [zero] + turned + [zero]
    return [jnp.where(lane < 8, sides[i], sides[i + 1]) for i in range(5)]


def words_of(fields):
    weights = [(weight * STEPS + 0.5).astype(jnp.int32) for weight, _ in fields]
    targets = []
    for _, target in fields:
        size = (jnp.sqrt(jnp.abs(target) * 0.5) * STEPS + 0.5).astype(jnp.int32)
        targets.append(jnp.where(target < 0.0, -size, size))
    words = []
    for low, own, high in (weights, targets):
        words += [(low << 11) | ((high >> 10) & 2047), (own << 11) | (high & 1023)]
    return words


def fields_of(words):
    a, b, c, d = words
    weights = [lax.shift_right_logical(part, 11) for part in (a, b)]
    weights.append(((a & 2047) << 10) | (b & 1023))
    targets = [c >> 11, d >> 11]
    targets.append(((((c & 2047) << 10) | (d & 1023)) << 11) >> 11)
    out = []
    for weight, target in zip(weights, targets):
        root = target.astype(F32) * (2.0**0.5 / STEPS)
        out.append((weight.astype(F32) * (1.0 / STEPS), root * jnp.abs(root)))
    return out


def make_fields(recv_ref, below_ref, own_ref, above_ref, out_ref, target_ref):
    zl = lax.axis_index("zl")
    lane32 = lax.broadcasted_iota(jnp.int32, (32, LANES), 1)
    lane = lane_ids()
    zero = jnp.zeros((SUB, LANES), F32)
    empty = jnp.zeros((SUB, LANES), jnp.int32)
    fields = [[], []]
    for trace, extra_ref in enumerate((below_ref, own_ref, above_ref)):
        slot0 = (zl + trace - 1) & 3
        for block in range(2):
            rows = slice(block * 8, block * 8 + 8)
            mon_rows = slice(16 + block * 8, 24 + block * 8)
            base = jnp.concatenate([recv_ref[4 * c + slot0, rows, :] for c in range(4)], axis=0)
            turned = [roll(recv_ref[4 * c + slot0, mon_rows, :], 64, 1) for c in range(4)]
            sides = [zero] + turned + [zero]
            padded = jnp.concatenate(
                [jnp.where(lane < 64, sides[i], sides[i + 1]) for i in range(5)], axis=0
            )
            bands = [
                jnp.max(extra_ref[16 + block * KB + s : 17 + block * KB + s, 0:LANES]).astype(jnp.int32)
                for s in range(KB)
            ]
            weight, moment = block_terms(base, padded, bands, lane32)
            quality = jnp.concatenate(
                [extra_ref[rows, c * LANES : (c + 1) * LANES] for c in range(4)], axis=0
            )
            weight, moment = weight * quality, moment * quality
            if trace == 1:
                target_ref[block] = moment
            fields[block].append((weight, moment))
    words = [[spread(word, lane, empty) for word in words_of(part)] for part in fields]
    for at in range(2):
        groups = [words[h][2 * at + k] for k in range(2) for h in range(2)]
        for piece in range(N_PLANE):
            part, offset = piece // 8, 16 * (piece % 8)
            packed = None
            for g, vregs in enumerate(groups):
                shift = (32 * g - offset) % LANES
                value = roll(vregs[part], shift, 1)
                if piece % 8 == 7:
                    value = jnp.where(lane < 32 * g + 16, value, roll(vregs[part + 1], shift, 1))
                packed = value if packed is None else jnp.where(lane < 32 * g, packed, value)
            out_ref[piece, at * 8 : at * 8 + 8, :] = packed


def swap_halves(low, high, lane):
    turned = roll(jnp.where(lane < 64, high, low), 64, 1)
    return jnp.where(lane < 64, low, turned), jnp.where(lane < 64, turned, high)


def beside(values, lane, row):
    low, high = values
    next_low, next_high = roll(low, 7, 1), roll(high, 7, 1)
    turn_low, turn_high = roll(next_low, 96, 2), roll(next_high, 96, 2)
    last = row == 7
    up_low = jnp.where(last, jnp.where(lane < 96, turn_low, turn_high), next_low)
    up_high = jnp.where(last, jnp.where(lane < 96, turn_high, 0.0), next_high)
    prev_low, prev_high = roll(low, 1, 1), roll(high, 1, 1)
    turn_low, turn_high = roll(prev_low, 32, 2), roll(prev_high, 32, 2)
    first = row == 0
    down_low = jnp.where(first, jnp.where(lane < 32, 0.0, turn_low), prev_low)
    down_high = jnp.where(first, jnp.where(lane < 32, turn_low, turn_high), prev_high)
    return up_low + down_low, up_high + down_high


CHUNK = 4


def chunks(begin, end):
    out = []
    while begin < end:
        stop = min(end, begin + CHUNK, (begin // 8 + 1) * 8)
        out.append((begin, stop))
        begin = stop
    return out


def powers(recv_ref, out_ref, diag_ref, basis_ref):
    group = lax.axis_index("zh") * 8 + lax.axis_index("core") * 4 + lax.axis_index("zl")
    slab = lax.axis_index("y") * 4 + lax.axis_index("x")
    lane, row = lane_ids(), row_ids()
    tau = lane & 31
    time = slab * 16 - 8 + tau
    inside = ((time >= 0) & (time < 512)).astype(F32)
    shares = [
        inside * (group > 0).astype(F32),
        inside,
        inside * (group < N_GROUP - 1).astype(F32),
    ]
    space = [share * (2.0 * smooth_space / CENTRE) for share in shares]
    along = [share * (2.0 * smooth_time / CENTRE) for share in shares]
    for y in range(8):
        for v in range(2):
            piece = y * 4 + 2 * v
            words = []
            for rows in (slice(0, 8), slice(8, 16)):
                words += swap_halves(recv_ref[piece, rows, :], recv_ref[piece + 1, rows, :], lane)
            for trace, (weight, target) in enumerate(fields_of(words)):
                centre = weight + (4.0 * smooth_space + 2.0 * smooth_time - CENTRE)
                diag_ref[v, trace * 8 + y] = centre * (shares[trace] * (2.0 / CENTRE))
                basis_ref[0, v, trace * 8 + y] = target
    own = (tau >= 8) & (tau < 24)
    squares, crosses = [], []
    for level in range(ITERS):
        square = jnp.zeros((SUB, LANES), F32)
        cross = jnp.zeros((SUB, LANES), F32)
        for begin, end in chunks(level + 1, DEPTH - 1 - level):
            region, here = begin // 8, slice(begin, end)
            centre = [basis_ref[level, v, here] for v in range(2)]
            sides = beside(centre, lane[None], row[None])
            for v in range(2):
                inlines = basis_ref[level, v, begin - 1 : end - 1] + basis_ref[level, v, begin + 1 : end + 1]
                times = roll(centre[v], 1, 2) + roll(centre[v], LANES - 1, 2)
                image = (
                    diag_ref[v, here] * centre[v]
                    - space[region] * (inlines + sides[v])
                    - along[region] * times
                )
                image = 0.5 * image if level == 0 else image - basis_ref[level - 1, v, here]
                basis_ref[level + 1, v, here] = image
                if region == 1:
                    square += jnp.sum(centre[v] * centre[v], axis=0)
                    cross += jnp.sum(centre[v] * image, axis=0)
        squares.append(jnp.where(own, square, 0.0))
        crosses.append(jnp.where(own, cross, 0.0))
    tiles = []
    for values in (squares, crosses):
        for amount in (4, 2, 1):
            values = [
                jnp.where(
                    (row & amount) == 0, a + roll(a, 8 - amount, 0), b + roll(b, amount, 0)
                )
                for a, b in zip(values[:amount], values[amount:])
            ]
        tile = values[0]
        for amount in (64, 32, 16, 8):
            tile = tile + roll(tile, amount, 1)
        tiles.append(tile)
    tile = jnp.where(((lane >> 3) & 7) == row, jnp.where(lane < 64, tiles[0], tiles[1]), 0.0)
    for amount in (4, 2, 1):
        tile = tile + roll(tile, amount, 0)
    for y in range(8):
        for v in range(2):
            pairs = []
            for k in range(1, 9, 2):
                pairs.append(
                    jnp.where(own, basis_ref[k, v, 8 + y], roll(basis_ref[k + 1, v, 8 + y], 16, 1))
                )
            for part in range(2):
                for half, tile_half in enumerate(swap_halves(*pairs[2 * part : 2 * part + 2], (lane - 8) & 127)):
                    at = (y * 4 + 2 * v + half) * ROWS + part * 8
                    out_ref[at : at + 8, :] = tile_half
    for piece in range(N_PLANE):
        out_ref[piece * ROWS + 16 : piece * ROWS + 17, :] = tile[0:1]


def spread_sums(recv_ref, out_ref):
    terms = [recv_ref[piece * ROWS + 16 : piece * ROWS + 17, :] for piece in range(N_PLANE)]
    while len(terms) > 1:
        terms = [terms[k] + terms[k + 1] for k in range(0, len(terms), 2)]
    out_ref[...] = jnp.broadcast_to(terms[0], (N_GROUP, LANES))


def two_sum(a, b):
    total = a + b
    part = total - a
    return total, (a - (total - part)) + (b - part)


def split(a):
    scaled = 4097.0 * a
    high = scaled - (scaled - a)
    return high, a - high


def across(tile, k):
    return jnp.broadcast_to(tile[k : k + 1], (SUB, LANES))


def lift(pair, turn):
    return tuple(turn(part) for part in pair)


def choose(mask, first, second):
    return tuple(jnp.where(mask, a, b) for a, b in zip(first, second))


def add_pairs(first, second):
    total, error = two_sum(first[0], second[0])
    return two_sum(total, error + (first[1] + second[1]))


def solve(total, lane, row, turn):
    zero = jnp.zeros((SUB, LANES), F32)
    fold = total
    for amount in (4, 2, 1):
        fold = add_pairs(fold, lift(fold, lambda part: turn(part, amount, 0)))
    for amount in (124, 126, 127):
        fold = add_pairs(fold, lift(fold, lambda part: turn(part, amount, 1)))

    def at_lane(pair, k):
        return lift(pair, lambda part: jnp.broadcast_to(part[:, k : k + 1], (SUB, LANES)))

    start = choose(lane < 64, at_lane(fold, 0), at_lane(fold, 64))
    doubled = add_pairs(lift(fold, lambda part: 2.0 * part), lift(start, lambda part: -part))
    moments = [at_lane(doubled, 64 * (k % 2) + 8 * (k // 2)) for k in range(2 * ITERS)]

    def column(values):
        out = values[0]
        for k in range(1, SUB):
            out = choose(row < k, out, values[k])
        return out

    ahead, beyond, behind = column(moments[:8]), column(moments[8:]), column(moments[8:0:-1])
    gram = []
    for k in range(ITERS + 1):
        later = choose(
            row < 8 - k,
            lift(ahead, lambda part: turn(part, (8 - k) % 8, 0)),
            lift(beyond, lambda part: turn(part, (8 - k) % 8, 0)),
        )
        earlier = choose(
            row < k,
            lift(behind, lambda part: turn(part, k % 8, 0)),
            lift(ahead, lambda part: turn(part, k % 8, 0)),
        )
        gram.append(add_pairs(later, earlier))
    inverse = [gram[k][0] + 0.5 * (gram[k + 1][0] + gram[abs(k - 1)][0]) for k in range(ITERS)]
    for k in range(ITERS):
        reciprocal = 1.0 / across(inverse[k], k)
        pivot = inverse[k]
        for j in range(ITERS):
            if j != k:
                share = across(inverse[j], k) * reciprocal
                inverse[j] = jnp.where(row == k, share, inverse[j] - pivot * share)
        inverse[k] = jnp.where(row == k, reciprocal, -pivot * reciprocal)

    def apply_inverse(right):
        terms = [inverse[k] * across(right, k) for k in range(ITERS)]
        while len(terms) > 1:
            terms = [terms[k] + terms[k + 1] for k in range(0, len(terms), 2)]
        return terms[0]

    def remainder(series):
        def lower(part):
            return jnp.where(row == 0, 0.0, jnp.where(row == 1, 1.0, 0.5) * turn(part, 1, 0))

        def upper(part):
            return jnp.where(row == 7, 0.0, 0.5 * turn(part, 7, 0))

        image = add_pairs(add_pairs(lift(series, lower), lift(series, upper)), series)
        start = (jnp.where(row == 0, 1.0, 0.0), zero)
        return add_pairs(start, lift(image, lambda part: -part)), lift(series, lambda part: -0.5 * across(part, 7))

    parts = [split(pair[0]) for pair in gram]
    series = (apply_inverse(gram[0][0]), zero)
    steps = []
    for _ in range(1):
        body, top = remainder(series)
        high, low = zero, zero
        for k in range(ITERS + 1):
            a, a_low = lift(body, lambda part: across(part, k)) if k < ITERS else top
            b, b_low = gram[k]
            (a0, a1), (b0, b1) = split(a), parts[k]
            product = a * b
            error = (((a0 * b0 - product) + a0 * b1) + a1 * b0) + a1 * b1
            high, rest = two_sum(high, product)
            low = low + (rest + (error + (a * b_low + a_low * b)))
        change = apply_inverse(high + low)
        steps.append(change)
        series = two_sum(series[0], series[1] + change)
    body, top = remainder(series)
    return (series[0] + series[1]) * (1.0 / CENTRE), body[0] + body[1], top[0] + top[1], steps, series[0]


def combine(basis_ref, sums_ref, target_ref, shift_ref, residual_ref, again_ref):
    lane, row = lane_ids(), row_ids()
    zero = jnp.zeros((SUB, LANES), F32)
    total = two_sum(sums_ref[0:8, :], sums_ref[8:16, :])
    shift, residual, last, steps, series = solve(total, lane, row, roll)
    fine = jnp.max(jnp.abs(steps[0])) <= TRUST * jnp.max(jnp.abs(series))
    again_ref[0] = 1 - fine.astype(jnp.int32)
    lane = (lane - 8) & 127
    first = (lane & 31) < 16
    for body, top, out_ref in ((shift, zero, shift_ref), (residual, last, residual_ref)):
        terms = [across(body, k) for k in range(ITERS)] + [top]
        low, high = (
            jnp.where(
                lane < 64,
                jnp.where(first, terms[k], terms[k + 1]),
                jnp.where(first, terms[k + 2], terms[k + 3]),
            )
            for k in (1, 5)
        )
        for part in range(4):
            def piece(step):
                at = (part * 8 + step) * ROWS
                return low * basis_ref[at : at + 8, :] + high * basis_ref[at + 8 : at + 16, :]

            def quad(step):
                halves = []
                for near in (step, step + 1):
                    a, b = piece(near), piece(near + 4)
                    halves.append(jnp.where(lane < 64, a, b) + roll(jnp.where(lane < 64, b, a), 64, 1))
                a, b = halves
                return jnp.where(first, a + roll(a, 112, 1), b + roll(b, 16, 1))

            even, odd = quad(0), quad(2)
            lower = (lane & 32) == 0
            blocks = (
                jnp.where(lower, even, roll(odd, 32, 1)),
                jnp.where(lower, roll(even, 96, 1), odd),
            )
            for h in range(2):
                out_ref[0, 0, h * 8 : h * 8 + 8, part * LANES : (part + 1) * LANES] = (
                    roll(blocks[h], 120, 1) + terms[0] * target_ref[h, part * 8 : part * 8 + 8, :]
                )


def limit(mebibytes):
    return pltpu.CompilerParams(vmem_limit_bytes=mebibytes * 1024 * 1024)


def arrays(*shapes):
    return [jax.ShapeDtypeStruct(shape, F32) for shape in shapes]


def padded_2(value, sides, width):
    for axis, dim in sides:
        size, length = (lax.axis_size(axis), value.shape[dim])
        up = [(i, (i + 1) % size) for i in range(size - 1)]
        down = [(j, i) for i, j in up]
        last = lax.slice_in_dim(value, length - width, length, axis=dim)
        first = lax.slice_in_dim(value, 0, width, axis=dim)
        before = lax.ppermute(last, axis, up)
        after = lax.ppermute(first, axis, down)
        value = jnp.concatenate([before, value, after], axis=dim)
    return value


def slot_window(block, band):
    start = band * BAND
    return lax.dynamic_slice(
        block, (jnp.int32(0), start), (block.shape[0], block.shape[1] - LAGS + BAND)
    )


def lag_table(band_list):
    steps = jnp.arange(BAND, dtype=jnp.float32)
    return (band_list.astype(jnp.float32)[..., None] * BAND + steps - HALF) / HALF


def moments(errors, lags):
    likeness = 1.0 / (1.0 + errors.astype(jnp.float32))
    weight_sum = jnp.sum(likeness, axis=(3, 4)) / (KB * BAND)
    moment_sum = jnp.sum(lags[..., None, None] * likeness, axis=(3, 4)) / (KB * BAND)
    return (weight_sum, moment_sum)


def operate(field, weight):
    padded = padded_2(field, ((FILT + IL, 0), ("x", 1)), 1)
    centre = padded[1:-1, 1:-1, :]
    across = (
        4.0 * centre
        - padded[2:, 1:-1, :]
        - padded[:-2, 1:-1, :]
        - padded[1:-1, 2:, :]
        - padded[1:-1, :-2, :]
    )
    timed = jnp.pad(field, ((0, 0), (0, 0), (1, 1)))
    along = 2.0 * field - timed[:, :, 2:] - timed[:, :, :-2]
    return weight * field + smooth_space * across + smooth_time * along


def squares(residual):
    return lax.psum(jnp.sum(residual * residual), FILT + IL + ("x",))


def step_by_step(baseline, monitor, band_ids, quality):
    quarters, inline_rows, cross_rows, samples = baseline.shape
    cross_blocks = cross_rows // BXL
    extended = padded_2(monitor, ((FILT, 3),), HALF)
    ext_blocks = extended.reshape(quarters, inline_rows, cross_blocks, BXL, samples + LAGS)
    base_blocks = baseline.reshape(quarters, inline_rows, cross_blocks, BXL, samples)
    per_slot = jax.vmap(slot_window, in_axes=(None, 0))
    windows = jax.vmap(jax.vmap(jax.vmap(per_slot)))(ext_blocks, band_ids)
    errors = jnp.stack(
        [
            jnp.square(
                base_blocks[:, :, :, None] - windows[..., lag_step : lag_step + samples]
            ).astype(jnp.bfloat16)
            for lag_step in range(BAND)
        ],
        axis=4,
    )
    local_weight, local_moment = moments(errors, lag_table(band_ids))
    weight_raw, moment_raw = (
        lax.all_to_all(local_weight, FILT, split_axis=0, concat_axis=4, tiled=True),
        lax.all_to_all(local_moment, FILT, split_axis=0, concat_axis=4, tiled=True),
    )
    total_time = weight_raw.shape[-1]
    quality_grid = quality.reshape(inline_rows, cross_rows, total_time)
    weight = quality_grid * weight_raw.reshape(inline_rows, cross_rows, total_time)
    target = quality_grid * moment_raw.reshape(inline_rows, cross_rows, total_time)
    shift = jnp.zeros_like(target)
    residual = target
    direction = target
    norm_now = squares(residual)
    for iteration in range(ITERS):
        image = operate(direction, weight)
        alpha = norm_now / lax.psum(jnp.sum(direction * image), FILT + IL + ("x",))
        shift = shift + alpha * direction
        residual = residual - alpha * image
        norm_next = squares(residual)
        direction = residual + norm_next / norm_now * direction
        norm_now = norm_next
    out_shape = (1, inline_rows, cross_rows, total_time)
    return (shift.reshape(out_shape), residual.reshape(out_shape))


def exchange(rows, axes, count):
    pieces = lax.all_to_all(rows.reshape(-1, count, 1, LANES), axes, 0, 0, tiled=True)
    return pieces.reshape(rows.shape)


def kernel(body, out_shape, mebibytes, **options):
    return pl.pallas_call(
        body, out_shape=out_shape, compiler_params=limit(mebibytes), name=body.__name__, **options
    )


def per_device(baseline, monitor, band_ids, quality):
    pieces, extra = kernel(
        pack_inputs,
        arrays((N_GROUP, 32, LANES), (24, 512)),
        4,
        in_specs=[HBM] * 4,
        scratch_shapes=[
            pltpu.VMEM((4, 1, 16, LANES), F32),
            pltpu.VMEM((4, 1, 16, LANES), F32),
            pltpu.SMEM((1, 2, KB, 4), jnp.int32),
            pltpu.SemaphoreType.DMA((4,)),
        ],
    )(baseline, monitor, quality, band_ids.transpose(1, 2, 3, 0))
    below = lax.ppermute(extra, GROUP, [(i, i + 1) for i in range(N_GROUP - 1)])
    above = lax.ppermute(extra, GROUP, [(i + 1, i) for i in range(N_GROUP - 1)])
    pieces = lax.all_to_all(pieces, GROUP, 0, 0, tiled=True)
    pieces, target = kernel(
        make_fields,
        [jax.ShapeDtypeStruct((N_PLANE, 16, LANES), jnp.int32)] + arrays((2, 32, LANES)),
        8,
    )(
        pieces, below, extra, above
    )
    pieces = lax.all_to_all(pieces, PLANE, 0, 0, tiled=True)
    (pieces,) = kernel(
        powers,
        arrays((N_PLANE * ROWS, LANES)),
        8,
        scratch_shapes=[
            pltpu.VMEM((2, DEPTH, SUB, LANES), F32),
            pltpu.VMEM((ITERS + 1, 2, DEPTH, SUB, LANES), F32),
        ],
    )(pieces)
    pieces = exchange(pieces, PLANE, ROWS)
    (sums,) = kernel(spread_sums, arrays((N_GROUP, LANES)), 4)(pieces)
    sums = exchange(sums, GROUP, 1)
    shift, residual, again = kernel(
        combine,
        arrays((1, 1, 16, 512), (1, 1, 16, 512)) + [jax.ShapeDtypeStruct((1,), jnp.int32)],
        4,
        out_specs=[VMEM, VMEM, SMEM],
    )(pieces, sums, target)

    def unsettled(state):
        return state[2][0] != 0

    def apart(state):
        return step_by_step(baseline, monitor, band_ids, quality) + (jnp.zeros((1,), jnp.int32),)

    return lax.while_loop(unsettled, apart, (shift, residual, again))[:2]


def solution(mesh):
    fine = Mesh(mesh.devices.reshape(2, 2, 4, 8, 4), ("zh", "core", "zl", "y", "x"))
    outs = P(FILT, IL, "x", None)
    in_specs = (P(None, IL, "x", FILT), P(None, IL, "x", FILT), P(None, IL, "x", None), outs)
    return jax.shard_map(
        per_device, mesh=fine, in_specs=in_specs, out_specs=(outs, outs), check_vma=False
    )
```
